256 devices in a mesh: gx: 32 (over z, y_hi, core), gy: 8 (over y_lo, x).
Axes of the slice: x: 4, y: 4 (y_hi: 2, y_lo: 2; y = y_hi * 2 + y_lo), z: 8, core: 2. Of those that a mesh axis runs over, the one named last changes fastest.
Arguments:
- hidden_in: bfloat16 [32, 64, 20, 1024], P('gx', 'gy'), may hold values from -6 to 6
- spectral: float32 [2, 2, 20, 20, 16, 16, 128], P(None, None, None, None, 'gy', None, 'gx'), may hold values from -1.25 to 1.25
- pointwise: bfloat16 [2, 20, 20], replicated, may hold values from -1.25 to 1.25
- biases: float32 [2, 20], replicated, may hold values from -3 to 3
- upstream: bfloat16 [32, 64, 20, 1024], P('gx', 'gy'), may hold values from -6 to 6
Outputs:
- hidden_out: float32 [32, 64, 20, 1024], P('gx', 'gy')
- grad_hidden: float32 [32, 64, 20, 1024], P('gx', 'gy')
- grad_spectral: float32 [2, 2, 20, 20, 16, 16, 128], P(None, None, None, None, 'gy', None, 'gx')
- grad_pointwise: float32 [2, 20, 20], replicated
- grad_biases: float32 [2, 20], replicated
The draws below stay inside these ranges and needn't reach their ends.
All inputs are finite; a program needn't handle non-finite values.
Results may differ from the reference program's by a relative error of at most 0.012.
The reference program's roundings to bfloat16 on the way count: a program that leaves them out, or rounds other values in their place, can miss the bound.
Values sent between devices are 32-bit elements; how exact they have to be, the bound alone decides.
No kernel may reach another device: no remote copies, remote signals or barrier semaphores. Data moves between devices by JAX's collectives and lax.ppermute only.
A program may use at most 128 MiB of HBM per device.

```python
import math
import jax
import jax.numpy as jnp
from jax import lax

WIDTH = 20
KX = 16
KY = 16
KZ = 16
KT = 8
NZ = 64
NT = 16
LAYERS = 2
NX = 32
NY = 64


def shard_levels(own_key, shape, cuts, low, high):
    level, own = 1.0, jax.random.fold_in(own_key, 6)
    for position, blocks in cuts:
        draws = jnp.exp(jax.random.uniform(jax.random.fold_in(own, position), (blocks,), jnp.float32, low / len(cuts), high / len(cuts)))
        level = level * jnp.repeat(draws, shape[position] // blocks).reshape([-1 if axis == position else 1 for axis in range(len(shape))])
    return level


def bell_draw(key, extent, scale, reach, cuts=(), kind=jnp.bfloat16):
    values = scale * jax.random.normal(key, extent, jnp.float32)
    if cuts:
        values = values * shard_levels(key, extent, cuts, -0.22, 0.18)
    return jnp.clip(values, -reach, reach).astype(kind)


def setup_inputs(seed: int = 0) -> dict:
    keys = jax.random.split(jax.random.key(seed), 6)
    return {
        "hidden_in": bell_draw(keys[0], (NX, NY, WIDTH, NZ * NT), 1.0, 6.0, ((0, 32), (1, 8))),
        "spectral": bell_draw(keys[1], (LAYERS, 2, WIDTH, WIDTH, KX, KY, KZ * KT), WIDTH ** -0.5, 1.25, ((4, 8), (6, 32)), jnp.float32),
        "pointwise": bell_draw(keys[2], (LAYERS, WIDTH, WIDTH), WIDTH ** -0.5, 1.25),
        "biases": bell_draw(keys[3], (LAYERS, WIDTH), 0.5, 3.0, (), jnp.float32),
        "upstream": bell_draw(keys[4], (NX, NY, WIDTH, NZ * NT), 1.0, 6.0, ((0, 32), (1, 8))),
    }


precise = lax.Precision.HIGHEST
root_half = 1.0 / math.sqrt(2.0)
root_gauss = 1.0 / math.sqrt(2.0 * math.pi)

def centered(number):
    return jnp.arange(number, dtype=jnp.int32) - number // 2

def pair_table(points, frequencies, length, direction, factor):
    phases = jnp.mod(points[:, None] * frequencies[None, :], length)
    angles = phases.astype(jnp.float32) * (2.0 * math.pi / length)
    cosines = jnp.cos(angles) * factor
    sines = jnp.sin(angles) * (direction * factor)
    first_row = jnp.stack([cosines, sines], axis=-1)
    second_row = jnp.stack([-sines, cosines], axis=-1)
    return jnp.stack([first_row, second_row], axis=-2)

def depth_tables():
    cell_ids = jnp.arange(NZ * NT, dtype=jnp.int32)
    depth_pos = cell_ids // NT
    step_pos = cell_ids % NT
    depth_freq = centered(KZ)
    step_freq = jnp.arange(KT, dtype=jnp.int32)
    phases = jnp.mod(depth_pos[:, None, None] * depth_freq[None, :, None] * NT + step_pos[:, None, None] * step_freq[None, None, :] * NZ, NZ * NT)
    angles = phases.astype(jnp.float32) * (2.0 * math.pi / (NZ * NT))
    parts = jnp.stack([jnp.cos(angles), -jnp.sin(angles)], axis=-1)
    weights = jnp.where(step_freq == 0, 1.0, 2.0).astype(jnp.float32)[None, None, :, None]
    ahead = (parts * (1.0 / math.sqrt(NZ * NT))).reshape(NZ * NT, -1).astype(jnp.bfloat16)
    behind = (parts * weights * (1.0 / math.sqrt(2 * KZ * KT))).reshape(NZ * NT, -1)
    return (ahead, jnp.transpose(behind).astype(jnp.bfloat16))

def grid_tables(size_x, size_y):
    zt_ahead, zt_behind = depth_tables()
    x_points = jnp.arange(size_x, dtype=jnp.int32)
    y_points = jnp.arange(size_y, dtype=jnp.int32)
    x_ahead = pair_table(x_points, centered(KX), size_x, -1.0, 1.0 / math.sqrt(size_x)).astype(jnp.bfloat16)
    x_behind = jnp.transpose(pair_table(x_points, centered(KX), size_x, 1.0, 1.0 / math.sqrt(KX)), (1, 0, 2, 3)).astype(jnp.bfloat16)
    y_ahead = pair_table(y_points, centered(KY), size_y, -1.0, 1.0 / math.sqrt(size_y))
    y_behind = jnp.transpose(pair_table(y_points, centered(KY), size_y, 1.0, 1.0 / math.sqrt(KY)), (1, 0, 2, 3))
    return (zt_ahead, zt_behind, x_ahead, x_behind, y_ahead, y_behind)

def gelu_value(preact):
    return preact * 0.5 * (1.0 + lax.erf(preact * root_half))

def gelu_slope(preact):
    return 0.5 * (1.0 + lax.erf(preact * root_half)) + preact * jnp.exp(-0.5 * preact * preact) * root_gauss

def analyze(field_in, zt_table, x_table, y_table):

    def project(row_block):
        return jnp.dot(row_block, zt_table, preferred_element_type=jnp.float32)
    spectra = lax.map(project, field_in)
    pairs = spectra.reshape(spectra.shape[:3] + (-1, 2)).astype(jnp.float32)
    along_x = jnp.einsum('xycmr,xkrs->kycms', pairs, x_table.astype(jnp.float32), precision=precise)
    return jnp.einsum('kycmr,yjrs->kjcms', along_x, y_table, precision=precise)

def synthesize(modes, y_table, x_table):
    along_y = jnp.einsum('kjcmr,jyrs->kycms', modes, y_table, precision=precise)
    along_x = jnp.einsum('kycmr,kxrs->xycms', along_y, x_table.astype(jnp.float32), precision=precise)
    return along_x.reshape(along_x.shape[:3] + (-1,))

def block_weights(weights):
    first = jnp.stack([weights[0], weights[1]], axis=2)
    second = jnp.stack([-weights[1], weights[0]], axis=2)
    return jnp.stack([first, second], axis=1)

def mix(spectrum, weights):
    return jnp.einsum('kycmr,crdskym->kydms', spectrum, block_weights(weights), precision=precise)

def mix_grad(spectrum, dmixed, weights):
    conj_spec = jnp.stack([spectrum[..., 0], -spectrum[..., 1]], axis=-1)
    grad_real = jnp.einsum('kycmr,kydmr->cdkym', conj_spec, dmixed, precision=precise)
    swapped = jnp.stack([-dmixed[..., 1], dmixed[..., 0]], axis=-1)
    grad_imag = -jnp.einsum('kycmr,kydmr->cdkym', conj_spec, swapped, precision=precise)
    back = jnp.einsum('crdskym,kydms->kycmr', block_weights(weights), dmixed, precision=precise)
    return (jnp.stack([grad_real, grad_imag]), back)

def pre_rows(back_row, field_row, zt_behind, mixing, offset):
    return jnp.dot(back_row, zt_behind.astype(jnp.float32), precision=precise) + jnp.einsum('ycq,cd->ydq', field_row.astype(jnp.float32), mixing.astype(jnp.float32), precision=precise) + offset[None, :, None]

def reference(hidden_in, spectral, pointwise, biases, upstream):
    zt_ahead, zt_behind, x_ahead, x_behind, y_ahead, y_behind = grid_tables(NX, NY)
    x_ahead_adj = jnp.transpose(x_behind, (1, 0, 3, 2))
    y_ahead_adj = jnp.transpose(y_behind, (1, 0, 3, 2))
    x_behind_adj = jnp.transpose(x_ahead, (1, 0, 3, 2))
    y_behind_adj = jnp.transpose(y_ahead, (1, 0, 3, 2))
    current = hidden_in
    stored = []
    for layer_id in range(LAYERS):
        spectrum = analyze(current, zt_ahead, x_ahead, y_ahead)
        returned = synthesize(mix(spectrum, spectral[layer_id]), y_behind, x_behind)
        mixing = pointwise[layer_id]
        offset = biases[layer_id]

        def activate(pieces, mixing=mixing, offset=offset):
            return gelu_value(pre_rows(pieces[0], pieces[1], zt_behind, mixing, offset))
        stored.append((current, spectrum, returned))
        current = lax.map(activate, (returned, current))
        if layer_id < LAYERS - 1:
            current = current.astype(jnp.bfloat16)
    hidden_out = current
    carried = upstream
    grad_modes, grad_mixing, grad_offset = ([], [], [])
    for layer_id in reversed(range(LAYERS)):
        field_in, spectrum, returned = stored[layer_id]
        mixing = pointwise[layer_id]
        offset = biases[layer_id]

        def descend(totals, pieces, mixing=mixing, offset=offset):
            preact = pre_rows(pieces[0], pieces[1], zt_behind, mixing, offset)
            slope_row = (pieces[2].astype(jnp.float32) * gelu_slope(preact)).astype(jnp.bfloat16)
            weight_total = totals[0] + jnp.einsum('ycq,ydq->cd', pieces[1].astype(jnp.float32), slope_row.astype(jnp.float32), precision=precise)
            bias_total = totals[1] + lax.optimization_barrier(jnp.sum(slope_row.astype(jnp.float32), axis=(0, 2)))
            return ((weight_total, bias_total), slope_row)
        initial = (jnp.zeros((WIDTH, WIDTH), jnp.float32), jnp.zeros((WIDTH,), jnp.float32))
        (weight_total, bias_total), slopes = lax.scan(descend, initial, (returned, field_in, carried))
        dmixed = analyze(slopes, jnp.transpose(zt_behind), x_ahead_adj, y_ahead_adj)
        weight_grad, spec_grad = mix_grad(spectrum, dmixed, spectral[layer_id])
        dreturned = synthesize(spec_grad, y_behind_adj, x_behind_adj)

        def climb(pieces, mixing=mixing):
            return jnp.dot(pieces[0], jnp.transpose(zt_ahead).astype(jnp.float32), precision=precise) + jnp.einsum('ydq,cd->ycq', pieces[1].astype(jnp.float32), mixing.astype(jnp.float32), precision=precise)
        carried = lax.map(climb, (dreturned, slopes))
        if layer_id > 0:
            carried = carried.astype(jnp.bfloat16)
        grad_modes.append(weight_grad)
        grad_mixing.append(weight_total)
        grad_offset.append(bias_total)
    cell_scale = 1.0 / math.sqrt(NX * NY * NZ * NT)
    mode_scale = math.sqrt(2.0 * KX * KY * KZ * KT / (NX * NY * NZ * NT))
    grad_spectral = jnp.stack(grad_modes[::-1]) * mode_scale
    grad_pointwise = jnp.stack(grad_mixing[::-1]) * cell_scale
    grad_biases = jnp.stack(grad_offset[::-1]) * cell_scale
    return (hidden_out, carried, grad_spectral, grad_pointwise, grad_biases)
```

```python
import functools
import math

import jax
import jax.numpy as jnp
import ml_dtypes
import numpy as np
from jax import lax
from jax.experimental import pallas as pl
from jax.experimental.pallas import tpu as pltpu
from jax.sharding import Mesh, PartitionSpec as P

KX = 16
KY = 16
KZ = 16
KT = 8
NZ = 64
NT = 16
NX = 32
NY = 64
C = 20
Q = NZ * NT
ROWS = 160
PADS = (2, 3, 6, 7)

F32 = jnp.float32
BF16 = jnp.bfloat16
HIGH = lax.Precision.HIGHEST
PARAMS = pltpu.CompilerParams(vmem_limit_bytes=32 * 1024 * 1024)


def depth_tables():
    rows = np.arange(256)
    g, m4, r, mh = rows % 16, rows // 16 % 4, rows // 64 % 2, rows // 128
    m = 8 * g + 4 * mh + m4
    freq_z, freq_t = m // KT - KZ // 2, m % KT
    cells = np.arange(Q)
    phase = (freq_z[:, None] * (cells // NT) * NT + freq_t[:, None] * (cells % NT) * NZ) % Q
    angle = phase * (2.0 * np.pi / Q)
    parts = np.where(r[:, None] == 0, np.cos(angle), -np.sin(angle))
    weight = np.where(freq_t == 0, 1.0, 2.0)[:, None]
    ahead = (parts / math.sqrt(Q)).astype(np.float32).astype(ml_dtypes.bfloat16)
    behind = (parts * weight / math.sqrt(2 * KZ * KT)).astype(np.float32)
    return ahead, behind.astype(ml_dtypes.bfloat16)


def row_table(sign, factor):
    core, jj, kx = np.meshgrid(np.arange(2), np.arange(4), np.arange(KX), indexing="ij")
    angle = ((2 * jj + core) * (kx - KX // 2) % NX) * (2.0 * np.pi / NX)
    pairs = np.stack([np.cos(angle), sign * np.sin(angle)], axis=-1) * factor
    pairs = pairs.astype(np.float32).astype(ml_dtypes.bfloat16).astype(np.float32)
    return pairs


def column_tables():
    y = 8 * np.arange(8)[:, None, None] + np.arange(128)[None, None, :] % 8
    ky = np.arange(64)[None, :, None] // 4
    angle = (y * (ky - KY // 2) % NY) * (2.0 * np.pi / NY)
    scale = 1.0 / math.sqrt(NY)
    return (np.cos(angle) * scale).astype(np.float32), (np.sin(angle) * scale).astype(np.float32)


def channel_table():
    rows = np.arange(256)
    owner = np.where(rows < 128, rows // 8, 16 + rows // 8 % 4)
    return (owner[:, None] == np.arange(128)[None, :]).astype(ml_dtypes.bfloat16)


def iota(shape, axis):
    return lax.broadcasted_iota(jnp.int32, shape, axis)


def halves(value):
    high = value.astype(BF16)
    return high, (value - high.astype(F32)).astype(BF16)


def dot2(value, table):
    high, low = halves(value)
    return jnp.dot(high, table, preferred_element_type=F32) + jnp.dot(
        low, table, preferred_element_type=F32
    )


def dot_rows(left, right):
    return lax.dot_general(left, right, (((1,), (1,)), ((), ())), preferred_element_type=F32)


def erf(value):
    value = jnp.clip(value, -3.832506856900711, 3.832506856900711)
    square = value * value
    top = jnp.full_like(value, 0.00022905065861350646)
    for term in (0.0034082910107109506, 0.050955695062380861, 0.18520832239976145, 1.128379143519084):
        top = top * square + term
    base = jnp.full_like(value, -1.1791602954361697e-7)
    for term in (
        0.000023547966471313185,
        0.0010179625278914885,
        0.014070470171167667,
        0.11098505178285362,
        0.49746925110067538,
        1.0,
    ):
        base = base * square + term
    return value * top / base


def gelu_parts(preact):
    ramp = 0.5 * (1.0 + erf(preact * (1.0 / math.sqrt(2.0))))
    bell = jnp.exp(-0.5 * preact * preact) * (1.0 / math.sqrt(2.0 * math.pi))
    return preact * ramp, ramp + preact * bell


def pack(spectra, out_ref, main, rest):
    main[...] = jnp.transpose(spectra[:128, :])
    for g in range(16):
        out_ref[g, 0:16, :] = main[pl.ds(g, 16, stride=16), :]
    left, right = spectra[128:, :128], spectra[128:, 128:]
    lane = iota((32, 128), 1) % 64 // 16
    pieces = []
    for m in range(4):
        first = pltpu.roll(left, (128 - 16 * m) % 128, 1)
        second = pltpu.roll(right, (144 - 16 * m) % 128, 1)
        pieces.append(jnp.where(lane == 0, first, jnp.where(lane == 1, second, 0.0)))
    rest[...] = jnp.transpose(jnp.concatenate(pieces, axis=0))
    for g in range(16):
        out_ref[g, 16:24, :] = rest[pl.ds(g, 8, stride=16), :]


def unpack(blocks, main, rest):
    for g in range(16):
        main[pl.ds(g, 16, stride=16), :] = blocks[g, 0:16, :]
        rest[pl.ds(g, 8, stride=16), :] = blocks[g, 16:24, :]
    turned = jnp.transpose(rest[...])
    lane = iota((32, 128), 1) % 64 // 16
    left = right = jnp.zeros((32, 128), F32)
    for m in range(4):
        piece = turned[32 * m : 32 * m + 32, :]
        left = jnp.where(lane == m, pltpu.roll(piece, 16 * m, 1), left)
        right = jnp.where(lane == m, pltpu.roll(piece, (112 + 16 * m) % 128, 1), right)
    return jnp.concatenate(
        [jnp.transpose(main[...]), jnp.concatenate([left, right], axis=1)], axis=0
    )


def rotate(value, sign):
    return sign * pltpu.roll(value, 4, 0)


def turn_sign():
    return jnp.where(iota((8, 128), 0) < 4, -1.0, 1.0).astype(F32)


def pad_rows():
    return iota((8, 128), 0) % 4 >= 2


def start_kernel(field, ahead, out_ref, main, rest, near, table, sems):
    first = pltpu.make_async_copy(field, near, sems.at[0])
    second = pltpu.make_async_copy(ahead, table, sems.at[1])
    first.start()
    second.start()
    first.wait()
    second.wait()
    pack(dot_rows(near[...], table[...]), out_ref, main, rest)


def prepare_kernel(pointwise, biases, local_back, local_ahead, offsets):
    owner = (iota((ROWS, C), 0) // 8 == iota((ROWS, C), 1)).astype(F32)
    same = iota((ROWS, ROWS), 0) % 8 == iota((ROWS, ROWS), 1) % 8
    for layer in range(2):
        mixing = pointwise[layer].astype(F32)
        rows = jnp.dot(owner, mixing, precision=HIGH, preferred_element_type=F32)
        wide = lax.dot_general(
            rows, owner, (((1,), (1,)), ((), ())), precision=HIGH, preferred_element_type=F32
        )
        wide = jnp.where(same, wide, 0.0)
        local_back[layer] = wide.astype(BF16)
        padded = jnp.zeros((256, 256), F32)
        padded = jnp.concatenate(
            [
                jnp.concatenate([wide, jnp.zeros((ROWS, 96), F32)], axis=1),
                jnp.zeros((96, 256), F32),
            ],
            axis=0,
        )
        local_ahead[layer] = jnp.transpose(padded)[:ROWS, :ROWS].astype(BF16)
    offsets[...] = lax.dot_general(
        owner, biases[...], (((1,), (1,)), ((), ())), precision=HIGH, preferred_element_type=F32
    )


def entry(table, core, jj, kx):
    first, second = (jnp.where(core == 0, float(a), float(b)) for a, b in zip(*table[:, jj, kx]))
    return first, second


def x_ahead_kernel(table, blocks, out_ref):
    core = lax.axis_index("core")
    sign = turn_sign()
    place = iota((8, 128), 0) % 4
    for part in range(3):
        rows = slice(8 * part, 8 * part + 8)
        groups = [[None] * 4 for _ in range(4)]
        turned = [[None] * 4 for _ in range(4)]
        for jj in range(4):
            x0, x1, x2, x3 = (blocks[jj + 4 * i, rows, :] for i in range(4))
            even, odd = x0 + x2, x0 - x2
            even_other, odd_other = x1 + x3, rotate(x1 - x3, sign)
            found = (even + even_other, odd - odd_other, even - even_other, odd + odd_other)
            for k in range(4):
                groups[k][jj] = found[k]
                turned[k][jj] = rotate(found[k], sign)
        modes = []
        for kx in range(KX):
            total = None
            for jj in range(4):
                real, imag = entry(table, core, jj, kx)
                term = real * groups[kx % 4][jj] + imag * turned[kx % 4][jj]
                total = term if total is None else total + term
            if part < 2:
                out_ref[part * 8 + kx // 2, (kx % 2) * 8 : (kx % 2) * 8 + 8, :] = total
            else:
                modes.append(total)
        if part == 2:
            for k in range(8):
                first, second = modes[2 * k], modes[2 * k + 1]
                out_ref[k, 16:24, :] = jnp.where(
                    place == 0, first, jnp.where(place == 1, pltpu.roll(second, 1, 0), 0.0)
                )
                out_ref[8 + k, 16:24, :] = jnp.where(
                    place == 0, pltpu.roll(first, 7, 0), jnp.where(place == 1, second, 0.0)
                )


def x_behind_kernel(table, blocks, out_ref):
    core = lax.axis_index("core")
    sign = turn_sign()
    place = iota((8, 128), 0) % 4
    sums = blocks[0, 16:24, :]
    for k in range(1, 16):
        sums = sums + blocks[k, 16:24, :]
    for part in range(3):
        totals = [[None] * 4 for _ in range(4)]
        for kx in range(KX):
            if part < 2:
                mode = blocks[part * 8 + kx // 2, (kx % 2) * 8 : (kx % 2) * 8 + 8, :]
            else:
                first, second = blocks[kx // 2, 16:24, :], blocks[8 + kx // 2, 16:24, :]
                if kx % 2 == 0:
                    second = pltpu.roll(second, 1, 0)
                else:
                    first = pltpu.roll(first, 7, 0)
                mode = jnp.where(place == 0, first, jnp.where(place == 1, second, 0.0))
            turned = rotate(mode, sign)
            for jj in range(4):
                real, imag = entry(table, core, jj, kx)
                term = real * mode + imag * turned
                old = totals[kx % 4][jj]
                totals[kx % 4][jj] = term if old is None else old + term
        for jj in range(4):
            h0, h1, h2, h3 = (totals[k][jj] for k in range(4))
            even, odd = h0 + h2, h0 - h2
            even_other, odd_other = h1 + h3, rotate(h1 - h3, sign)
            found = (even + even_other, odd + odd_other, even - even_other, odd - odd_other)
            for i in range(4):
                value = found[i] if part < 2 else jnp.where(place >= 2, sums, found[i])
                out_ref[jj + 4 * i, 8 * part : 8 * part + 8, :] = value


def y_ahead(blocks, cosines, sines, channels, wide):
    low = iota((8, 128), 0) < 4
    keep = iota((8, 128), 0) % 4 == iota((8, 128), 1) // 32
    mains, rests = [], []
    for y in range(8):
        main, rest = [], []
        other = blocks[y, 16:24, :] + blocks[8 + y, 16:24, :]
        for k in range(2):
            rows = slice(8 * k, 8 * k + 8)
            value = blocks[y, rows, :] + blocks[8 + y, rows, :]
            swapped = pltpu.roll(value, 4, 0)
            main.append((jnp.where(low, value, swapped), jnp.where(low, swapped, value)))
            rest.append(
                (
                    jnp.broadcast_to(other[k : k + 1, :], (8, 128)),
                    jnp.broadcast_to(other[4 + k : 5 + k, :], (8, 128)),
                )
            )
        mains.append(main)
        rests.append(rest)
    for pair in range(8):
        rows = slice(8 * pair, 8 * pair + 8)
        for lanes, source in ((slice(0, 128), mains), (slice(128, 256), rests)):
            for k in range(2):
                real = imag = None
                for y in range(8):
                    cos, sin = cosines[y, rows, :], sines[y, rows, :]
                    first, second = source[y][k]
                    add_real = first * cos + second * sin
                    add_imag = second * cos - first * sin
                    real = add_real if real is None else real + add_real
                    imag = add_imag if imag is None else imag + add_imag
                if source is rests:
                    real, imag = jnp.where(keep, real, 0.0), jnp.where(keep, imag, 0.0)
                at = 64 * k + 8 * pair
                wide[at : at + 8, lanes] = real
                wide[128 + at : 136 + at, lanes] = imag
    return dot2(wide[...], channels[...])


def y_behind(modes, cosines, sines, spread, scale, pads, wide, out_ref):
    wide[...] = dot2(modes, spread[...])
    row = iota((8, 128), 0)
    low = row < 4
    keep = row % 4 == iota((8, 128), 1) // 32
    for y in range(8):
        rests = []
        for k in range(2):
            for lanes in (slice(0, 128), slice(128, 256)):
                real = imag = None
                for pair in range(8):
                    rows = slice(8 * pair, 8 * pair + 8)
                    cos, sin = cosines[y, rows, :], sines[y, rows, :]
                    at = 64 * k + 8 * pair
                    first, second = wide[at : at + 8, lanes], wide[128 + at : 136 + at, lanes]
                    add_real = first * cos - second * sin
                    add_imag = first * sin + second * cos
                    real = add_real if real is None else real + add_real
                    imag = add_imag if imag is None else imag + add_imag
                if lanes.start == 0:
                    real = real + pltpu.roll(real, 4, 0)
                    imag = imag + pltpu.roll(imag, 4, 0)
                    value = jnp.where(low, real, imag) * scale
                    out_ref[y, 8 * k : 8 * k + 8, :] = value
                    out_ref[8 + y, 8 * k : 8 * k + 8, :] = value
                else:
                    both = []
                    for value in (real, imag):
                        value = jnp.where(keep, value, 0.0)
                        for step in (4, 2, 1):
                            value = value + pltpu.roll(value, step, 0)
                        both.append(value * scale)
                    rests.append(both)
        value = pads
        for k in range(2):
            for r in range(2):
                value = jnp.where(row == 4 * r + k, rests[k][r], value)
        out_ref[y, 16:24, :] = value
        out_ref[8 + y, 16:24, :] = value


def fetch(layer, weights, near, sem):
    copy = pltpu.make_async_copy(weights.at[layer], near, sem)
    copy.start()
    return copy


def mix_kernel(
    layer, blocks, far, cosines, sines, channels, spread, out_ref, spectrum, wide, mixed, weights, sem
):
    copy = fetch(layer, far, weights, sem)
    spectrum[...] = y_ahead(blocks, cosines, sines, channels, wide)
    mixed[...] = jnp.zeros_like(mixed)
    copy.wait()
    for at in range(0, 128, 32):
        rows = slice(at, at + 32)
        under = slice(128 + at, 160 + at)
        real, imag = spectrum[rows, :], spectrum[under, :]
        out_real = out_imag = jnp.zeros((32, C), F32)
        for c in range(C):
            first = jnp.broadcast_to(real[:, c : c + 1], (32, C))
            second = jnp.broadcast_to(imag[:, c : c + 1], (32, C))
            w_real, w_imag = weights[0, c, rows, :], weights[1, c, rows, :]
            out_real += first * w_real - second * w_imag
            out_imag += first * w_imag + second * w_real
        mixed[rows, 0:C] = out_real
        mixed[under, 0:C] = out_imag
    y_behind(mixed[...], cosines, sines, spread, 2.0, jnp.zeros((8, 128), F32), wide, out_ref)


def mix_grad_kernel(
    layer, blocks, far, cosines, sines, channels, spread, field, slopes,
    out_ref, dmixed, wide, mixed, weights, sem,
):
    copy = fetch(layer, far, weights, sem)
    sums = cell_sums(field, slopes)
    dmixed[...] = 2.0 * y_ahead(blocks, cosines, sines, channels, wide)
    lane = iota((32, 128), 1)
    copy.wait()
    for at in range(0, 128, 32):
        rows = slice(at, at + 32)
        under = slice(128 + at, 160 + at)
        real, imag = dmixed[rows, 0:C], dmixed[under, 0:C]
        out_real = out_imag = jnp.zeros((32, 128), F32)
        for c in range(C):
            w_real, w_imag = weights[0, c, rows, :], weights[1, c, rows, :]
            add_real = jnp.sum(w_real * real + w_imag * imag, axis=1, keepdims=True)
            add_imag = jnp.sum(w_real * imag - w_imag * real, axis=1, keepdims=True)
            out_real = jnp.where(lane == c, add_real, out_real)
            out_imag = jnp.where(lane == c, add_imag, out_imag)
        mixed[rows, :] = out_real
        mixed[under, :] = out_imag
    y_behind(mixed[...], cosines, sines, spread, 1.0, sums, wide, out_ref)


def weight_grad_body(spectrum, dmixed, out_ref, scale):
    for at in range(0, 128, 32):
        rows = slice(at, at + 32)
        under = slice(128 + at, 160 + at)
        real, imag = dmixed[rows, 0:C] * scale, dmixed[under, 0:C] * scale
        s_real, s_imag = spectrum[rows, :], spectrum[under, :]
        for c in range(C):
            first = jnp.broadcast_to(s_real[:, c : c + 1], (32, C))
            second = jnp.broadcast_to(s_imag[:, c : c + 1], (32, C))
            out_ref[0, 0, c, rows, :] = first * real - second * imag
            out_ref[0, 1, c, rows, :] = first * imag + second * real


MODE_SCALE = math.sqrt(2.0 * KX * KY * KZ * KT / (NX * NY * NZ * NT))
CELL_SCALE = 1.0 / math.sqrt(NX * NY * NZ * NT)


def weight_grad_first(spectrum, dmixed, out_ref):
    weight_grad_body(spectrum, dmixed, out_ref, MODE_SCALE)


def weight_grad_second(spectrum, dmixed, held, out_ref):
    weight_grad_body(spectrum, dmixed, out_ref, MODE_SCALE)


def layer_kernel(blocks, field, local, offset, ahead, behind, out_ref, new_field, slope, main, rest):
    layer = 0
    high, low = halves(unpack(blocks, main, rest))
    spectra = None
    for at in range(0, Q, 256):
        cols = slice(at, at + 256)
        table = behind[:, cols]
        preact = jnp.dot(high, table, preferred_element_type=F32)
        preact += jnp.dot(low, table, preferred_element_type=F32)
        preact += jnp.dot(local[layer], field[:, cols], preferred_element_type=F32)
        preact += offset[:, layer : layer + 1]
        value, factor = gelu_parts(preact)
        value = value.astype(BF16)
        new_field[:, cols] = value
        slope[:, cols] = factor
        term = dot_rows(value, ahead[:, cols])
        spectra = term if spectra is None else spectra + term
    pack(spectra, out_ref, main, rest)


def top_kernel(
    blocks, field, local, offset, above, behind, out_ref, final, slopes, main, rest, upstream, sem
):
    layer = 1
    copy = pltpu.make_async_copy(above, upstream, sem)
    copy.start()
    high, low = halves(unpack(blocks, main, rest))
    copy.wait()
    spectra = None
    for at in range(0, Q, 256):
        cols = slice(at, at + 256)
        table = behind[:, cols]
        preact = jnp.dot(high, table, preferred_element_type=F32)
        preact += jnp.dot(low, table, preferred_element_type=F32)
        preact += jnp.dot(local[layer], field[:, cols], preferred_element_type=F32)
        preact += offset[:, layer : layer + 1]
        value, factor = gelu_parts(preact)
        final[:, cols] = value
        slope = (upstream[:, cols].astype(F32) * factor).astype(BF16)
        slopes[:, cols] = slope
        term = dot_rows(slope, table)
        spectra = term if spectra is None else spectra + term
    pack(spectra, out_ref, main, rest)


def block_sums(blocks):
    total = blocks[0, 16:24, :]
    for g in range(1, 16):
        total = total + blocks[g, 16:24, :]
    return jnp.where(pad_rows(), total, 0.0)


def back_kernel(
    blocks, slopes, local, factor, ahead, behind, out_ref, new_slopes, sums, main, rest
):
    layer = 1
    sums[...] = block_sums(blocks)
    high, low = halves(unpack(blocks, main, rest))
    spectra = None
    for at in range(0, Q, 256):
        cols = slice(at, at + 256)
        table = ahead[:, cols]
        grad = jnp.dot(high, table, preferred_element_type=F32)
        grad += jnp.dot(low, table, preferred_element_type=F32)
        grad += jnp.dot(local[layer], slopes[:, cols], preferred_element_type=F32)
        grad = grad.astype(BF16).astype(F32)
        slope = (grad * factor[:, cols]).astype(BF16)
        new_slopes[:, cols] = slope
        term = dot_rows(slope, behind[:, cols])
        spectra = term if spectra is None else spectra + term
    pack(spectra, out_ref, main, rest)


def end_kernel(blocks, slopes, local, ahead, later, grad_ref, mixing, offsets, main, rest):
    for at_layer, total in ((0, block_sums(blocks)), (1, later[...])):
        row = iota((24, 8), 0) // 6
        col = iota((24, 8), 1)
        pick = sum(((row == i) & (col == PADS[i])).astype(F32) for i in range(4))
        wide = jnp.dot(pick, total, precision=HIGH, preferred_element_type=F32)
        wide = jnp.where(iota((24, 128), 1) // C == iota((24, 128), 0) % 6, wide, 0.0)
        place = (iota((128, 128), 0) % C == iota((128, 128), 1)).astype(F32)
        found = jnp.dot(wide, place, precision=HIGH, preferred_element_type=F32) * CELL_SCALE
        for c in range(C):
            mixing[c, at_layer : at_layer + 1, :] = found[c : c + 1, 0:C]
        offsets[at_layer : at_layer + 1, :] = found[C : C + 1, 0:C]
    layer = 0
    high, low = halves(unpack(blocks, main, rest))
    for at in range(0, Q, 256):
        cols = slice(at, at + 256)
        table = ahead[:, cols]
        grad = jnp.dot(high, table, preferred_element_type=F32)
        grad += jnp.dot(low, table, preferred_element_type=F32)
        grad += jnp.dot(local[layer], slopes[:, cols], preferred_element_type=F32)
        grad_ref[:, cols] = grad


def cell_sums(field, slopes):
    slope = slopes[...]
    pairs = jnp.concatenate(
        [dot_rows(field[...], slope), dot_rows(jnp.ones((8, Q), BF16), slope)], axis=0
    )
    pairs = jnp.where(iota((168, ROWS), 0) % 8 == iota((168, ROWS), 1) % 8, pairs, 0.0)
    lane = iota((ROWS, 128), 1)
    place = ((lane < 6 * C) & (lane % C == iota((ROWS, 128), 0) // 8)).astype(F32)
    wide = jnp.dot(pairs, place, precision=HIGH, preferred_element_type=F32)
    wide = jnp.where(iota((168, 128), 1) // C == iota((168, 128), 0) // 8 % 6, wide, 0.0)
    row = iota((8, 168), 0)
    owner = iota((8, 168), 1) // 48
    pick = sum(((owner == i) & (row == PADS[i])).astype(F32) for i in range(4))
    return jnp.dot(pick, wide, precision=HIGH, preferred_element_type=F32)


VM = pl.BlockSpec(memory_space=pltpu.VMEM)
FAR = pl.BlockSpec(memory_space=pltpu.HBM)
BLOCKS = jax.ShapeDtypeStruct((16, 24, 128), F32)
MODES = jax.ShapeDtypeStruct((256, 128), F32)
WIDE16 = jax.ShapeDtypeStruct((ROWS, Q), BF16)
WIDE32 = jax.ShapeDtypeStruct((ROWS, Q), F32)
SUMS = jax.ShapeDtypeStruct((8, 128), F32)
TURN = [pltpu.VMEM((256, 128), F32), pltpu.VMEM((128, 128), F32)]
MIX = [
    pltpu.VMEM((256, 256), F32),
    pltpu.VMEM((256, 128), F32),
    pltpu.VMEM((2, C, 128, C), F32),
    pltpu.SemaphoreType.DMA,
]


def call(kernel, shapes, scratch, *operands, specs=None, cost=None):
    many = isinstance(shapes, (list, tuple))
    return pl.pallas_call(
        kernel,
        out_shape=shapes,
        in_specs=specs or [VM] * len(operands),
        out_specs=[VM] * len(shapes) if many else VM,
        scratch_shapes=scratch,
        compiler_params=PARAMS,
        cost_estimate=cost,
    )(*operands)


def swap_rows(value):
    return lax.all_to_all(value, ("z", "h"), split_axis=0, concat_axis=0, tiled=True)


def swap_cols(value):
    return lax.all_to_all(value, ("core", "ylo", "x"), split_axis=0, concat_axis=0, tiled=True)


def per_device(hidden_in, spectral, pointwise, biases, upstream):
    ahead, behind = (jnp.asarray(t) for t in depth_tables())
    cosines, sines = (jnp.asarray(t) for t in column_tables())
    channels = jnp.asarray(channel_table())
    spread = jnp.asarray(np.ascontiguousarray(channel_table().T))
    root = 1.0 / math.sqrt(NX)
    to_modes = [row_table(-1.0, f) for f in (root, 0.25)]
    to_rows = [row_table(1.0, f) for f in (0.25, root)]
    field = jnp.transpose(hidden_in[0], (1, 0, 2)).reshape(ROWS, Q)
    above = jnp.transpose(upstream[0], (1, 0, 2)).reshape(ROWS, Q)
    weights = jnp.transpose(spectral, (0, 1, 2, 4, 5, 6, 3)).reshape(2, 2, C, 128, C)

    def x_step(kernel, table, blocks):
        return call(functools.partial(kernel, table), BLOCKS, [], blocks)

    def mix_step(kernel, layer, blocks, *more):
        operands = (blocks, weights, cosines, sines, channels, spread) + more
        return call(
            functools.partial(kernel, layer),
            [BLOCKS, MODES],
            MIX,
            *operands,
            specs=[VM, FAR] + [VM] * (len(operands) - 2),
        )

    def weight_grad(layer, spectrum, dmixed, held=None):
        out_spec = pl.BlockSpec((1, 2, C, 128, C), lambda i: (layer, 0, 0, 0, 0))
        mode_spec = pl.BlockSpec((256, 128), lambda i: (0, 0))
        operands = (spectrum, dmixed) + (() if held is None else (held,))
        return pl.pallas_call(
            weight_grad_first if held is None else weight_grad_second,
            grid=(1,),
            out_shape=jax.ShapeDtypeStruct((2, 2, C, 128, C), F32),
            in_specs=[mode_spec, mode_spec] + [pl.BlockSpec(memory_space=pl.ANY)] * (held is not None),
            out_specs=out_spec,
            input_output_aliases={} if held is None else {2: 0},
            compiler_params=PARAMS,
            cost_estimate=pl.CostEstimate(flops=2000000, bytes_accessed=3000000, transcendentals=0),
        )(*operands)

    def round_trip(blocks, step, side):
        blocks = swap_rows(blocks)
        blocks = swap_cols(x_step(x_ahead_kernel, to_modes[side], blocks))
        blocks, modes = step(blocks)
        blocks = swap_cols(blocks)
        blocks = swap_rows(x_step(x_behind_kernel, to_rows[side], blocks))
        return blocks, modes

    loads = [pltpu.VMEM((ROWS, Q), BF16), pltpu.VMEM((256, Q), BF16), pltpu.SemaphoreType.DMA((2,))]
    blocks = call(start_kernel, BLOCKS, TURN + loads, field, ahead, specs=[FAR, FAR])
    squares = jax.ShapeDtypeStruct((2, ROWS, ROWS), BF16)
    local_back, local_ahead, offsets = call(
        prepare_kernel,
        [squares, squares, jax.ShapeDtypeStruct((ROWS, 2), F32)],
        [],
        pointwise,
        biases,
        cost=pl.CostEstimate(flops=60000000, bytes_accessed=700000, transcendentals=0),
    )
    blocks, spectrum_0 = round_trip(blocks, lambda b: mix_step(mix_kernel, 0, b), 0)
    blocks, field_1, factor_0 = call(
        layer_kernel, [BLOCKS, WIDE16, WIDE32], TURN,
        blocks, field, local_ahead, offsets, ahead, behind,
    )
    blocks, spectrum_1 = round_trip(blocks, lambda b: mix_step(mix_kernel, 1, b), 0)
    blocks, final, slopes_1 = call(
        top_kernel, [BLOCKS, WIDE32, WIDE16],
        TURN + [pltpu.VMEM((ROWS, Q), BF16), pltpu.SemaphoreType.DMA],
        blocks, field_1, local_ahead, offsets, above, behind,
        specs=[VM] * 4 + [FAR, VM],
    )
    blocks, dmixed_1 = round_trip(blocks, lambda b: mix_step(mix_grad_kernel, 1, b, field_1, slopes_1), 1)
    grads = weight_grad(1, spectrum_1, dmixed_1)
    blocks, slopes_0, later = call(
        back_kernel, [BLOCKS, WIDE16, SUMS], TURN,
        blocks, slopes_1, local_back, factor_0, ahead, behind,
    )
    blocks, dmixed_0 = round_trip(blocks, lambda b: mix_step(mix_grad_kernel, 0, b, field, slopes_0), 1)
    grads = weight_grad(0, spectrum_0, dmixed_0, grads)
    grad_hidden, mixing, offset_grads = call(
        end_kernel,
        [WIDE32, jax.ShapeDtypeStruct((C, 2, C), F32), jax.ShapeDtypeStruct((2, C), F32)],
        TURN,
        blocks, slopes_0, local_back, ahead, later,
    )

    def cells(value):
        return jnp.transpose(value.reshape(C, 8, Q), (1, 0, 2))[None]

    grad_spectral = jnp.transpose(grads.reshape(2, 2, C, 2, 16, 4, C), (0, 1, 2, 6, 3, 4, 5))
    return (
        cells(final),
        cells(grad_hidden),
        grad_spectral,
        jnp.transpose(mixing, (1, 0, 2)),
        offset_grads,
    )


def solution(mesh):
    names = ("z", "h", "core", "ylo", "x")
    fine = Mesh(mesh.devices.reshape(8, 2, 2, 2, 4), names)
    rows, cols = ("z", "h", "core"), ("ylo", "x")
    grid = P(rows, cols, None, None)
    modes = P(None, None, None, None, cols, None, rows)
    return jax.shard_map(
        per_device,
        mesh=fine,
        in_specs=(grid, modes, P(), P(), grid),
        out_specs=(grid, grid, modes, P(), P()),
        check_vma=False,
    )
```

```python
import functools
import math

import jax
import jax.numpy as jnp
import ml_dtypes
import numpy as np
from jax import lax
from jax.experimental import pallas as pl
from jax.experimental.pallas import tpu as pltpu
from jax.sharding import Mesh, PartitionSpec as P

KX = 16
KY = 16
KZ = 16
KT = 8
NZ = 64
NT = 16
NX = 32
NY = 64
C = 20
Q = NZ * NT
ROWS = 160
PADS = (2, 3, 6, 7)

F32 = jnp.float32
BF16 = jnp.bfloat16
HIGH = lax.Precision.HIGHEST
PARAMS = pltpu.CompilerParams(vmem_limit_bytes=32 * 1024 * 1024)


def depth_tables():
    rows = np.arange(256)
    g, m4, r, mh = rows % 16, rows // 16 % 4, rows // 64 % 2, rows // 128
    m = 16 * (g // 2) + 8 * mh + 4 * (g % 2) + m4
    freq_z, freq_t = m // KT - KZ // 2, m % KT
    cells = np.arange(Q)
    phase = (freq_z[:, None] * (cells // NT) * NT + freq_t[:, None] * (cells % NT) * NZ) % Q
    angle = phase * (2.0 * np.pi / Q)
    parts = np.where(r[:, None] == 0, np.cos(angle), -np.sin(angle))
    weight = np.where(freq_t == 0, 1.0, 2.0)[:, None]
    ahead = (parts / math.sqrt(Q)).astype(np.float32).astype(ml_dtypes.bfloat16)
    behind = (parts * weight / math.sqrt(2 * KZ * KT)).astype(np.float32)
    return ahead, behind.astype(ml_dtypes.bfloat16)


def row_table(sign, factor):
    half, jj, kx = np.meshgrid(np.arange(2), np.arange(4), np.arange(KX), indexing="ij")
    x = 4 * (jj // 2) + 2 * half + jj % 2
    angle = (x * (kx - KX // 2) % NX) * (2.0 * np.pi / NX)
    pairs = np.stack([np.cos(angle), sign * np.sin(angle)], axis=-1) * factor
    pairs = pairs.astype(np.float32).astype(ml_dtypes.bfloat16).astype(np.float32)
    return pairs


def column_table():
    y = np.arange(128)[None, :] % 8
    ky = np.arange(64)[:, None] // 4
    angle = (y * (ky - KY // 2) % NY) * (2.0 * np.pi / NY)
    both = np.concatenate([np.cos(angle), np.sin(angle)], axis=0) / math.sqrt(NY)
    return both.astype(np.float32)


def iota(shape, axis):
    return lax.broadcasted_iota(jnp.int32, shape, axis)


def halves(value):
    high = value.astype(BF16)
    return high, (value - high.astype(F32)).astype(BF16)


def dot2(value, table):
    high, low = halves(value)
    return jnp.dot(high, table, preferred_element_type=F32) + jnp.dot(
        low, table, preferred_element_type=F32
    )


def dot_rows(left, right):
    return lax.dot_general(left, right, (((1,), (1,)), ((), ())), preferred_element_type=F32)


def erf(value):
    value = jnp.clip(value, -3.832506856900711, 3.832506856900711)
    square = value * value
    top = jnp.full_like(value, 0.00022905065861350646)
    for term in (0.0034082910107109506, 0.050955695062380861, 0.18520832239976145, 1.128379143519084):
        top = top * square + term
    base = jnp.full_like(value, -1.1791602954361697e-7)
    for term in (
        0.000023547966471313185,
        0.0010179625278914885,
        0.014070470171167667,
        0.11098505178285362,
        0.49746925110067538,
        1.0,
    ):
        base = base * square + term
    return value * top / base


def gelu_parts(preact):
    ramp = 0.5 * (1.0 + erf(preact * (1.0 / math.sqrt(2.0))))
    bell = jnp.exp(-0.5 * preact * preact) * (1.0 / math.sqrt(2.0 * math.pi))
    return preact * ramp, ramp + preact * bell


def pack(spectra, out_ref, main, rest):
    main[...] = jnp.transpose(spectra[:128, :])
    for g in range(16):
        out_ref[g, 0:16, :] = main[pl.ds(g, 16, stride=16), :]
    left, right = spectra[128:, :128], spectra[128:, 128:]
    lane = iota((32, 128), 1) % 64 // 16
    pieces = []
    for m in range(4):
        first = pltpu.roll(left, (128 - 16 * m) % 128, 1)
        second = pltpu.roll(right, (144 - 16 * m) % 128, 1)
        pieces.append(jnp.where(lane == 0, first, jnp.where(lane == 1, second, 0.0)))
    rest[...] = jnp.transpose(jnp.concatenate(pieces, axis=0))
    for g in range(16):
        out_ref[g, 16:24, :] = rest[pl.ds(g, 8, stride=16), :]


def unpack(blocks, main, rest):
    for g in range(16):
        main[pl.ds(g, 16, stride=16), :] = blocks[g, 0:16, :]
        rest[pl.ds(g, 8, stride=16), :] = blocks[g, 16:24, :]
    turned = jnp.transpose(rest[...])
    lane = iota((32, 128), 1) % 64 // 16
    left = right = jnp.zeros((32, 128), F32)
    for m in range(4):
        piece = turned[32 * m : 32 * m + 32, :]
        left = jnp.where(lane == m, pltpu.roll(piece, 16 * m, 1), left)
        right = jnp.where(lane == m, pltpu.roll(piece, (112 + 16 * m) % 128, 1), right)
    return jnp.concatenate(
        [jnp.transpose(main[...]), jnp.concatenate([left, right], axis=1)], axis=0
    )


def rotate(value, sign):
    return sign * pltpu.roll(value, 4, 0)


def turn_sign():
    return jnp.where(iota((8, 128), 0) < 4, -1.0, 1.0).astype(F32)


def pad_rows():
    return iota((8, 128), 0) % 4 >= 2


def start_kernel(field, ahead, out_ref, token, main, rest, near, table, sems):
    first = pltpu.make_async_copy(field, near, sems.at[0])
    second = pltpu.make_async_copy(ahead, table, sems.at[1])
    first.start()
    second.start()
    first.wait()
    second.wait()
    token[...] = jnp.zeros_like(token)
    pack(dot_rows(near[...], table[...]), out_ref, main, rest)


def prepare_kernel(
    token, weights, table, pointwise, biases,
    first, second, twiddle, local_back, local_ahead, offsets, near, padded_rows, sems,
):
    copies = [
        pltpu.make_async_copy(weights.at[layer], near.at[layer], sems.at[layer]) for layer in range(2)
    ]
    for copy in copies:
        copy.start()
    twiddle[...] = table[...] + 0.0 * token[0:1, :]
    padded_rows[...] = jnp.zeros_like(padded_rows)
    owner = (iota((ROWS, C), 0) // 8 == iota((ROWS, C), 1)).astype(F32)
    same = iota((ROWS, ROWS), 0) % 8 == iota((ROWS, ROWS), 1) % 8
    for layer in range(2):
        mixing = pointwise[layer].astype(F32)
        rows = jnp.dot(owner, mixing, precision=HIGH, preferred_element_type=F32)
        wide = lax.dot_general(
            rows, owner, (((1,), (1,)), ((), ())), precision=HIGH, preferred_element_type=F32
        )
        wide = jnp.where(same, wide, 0.0)
        local_back[layer] = wide.astype(BF16)
        padded = jnp.zeros((256, 256), F32)
        padded = jnp.concatenate(
            [
                jnp.concatenate([wide, jnp.zeros((ROWS, 96), F32)], axis=1),
                jnp.zeros((96, 256), F32),
            ],
            axis=0,
        )
        local_ahead[layer] = jnp.transpose(padded)[:ROWS, :ROWS].astype(BF16)
    offsets[...] = lax.dot_general(
        owner, biases[...], (((1,), (1,)), ((), ())), precision=HIGH, preferred_element_type=F32
    )
    for layer, out_ref in ((0, first), (1, second)):
        copies[layer].wait()
        for part in range(2):
            for c in range(C):
                slot = c % 4
                padded_rows[slot, :, 0:C] = near[layer, part, c]
                out_ref[part, c] = jnp.transpose(padded_rows[slot])[:24, :]


def entry(table, half, jj, kx):
    first, second = (jnp.where(half == 0, float(a), float(b)) for a, b in zip(*table[:, jj, kx]))
    return first, second


def x_ahead_kernel(table, blocks, *others):
    out_ref = others[-1]
    half = lax.axis_index("h")
    sign = turn_sign()
    place = iota((8, 128), 0) % 4
    for part in range(3):
        rows = slice(8 * part, 8 * part + 8)
        groups = [[None] * 4 for _ in range(4)]
        turned = [[None] * 4 for _ in range(4)]
        for jj in range(4):
            x0, x1, x2, x3 = (blocks[jj + 4 * i, rows, :] for i in range(4))
            even, odd = x0 + x2, x0 - x2
            even_other, odd_other = x1 + x3, rotate(x1 - x3, sign)
            found = (even + even_other, odd - odd_other, even - even_other, odd + odd_other)
            for k in range(4):
                groups[k][jj] = found[k]
                turned[k][jj] = rotate(found[k], sign)
        modes = []
        for kx in range(KX):
            total = None
            for jj in range(4):
                real, imag = entry(table, half, jj, kx)
                term = real * groups[kx % 4][jj] + imag * turned[kx % 4][jj]
                total = term if total is None else total + term
            if part < 2:
                out_ref[part * 8 + kx // 2, (kx % 2) * 8 : (kx % 2) * 8 + 8, :] = total
            else:
                modes.append(total)
        if part == 2:
            for k in range(8):
                first, second = modes[2 * k], modes[2 * k + 1]
                out_ref[k, 16:24, :] = jnp.where(
                    place == 0, first, jnp.where(place == 1, pltpu.roll(second, 1, 0), 0.0)
                )
                out_ref[8 + k, 16:24, :] = jnp.where(
                    place == 0, pltpu.roll(first, 7, 0), jnp.where(place == 1, second, 0.0)
                )


def x_behind_kernel(table, blocks, out_ref):
    half = lax.axis_index("h")
    sign = turn_sign()
    place = iota((8, 128), 0) % 4
    sums = blocks[0, 16:24, :]
    for k in range(1, 16):
        sums = sums + blocks[k, 16:24, :]
    for part in range(3):
        totals = [[None] * 4 for _ in range(4)]
        for kx in range(KX):
            if part < 2:
                mode = blocks[part * 8 + kx // 2, (kx % 2) * 8 : (kx % 2) * 8 + 8, :]
            else:
                first, second = blocks[kx // 2, 16:24, :], blocks[8 + kx // 2, 16:24, :]
                if kx % 2 == 0:
                    second = pltpu.roll(second, 1, 0)
                else:
                    first = pltpu.roll(first, 7, 0)
                mode = jnp.where(place == 0, first, jnp.where(place == 1, second, 0.0))
            turned = rotate(mode, sign)
            for jj in range(4):
                real, imag = entry(table, half, jj, kx)
                term = real * mode + imag * turned
                old = totals[kx % 4][jj]
                totals[kx % 4][jj] = term if old is None else old + term
        for jj in range(4):
            h0, h1, h2, h3 = (totals[k][jj] for k in range(4))
            even, odd = h0 + h2, h0 - h2
            even_other, odd_other = h1 + h3, rotate(h1 - h3, sign)
            found = (even + even_other, odd + odd_other, even - even_other, odd - odd_other)
            for i in range(4):
                value = found[i] if part < 2 else jnp.where(place >= 2, sums, found[i])
                out_ref[jj + 4 * i, 8 * part : 8 * part + 8, :] = value


def channel_rows():
    lane = iota((32, 256), 1)
    owner = jnp.where(lane < 128, lane // 8, 16 + lane // 8 % 4)
    return (owner == iota((32, 256), 0)).astype(F32).astype(BF16)


def times(value, factor):
    return (
        value[0] * factor[0] - value[1] * factor[1],
        value[0] * factor[1] + value[1] * factor[0],
    )


def plus(one, two):
    return one[0] + two[0], one[1] + two[1]


def minus(one, two):
    return one[0] - two[0], one[1] - two[1]


def fourth(values, sign):
    even, odd = plus(values[0], values[2]), minus(values[0], values[2])
    even_other, odd_other = plus(values[1], values[3]), minus(values[1], values[3])
    turned = (-sign * odd_other[1], sign * odd_other[0])
    return plus(even, even_other), plus(odd, turned), minus(even, even_other), minus(odd, turned)


def odd_turn(y, sign):
    low = iota((8, 128), 0) < 4
    angle = math.pi * y / 4
    return jnp.where(low, 1.0, math.cos(angle)), jnp.where(low, 0.0, sign * math.sin(angle))


def y_ahead(blocks, twiddle, wide):
    low = iota((8, 128), 0) < 4
    keep = iota((8, 128), 0) % 4 == iota((8, 128), 1) // 32
    units = [[] for _ in range(4)]
    for y in range(8):
        other = blocks[y, 16:24, :] + blocks[8 + y, 16:24, :]
        for k in range(2):
            rows = slice(8 * k, 8 * k + 8)
            value = blocks[y, rows, :] + blocks[8 + y, rows, :]
            swapped = pltpu.roll(value, 4, 0)
            units[k].append((jnp.where(low, value, swapped), jnp.where(low, swapped, value)))
            units[2 + k].append(
                (
                    jnp.broadcast_to(other[k : k + 1, :], (8, 128)),
                    jnp.broadcast_to(other[4 + k : 5 + k, :], (8, 128)),
                )
            )
    turns = [odd_turn(y, -1.0) for y in range(8)]
    for unit in range(4):
        values = [units[unit][0]] + [times(units[unit][y], turns[y]) for y in range(1, 8)]
        groups = fourth([plus(values[n], values[n + 4]) for n in range(4)], -1.0)
        lanes = slice(0, 128) if unit < 2 else slice(128, 256)
        for pair in range(8):
            at = 8 * pair
            factor = (twiddle[at : at + 8, :], -twiddle[64 + at : 72 + at, :])
            real, imag = times(groups[pair % 4], factor)
            if unit >= 2:
                real, imag = jnp.where(keep, real, 0.0), jnp.where(keep, imag, 0.0)
            at += 64 * (unit % 2)
            wide[at : at + 8, lanes] = real
            wide[128 + at : 136 + at, lanes] = imag
    high, low_part = halves(wide[...])
    table = channel_rows()
    return dot_rows(table, high) + dot_rows(table, low_part)


def y_behind(modes, twiddle, scale, pads, wide, out_ref):
    wide[...] = dot2(jnp.transpose(modes), channel_rows())
    row = iota((8, 128), 0)
    low = row < 4
    keep = row % 4 == iota((8, 128), 1) // 32
    turns = [odd_turn(y, 1.0) for y in range(8)]
    rests = [pads] * 8
    for unit in range(4):
        k = unit % 2
        lanes = slice(0, 128) if unit < 2 else slice(128, 256)
        values = []
        for pair in range(8):
            at = 8 * pair
            factor = (twiddle[at : at + 8, :] * scale, twiddle[64 + at : 72 + at, :] * scale)
            at += 64 * k
            values.append(times((wide[at : at + 8, lanes], wide[128 + at : 136 + at, lanes]), factor))
        groups = fourth([plus(values[n], values[n + 4]) for n in range(4)], 1.0)
        for y in range(8):
            real, imag = groups[y % 4] if y == 0 else times(groups[y % 4], turns[y])
            if unit < 2:
                real = real + pltpu.roll(real, 4, 0)
                imag = imag + pltpu.roll(imag, 4, 0)
                value = jnp.where(low, real, imag)
                out_ref[y, 8 * k : 8 * k + 8, :] = value
                out_ref[8 + y, 8 * k : 8 * k + 8, :] = value
            else:
                for r, value in ((0, real), (1, imag)):
                    value = jnp.where(keep, value, 0.0)
                    for step in (4, 2, 1):
                        value = value + pltpu.roll(value, step, 0)
                    rests[y] = jnp.where(row == 4 * r + k, value, rests[y])
    for y in range(8):
        out_ref[y, 16:24, :] = rests[y]
        out_ref[8 + y, 16:24, :] = rests[y]


def mix_kernel(blocks, weights, twiddle, out_ref, spectrum, wide, mixed):
    spectrum[...] = y_ahead(blocks, twiddle, wide)
    out_real = out_imag = jnp.zeros((24, 128), F32)
    for c in range(C):
        first = jnp.broadcast_to(spectrum[c : c + 1, 0:128], (24, 128))
        second = jnp.broadcast_to(spectrum[c : c + 1, 128:256], (24, 128))
        w_real, w_imag = weights[0, c], weights[1, c]
        out_real += first * w_real - second * w_imag
        out_imag += first * w_imag + second * w_real
    mixed[0:24, 0:128] = out_real
    mixed[0:24, 128:256] = out_imag
    mixed[24:32, :] = jnp.zeros((8, 256), F32)
    y_behind(mixed[...], twiddle, 2.0, jnp.zeros((8, 128), F32), wide, out_ref)


def mix_grad_kernel(blocks, weights, twiddle, field, slopes, out_ref, dmixed, wide, mixed):
    sums = cell_sums(field, slopes)
    dmixed[...] = 2.0 * y_ahead(blocks, twiddle, wide)
    real, imag = dmixed[0:24, 0:128], dmixed[0:24, 128:256]
    for c in range(C):
        w_real, w_imag = weights[0, c], weights[1, c]
        mixed[c : c + 1, 0:128] = jnp.sum(w_real * real + w_imag * imag, axis=0, keepdims=True)
        mixed[c : c + 1, 128:256] = jnp.sum(w_real * imag - w_imag * real, axis=0, keepdims=True)
    mixed[C:32, :] = jnp.zeros((32 - C, 256), F32)
    y_behind(mixed[...], twiddle, 1.0, sums, wide, out_ref)


def weight_grad_body(spectrum, dmixed, out_ref, scale):
    turned, other = jnp.transpose(spectrum[...]), jnp.transpose(dmixed[...]) * scale
    for at in range(0, 128, 32):
        rows = slice(at, at + 32)
        under = slice(128 + at, 160 + at)
        real, imag = other[rows, 0:C], other[under, 0:C]
        s_real, s_imag = turned[rows, :], turned[under, :]
        for c in range(C):
            first = jnp.broadcast_to(s_real[:, c : c + 1], (32, C))
            second = jnp.broadcast_to(s_imag[:, c : c + 1], (32, C))
            out_ref[0, 0, c, rows, :] = first * real - second * imag
            out_ref[0, 1, c, rows, :] = first * imag + second * real


MODE_SCALE = math.sqrt(2.0 * KX * KY * KZ * KT / (NX * NY * NZ * NT))
CELL_SCALE = 1.0 / math.sqrt(NX * NY * NZ * NT)


def weight_grad_first(spectrum, dmixed, out_ref):
    weight_grad_body(spectrum, dmixed, out_ref, MODE_SCALE)


def weight_grad_second(spectrum, dmixed, held, out_ref):
    weight_grad_body(spectrum, dmixed, out_ref, MODE_SCALE)


def layer_kernel(blocks, field, local, offset, ahead, behind, out_ref, new_field, slope, main, rest):
    layer = 0
    high, low = halves(unpack(blocks, main, rest))
    spectra = None
    for at in range(0, Q, 256):
        cols = slice(at, at + 256)
        table = behind[:, cols]
        preact = jnp.dot(high, table, preferred_element_type=F32)
        preact += jnp.dot(low, table, preferred_element_type=F32)
        preact += jnp.dot(local[layer], field[:, cols], preferred_element_type=F32)
        preact += offset[:, layer : layer + 1]
        value, factor = gelu_parts(preact)
        value = value.astype(BF16)
        new_field[:, cols] = value
        slope[:, cols] = factor
        term = dot_rows(value, ahead[:, cols])
        spectra = term if spectra is None else spectra + term
    pack(spectra, out_ref, main, rest)


def top_kernel(
    blocks, field, local, offset, above, behind, out_ref, slopes, main, rest, upstream, sem
):
    layer = 1
    copy = pltpu.make_async_copy(above, upstream, sem)
    copy.start()
    high, low = halves(unpack(blocks, main, rest))
    copy.wait()
    spectra = None
    for at in range(0, Q, 256):
        cols = slice(at, at + 256)
        table = behind[:, cols]
        preact = jnp.dot(high, table, preferred_element_type=F32)
        preact += jnp.dot(low, table, preferred_element_type=F32)
        preact += jnp.dot(local[layer], field[:, cols], preferred_element_type=F32)
        preact += offset[:, layer : layer + 1]
        factor = gelu_parts(preact)[1]
        slope = (upstream[:, cols].astype(F32) * factor).astype(BF16)
        slopes[:, cols] = slope
        term = dot_rows(slope, table)
        spectra = term if spectra is None else spectra + term
    pack(spectra, out_ref, main, rest)


def final_kernel(blocks, field, local, offset, behind, final, main, rest):
    layer = 1
    high, low = halves(unpack(blocks, main, rest))
    for at in range(0, Q, 256):
        cols = slice(at, at + 256)
        table = behind[:, cols]
        preact = jnp.dot(high, table, preferred_element_type=F32)
        preact += jnp.dot(low, table, preferred_element_type=F32)
        preact += jnp.dot(local[layer], field[:, cols], preferred_element_type=F32)
        preact += offset[:, layer : layer + 1]
        final[:, cols] = gelu_parts(preact)[0]


def block_sums(blocks):
    total = blocks[0, 16:24, :]
    for g in range(1, 16):
        total = total + blocks[g, 16:24, :]
    return jnp.where(pad_rows(), total, 0.0)


def back_kernel(
    blocks, slopes, local, factor, ahead, behind, out_ref, new_slopes, sums, main, rest
):
    layer = 1
    sums[...] = block_sums(blocks)
    high, low = halves(unpack(blocks, main, rest))
    spectra = None
    for at in range(0, Q, 256):
        cols = slice(at, at + 256)
        table = ahead[:, cols]
        grad = jnp.dot(high, table, preferred_element_type=F32)
        grad += jnp.dot(low, table, preferred_element_type=F32)
        grad += jnp.dot(local[layer], slopes[:, cols], preferred_element_type=F32)
        grad = grad.astype(BF16).astype(F32)
        slope = (grad * factor[:, cols]).astype(BF16)
        new_slopes[:, cols] = slope
        term = dot_rows(slope, behind[:, cols])
        spectra = term if spectra is None else spectra + term
    pack(spectra, out_ref, main, rest)


def end_kernel(blocks, slopes, local, ahead, later, grad_ref, mixing, offsets, main, rest):
    for at_layer, total in ((0, block_sums(blocks)), (1, later[...])):
        row = iota((24, 8), 0) // 6
        col = iota((24, 8), 1)
        pick = sum(((row == i) & (col == PADS[i])).astype(F32) for i in range(4))
        wide = jnp.dot(pick, total, precision=HIGH, preferred_element_type=F32)
        wide = jnp.where(iota((24, 128), 1) // C == iota((24, 128), 0) % 6, wide, 0.0)
        place = (iota((128, 128), 0) % C == iota((128, 128), 1)).astype(F32)
        found = jnp.dot(wide, place, precision=HIGH, preferred_element_type=F32) * CELL_SCALE
        for c in range(C):
            mixing[c, at_layer : at_layer + 1, :] = found[c : c + 1, 0:C]
        offsets[at_layer : at_layer + 1, :] = found[C : C + 1, 0:C]
    layer = 0
    high, low = halves(unpack(blocks, main, rest))
    for at in range(0, Q, 256):
        cols = slice(at, at + 256)
        table = ahead[:, cols]
        grad = jnp.dot(high, table, preferred_element_type=F32)
        grad += jnp.dot(low, table, preferred_element_type=F32)
        grad += jnp.dot(local[layer], slopes[:, cols], preferred_element_type=F32)
        grad_ref[:, cols] = grad


def cell_sums(field, slopes):
    slope = slopes[...]
    pairs = jnp.concatenate(
        [dot_rows(field[...], slope), dot_rows(jnp.ones((8, Q), BF16), slope)], axis=0
    )
    pairs = jnp.where(iota((168, ROWS), 0) % 8 == iota((168, ROWS), 1) % 8, pairs, 0.0)
    lane = iota((ROWS, 128), 1)
    place = ((lane < 6 * C) & (lane % C == iota((ROWS, 128), 0) // 8)).astype(F32)
    wide = dot2(pairs, place.astype(BF16))
    wide = jnp.where(iota((168, 128), 1) // C == iota((168, 128), 0) // 8 % 6, wide, 0.0)
    row = iota((8, 168), 0)
    owner = iota((8, 168), 1) // 48
    pick = sum(((owner == i) & (row == PADS[i])).astype(F32) for i in range(4))
    pick, (high, low) = pick.astype(BF16), halves(wide)
    return jnp.dot(pick, high, preferred_element_type=F32) + jnp.dot(
        pick, low, preferred_element_type=F32
    )


VM = pl.BlockSpec(memory_space=pltpu.VMEM)
FAR = pl.BlockSpec(memory_space=pltpu.HBM)
BLOCKS = jax.ShapeDtypeStruct((16, 24, 128), F32)
MODES = jax.ShapeDtypeStruct((32, 256), F32)
WIDE16 = jax.ShapeDtypeStruct((ROWS, Q), BF16)
WIDE32 = jax.ShapeDtypeStruct((ROWS, Q), F32)
SUMS = jax.ShapeDtypeStruct((8, 128), F32)
TURN = [pltpu.VMEM((256, 128), F32), pltpu.VMEM((128, 128), F32)]
MIX = [pltpu.VMEM((256, 256), F32), pltpu.VMEM((32, 256), F32)]
WEIGHTS = jax.ShapeDtypeStruct((2, C, 24, 128), F32)


def call(kernel, shapes, scratch, *operands, specs=None, cost=None, params=PARAMS):
    many = isinstance(shapes, (list, tuple))
    return pl.pallas_call(
        kernel,
        out_shape=shapes,
        in_specs=specs or [VM] * len(operands),
        out_specs=[VM] * len(shapes) if many else VM,
        scratch_shapes=scratch,
        compiler_params=params,
        cost_estimate=cost,
    )(*operands)


def swap_rows(value):
    return lax.all_to_all(value, ("z", "core"), split_axis=0, concat_axis=0, tiled=True)


def swap_cols(value):
    return lax.all_to_all(value, ("h", "ylo", "x"), split_axis=0, concat_axis=0, tiled=True)


def per_device(hidden_in, spectral, pointwise, biases, upstream):
    ahead, behind = (jnp.asarray(t) for t in depth_tables())
    root = 1.0 / math.sqrt(NX)
    to_modes = [row_table(-1.0, f) for f in (root, 0.25)]
    to_rows = [row_table(1.0, f) for f in (0.25, root)]
    field = jnp.transpose(hidden_in[0], (1, 0, 2)).reshape(ROWS, Q)
    above = jnp.transpose(upstream[0], (1, 0, 2)).reshape(ROWS, Q)
    weights = jnp.transpose(spectral, (0, 1, 2, 4, 5, 6, 3)).reshape(2, 2, C, 128, C)

    def x_step(kernel, table, blocks, *after):
        return call(
            functools.partial(kernel, table), BLOCKS, [], blocks, *after,
            specs=[VM] + [FAR] * len(after),
        )

    def mix_step(kernel, layer, blocks, *more):
        return call(kernel, [BLOCKS, MODES], MIX, blocks, turned[layer], twiddle, *more)

    def weight_grad(layer, spectrum, dmixed, held=None):
        out_spec = pl.BlockSpec((1, 2, C, 128, C), lambda i: (layer, 0, 0, 0, 0))
        mode_spec = pl.BlockSpec((32, 256), lambda i: (0, 0))
        operands = (spectrum, dmixed) + (() if held is None else (held,))
        return pl.pallas_call(
            weight_grad_first if held is None else weight_grad_second,
            grid=(1,),
            out_shape=jax.ShapeDtypeStruct((2, 2, C, 128, C), F32),
            in_specs=[mode_spec, mode_spec] + [pl.BlockSpec(memory_space=pl.ANY)] * (held is not None),
            out_specs=out_spec,
            input_output_aliases={} if held is None else {2: 0},
            compiler_params=PARAMS,
            cost_estimate=pl.CostEstimate(flops=2000000, bytes_accessed=3000000, transcendentals=0),
        )(*operands)

    def round_trip(blocks, step, side, *after):
        blocks = swap_rows(blocks)
        blocks = swap_cols(x_step(x_ahead_kernel, to_modes[side], blocks, *after))
        blocks, modes = step(blocks)
        blocks = swap_cols(blocks)
        blocks = swap_rows(x_step(x_behind_kernel, to_rows[side], blocks))
        return blocks, modes

    loads = [pltpu.VMEM((ROWS, Q), BF16), pltpu.VMEM((256, Q), BF16), pltpu.SemaphoreType.DMA((2,))]
    blocks, token = call(
        start_kernel, [BLOCKS, SUMS], TURN + loads, field, ahead, specs=[FAR, FAR], params=None
    )
    squares = jax.ShapeDtypeStruct((2, ROWS, ROWS), BF16)
    first, second, twiddle, local_back, local_ahead, offsets = call(
        prepare_kernel,
        [
            WEIGHTS, WEIGHTS, jax.ShapeDtypeStruct((128, 128), F32),
            squares, squares, jax.ShapeDtypeStruct((ROWS, 2), F32),
        ],
        [
            pltpu.VMEM((2, 2, C, 128, C), F32),
            pltpu.VMEM((4, 128, 128), F32),
            pltpu.SemaphoreType.DMA((2,)),
        ],
        token, weights, jnp.asarray(column_table()), pointwise, biases,
        specs=[VM, FAR, VM, VM, VM],
        cost=pl.CostEstimate(flops=60000000, bytes_accessed=8000000, transcendentals=0),
    )
    turned = (first, second)
    blocks, spectrum_0 = round_trip(blocks, lambda b: mix_step(mix_kernel, 0, b), 0, twiddle)
    blocks, field_1, factor_0 = call(
        layer_kernel, [BLOCKS, WIDE16, WIDE32], TURN,
        blocks, field, local_ahead, offsets, ahead, behind,
    )
    blocks, spectrum_1 = round_trip(blocks, lambda b: mix_step(mix_kernel, 1, b), 0)
    final = call(
        final_kernel, WIDE32, TURN,
        blocks, field_1, local_ahead, offsets, behind,
        cost=pl.CostEstimate(flops=200000000, bytes_accessed=2000000, transcendentals=0),
    )
    blocks, slopes_1 = call(
        top_kernel, [BLOCKS, WIDE16],
        TURN + [pltpu.VMEM((ROWS, Q), BF16), pltpu.SemaphoreType.DMA],
        blocks, field_1, local_ahead, offsets, above, behind,
        specs=[VM] * 4 + [FAR, VM], params=None,
    )
    blocks, dmixed_1 = round_trip(blocks, lambda b: mix_step(mix_grad_kernel, 1, b, field_1, slopes_1), 1)
    grads = weight_grad(1, spectrum_1, dmixed_1)
    blocks, slopes_0, later = call(
        back_kernel, [BLOCKS, WIDE16, SUMS], TURN,
        blocks, slopes_1, local_back, factor_0, ahead, behind,
    )
    blocks, dmixed_0 = round_trip(blocks, lambda b: mix_step(mix_grad_kernel, 0, b, field, slopes_0), 1)
    grads = weight_grad(0, spectrum_0, dmixed_0, grads)
    grad_hidden, mixing, offset_grads = call(
        end_kernel,
        [WIDE32, jax.ShapeDtypeStruct((C, 2, C), F32), jax.ShapeDtypeStruct((2, C), F32)],
        TURN,
        blocks, slopes_0, local_back, ahead, later,
    )

    def cells(value):
        return jnp.transpose(value.reshape(C, 8, Q), (1, 0, 2))[None]

    grad_spectral = jnp.transpose(grads.reshape(2, 2, C, 2, 16, 4, C), (0, 1, 2, 6, 3, 4, 5))
    return (
        cells(final),
        cells(grad_hidden),
        grad_spectral,
        jnp.transpose(mixing, (1, 0, 2)),
        offset_grads,
    )


def solution(mesh):
    names = ("z", "h", "core", "ylo", "x")
    fine = Mesh(mesh.devices.reshape(8, 2, 2, 2, 4), names)
    rows, cols = ("z", "h", "core"), ("ylo", "x")
    grid = P(rows, cols, None, None)
    modes = P(None, None, None, None, cols, None, rows)
    return jax.shard_map(
        per_device,
        mesh=fine,
        in_specs=(grid, modes, P(), P(), grid),
        out_specs=(grid, grid, modes, P(), P()),
        check_vma=False,
    )
```

```python
import functools
import math

import jax
import jax.numpy as jnp
import ml_dtypes
import numpy as np
from jax import lax
from jax.experimental import pallas as pl
from jax.experimental.pallas import tpu as pltpu
from jax.sharding import Mesh, PartitionSpec as P

KX = 16
KY = 16
KZ = 16
KT = 8
NZ = 64
NT = 16
NX = 32
NY = 64
C = 20
Q = NZ * NT
ROWS = 160
PADS = (2, 3, 6, 7)

F32 = jnp.float32
BF16 = jnp.bfloat16
HIGH = lax.Precision.HIGHEST
PARAMS = pltpu.CompilerParams(vmem_limit_bytes=32 * 1024 * 1024)


def depth_tables():
    rows = np.arange(256)
    g, m4, r, mh = rows % 16, rows // 16 % 4, rows // 64 % 2, rows // 128
    m = 16 * (g // 2) + 8 * mh + 4 * (g % 2) + m4
    freq_z, freq_t = m // KT - KZ // 2, m % KT
    cells = np.arange(Q)
    phase = (freq_z[:, None] * (cells // NT) * NT + freq_t[:, None] * (cells % NT) * NZ) % Q
    angle = phase * (2.0 * np.pi / Q)
    parts = np.where(r[:, None] == 0, np.cos(angle), -np.sin(angle))
    weight = np.where(freq_t == 0, 1.0, 2.0)[:, None]
    ahead = (parts / math.sqrt(Q)).astype(np.float32).astype(ml_dtypes.bfloat16)
    behind = (parts * weight / math.sqrt(2 * KZ * KT)).astype(np.float32)
    return ahead, behind.astype(ml_dtypes.bfloat16)


def row_table(sign, factor):
    half, jj, kx = np.meshgrid(np.arange(2), np.arange(4), np.arange(KX), indexing="ij")
    x = 4 * (jj // 2) + 2 * half + jj % 2
    angle = (x * (kx - KX // 2) % NX) * (2.0 * np.pi / NX)
    pairs = np.stack([np.cos(angle), sign * np.sin(angle)], axis=-1) * factor
    pairs = pairs.astype(np.float32).astype(ml_dtypes.bfloat16).astype(np.float32)
    return pairs


def column_table():
    y = np.arange(128)[None, :] % 8
    ky = np.arange(64)[:, None] // 4
    angle = (y * (ky - KY // 2) % NY) * (2.0 * np.pi / NY)
    both = np.concatenate([np.cos(angle), np.sin(angle)], axis=0) / math.sqrt(NY)
    return both.astype(np.float32)


def iota(shape, axis):
    return lax.broadcasted_iota(jnp.int32, shape, axis)


def halves(value):
    high = value.astype(BF16)
    return high, (value - high.astype(F32)).astype(BF16)


def dot2(value, table):
    high, low = halves(value)
    return jnp.dot(high, table, preferred_element_type=F32) + jnp.dot(
        low, table, preferred_element_type=F32
    )


def dot_rows(left, right):
    return lax.dot_general(left, right, (((1,), (1,)), ((), ())), preferred_element_type=F32)


def erf(value):
    value = jnp.clip(value, -3.832506856900711, 3.832506856900711)
    square = value * value
    top = jnp.full_like(value, 0.00022905065861350646)
    for term in (0.0034082910107109506, 0.050955695062380861, 0.18520832239976145, 1.128379143519084):
        top = top * square + term
    base = jnp.full_like(value, -1.1791602954361697e-7)
    for term in (
        0.000023547966471313185,
        0.0010179625278914885,
        0.014070470171167667,
        0.11098505178285362,
        0.49746925110067538,
        1.0,
    ):
        base = base * square + term
    return value * top / base


def gelu_parts(preact):
    ramp = 0.5 * (1.0 + erf(preact * (1.0 / math.sqrt(2.0))))
    bell = jnp.exp(-0.5 * preact * preact) * (1.0 / math.sqrt(2.0 * math.pi))
    return preact * ramp, ramp + preact * bell


def compact(ref):
    return len(ref.shape) == 4


def read_main(ref, g, k):
    if compact(ref):
        return jnp.concatenate([ref[g, 2 * k], ref[g, 2 * k + 1]], axis=0)
    return ref[g, 8 * k : 8 * k + 8, :]


def read_rest(ref, g):
    if compact(ref):
        both = jnp.concatenate([ref[g, 4], ref[g, 4]], axis=0)
        return jnp.where(iota((8, 128), 0) < 4, both, pltpu.roll(both, 2, 0))
    return ref[g, 16:24, :]


def write_main(ref, g, k, value):
    if compact(ref):
        ref[g, 2 * k] = value[0:4, :]
        ref[g, 2 * k + 1] = value[4:8, :]
    else:
        ref[g, 8 * k : 8 * k + 8, :] = value


def write_rest(ref, g, value):
    if compact(ref):
        ref[g, 4] = jnp.where(iota((8, 128), 0) < 2, value, pltpu.roll(value, 6, 0))[0:4, :]
    else:
        ref[g, 16:24, :] = value


def pack(spectra, out_ref, main, rest):
    main[...] = jnp.transpose(spectra[:128, :])
    for g in range(16):
        for k in range(2):
            write_main(out_ref, g, k, main[pl.ds(128 * k + g, 8, stride=16), :])
    left, right = spectra[128:, :128], spectra[128:, 128:]
    lane = iota((32, 128), 1) % 64 // 16
    pieces = []
    for m in range(4):
        first = pltpu.roll(left, (128 - 16 * m) % 128, 1)
        second = pltpu.roll(right, (144 - 16 * m) % 128, 1)
        pieces.append(jnp.where(lane == 0, first, jnp.where(lane == 1, second, 0.0)))
    rest[...] = jnp.transpose(jnp.concatenate(pieces, axis=0))
    for g in range(16):
        write_rest(out_ref, g, rest[pl.ds(g, 8, stride=16), :])


def unpack(blocks, main, rest):
    for g in range(16):
        for k in range(2):
            main[pl.ds(128 * k + g, 8, stride=16), :] = read_main(blocks, g, k)
        rest[pl.ds(g, 8, stride=16), :] = read_rest(blocks, g)
    turned = jnp.transpose(rest[...])
    lane = iota((32, 128), 1) % 64 // 16
    left = right = jnp.zeros((32, 128), F32)
    for m in range(4):
        piece = turned[32 * m : 32 * m + 32, :]
        left = jnp.where(lane == m, pltpu.roll(piece, 16 * m, 1), left)
        right = jnp.where(lane == m, pltpu.roll(piece, (112 + 16 * m) % 128, 1), right)
    return jnp.concatenate(
        [jnp.transpose(main[...]), jnp.concatenate([left, right], axis=1)], axis=0
    )


def rotate(value, sign):
    return sign * pltpu.roll(value, 4, 0)


def turn_sign():
    return jnp.where(iota((8, 128), 0) < 4, -1.0, 1.0).astype(F32)


def pad_rows():
    return iota((8, 128), 0) % 4 >= 2


def start_kernel(field, ahead, out_ref, token, main, rest, near, table, sems):
    copies = []
    for part in range(2):
        cols = pl.ds(512 * part, 512)
        copies.append(
            (
                pltpu.make_async_copy(field.at[:, cols], near.at[part], sems.at[2 * part]),
                pltpu.make_async_copy(ahead.at[:, cols], table.at[part], sems.at[2 * part + 1]),
            )
        )
        for copy in copies[-1]:
            copy.start()
    token[...] = jnp.zeros_like(token)
    spectra = None
    for part in range(2):
        for copy in copies[part]:
            copy.wait()
        term = dot_rows(near[part], table[part])
        spectra = term if spectra is None else spectra + term
    pack(spectra, out_ref, main, rest)


def prepare_kernel(
    token, weights, table, above, pointwise, biases,
    first, second, twiddle, near_above, local_back, local_ahead, offsets, near, padded_rows, sems,
):
    copies = [
        pltpu.make_async_copy(weights.at[layer], near.at[layer], sems.at[layer]) for layer in range(2)
    ]
    for copy in copies:
        copy.start()
    copy = pltpu.make_async_copy(above, near_above, sems.at[2])
    copy.start()
    twiddle[...] = table[...] + 0.0 * token[0:1, :]
    padded_rows[...] = jnp.zeros_like(padded_rows)
    owner = (iota((ROWS, C), 0) // 8 == iota((ROWS, C), 1)).astype(F32)
    same = iota((ROWS, ROWS), 0) % 8 == iota((ROWS, ROWS), 1) % 8
    for layer in range(2):
        mixing = pointwise[layer].astype(F32)
        rows = jnp.dot(owner, mixing, precision=HIGH, preferred_element_type=F32)
        wide = lax.dot_general(
            rows, owner, (((1,), (1,)), ((), ())), precision=HIGH, preferred_element_type=F32
        )
        wide = jnp.where(same, wide, 0.0)
        local_back[layer] = wide.astype(BF16)
        padded = jnp.zeros((256, 256), F32)
        padded = jnp.concatenate(
            [
                jnp.concatenate([wide, jnp.zeros((ROWS, 96), F32)], axis=1),
                jnp.zeros((96, 256), F32),
            ],
            axis=0,
        )
        local_ahead[layer] = jnp.transpose(padded)[:ROWS, :ROWS].astype(BF16)
    offsets[...] = lax.dot_general(
        owner, biases[...], (((1,), (1,)), ((), ())), precision=HIGH, preferred_element_type=F32
    )
    for layer, out_ref in ((0, first), (1, second)):
        copies[layer].wait()
        for part in range(2):
            for c in range(C):
                slot = c % 4
                padded_rows[slot, :, 0:C] = near[layer, part, c]
                out_ref[part, c] = jnp.transpose(padded_rows[slot])[:24, :]
    copy.wait()


def entry(table, half, jj, kx):
    first, second = (jnp.where(half == 0, float(a), float(b)) for a, b in zip(*table[:, jj, kx]))
    return first, second


def x_ahead_kernel(table, blocks, *others):
    out_ref = others[-1]
    half = lax.axis_index("h")
    sign = turn_sign()
    place = iota((8, 128), 0) % 4
    for part in range(3):
        groups = [[None] * 4 for _ in range(4)]
        turned = [[None] * 4 for _ in range(4)]
        for jj in range(4):
            x0, x1, x2, x3 = (
                read_main(blocks, jj + 4 * i, part) if part < 2 else read_rest(blocks, jj + 4 * i)
                for i in range(4)
            )
            even, odd = x0 + x2, x0 - x2
            even_other, odd_other = x1 + x3, rotate(x1 - x3, sign)
            found = (even + even_other, odd - odd_other, even - even_other, odd + odd_other)
            for k in range(4):
                groups[k][jj] = found[k]
                turned[k][jj] = rotate(found[k], sign)
        modes = []
        for kx in range(KX):
            total = None
            for jj in range(4):
                real, imag = entry(table, half, jj, kx)
                term = real * groups[kx % 4][jj] + imag * turned[kx % 4][jj]
                total = term if total is None else total + term
            if part < 2:
                write_main(out_ref, part * 8 + kx // 2, kx % 2, total)
            else:
                modes.append(total)
        if part == 2:
            for k in range(8):
                first, second = modes[2 * k], modes[2 * k + 1]
                near = jnp.where(place == 0, first, pltpu.roll(second, 1, 0))
                write_rest(out_ref, k, near)
                near = jnp.where(place == 0, pltpu.roll(first, 7, 0), second)
                write_rest(out_ref, 8 + k, near)


def x_behind_kernel(table, blocks, out_ref):
    half = lax.axis_index("h")
    sign = turn_sign()
    place = iota((8, 128), 0) % 4
    sums = None if compact(blocks) else block_sums(blocks)
    for part in range(3):
        totals = [[None] * 4 for _ in range(4)]
        for kx in range(KX):
            if part < 2:
                mode = read_main(blocks, part * 8 + kx // 2, kx % 2)
            else:
                first, second = read_rest(blocks, kx // 2), read_rest(blocks, 8 + kx // 2)
                if kx % 2 == 0:
                    second = pltpu.roll(second, 1, 0)
                else:
                    first = pltpu.roll(first, 7, 0)
                mode = jnp.where(place == 0, first, jnp.where(place == 1, second, 0.0))
            turned = rotate(mode, sign)
            for jj in range(4):
                real, imag = entry(table, half, jj, kx)
                term = real * mode + imag * turned
                old = totals[kx % 4][jj]
                totals[kx % 4][jj] = term if old is None else old + term
        for jj in range(4):
            h0, h1, h2, h3 = (totals[k][jj] for k in range(4))
            even, odd = h0 + h2, h0 - h2
            even_other, odd_other = h1 + h3, rotate(h1 - h3, sign)
            found = (even + even_other, odd + odd_other, even - even_other, odd - odd_other)
            for i in range(4):
                if part < 2:
                    write_main(out_ref, jj + 4 * i, part, found[i])
                elif sums is None:
                    write_rest(out_ref, jj + 4 * i, found[i])
                else:
                    write_rest(out_ref, jj + 4 * i, jnp.where(place >= 2, sums, found[i]))


def channel_rows():
    lane = iota((32, 256), 1)
    owner = jnp.where(lane < 128, lane // 8, 16 + lane // 8 % 4)
    return (owner == iota((32, 256), 0)).astype(F32).astype(BF16)


def times(value, factor):
    return (
        value[0] * factor[0] - value[1] * factor[1],
        value[0] * factor[1] + value[1] * factor[0],
    )


def plus(one, two):
    return one[0] + two[0], one[1] + two[1]


def minus(one, two):
    return one[0] - two[0], one[1] - two[1]


def fourth(values, sign):
    even, odd = plus(values[0], values[2]), minus(values[0], values[2])
    even_other, odd_other = plus(values[1], values[3]), minus(values[1], values[3])
    turned = (-sign * odd_other[1], sign * odd_other[0])
    return plus(even, even_other), plus(odd, turned), minus(even, even_other), minus(odd, turned)


def odd_turn(y, sign):
    low = iota((8, 128), 0) < 4
    angle = math.pi * y / 4
    return jnp.where(low, 1.0, math.cos(angle)), jnp.where(low, 0.0, sign * math.sin(angle))


def y_ahead(blocks, twiddle, wide):
    low = iota((8, 128), 0) < 4
    keep = iota((8, 128), 0) % 4 == iota((8, 128), 1) // 32
    units = [[] for _ in range(4)]
    for y in range(8):
        other = read_rest(blocks, y) + read_rest(blocks, 8 + y)
        for k in range(2):
            value = read_main(blocks, y, k) + read_main(blocks, 8 + y, k)
            swapped = pltpu.roll(value, 4, 0)
            units[k].append((jnp.where(low, value, swapped), jnp.where(low, swapped, value)))
            units[2 + k].append(
                (
                    jnp.broadcast_to(other[k : k + 1, :], (8, 128)),
                    jnp.broadcast_to(other[4 + k : 5 + k, :], (8, 128)),
                )
            )
    turns = [odd_turn(y, -1.0) for y in range(8)]
    for unit in range(4):
        values = [units[unit][0]] + [times(units[unit][y], turns[y]) for y in range(1, 8)]
        groups = fourth([plus(values[n], values[n + 4]) for n in range(4)], -1.0)
        lanes = slice(0, 128) if unit < 2 else slice(128, 256)
        for pair in range(8):
            at = 8 * pair
            factor = (twiddle[at : at + 8, :], -twiddle[64 + at : 72 + at, :])
            real, imag = times(groups[pair % 4], factor)
            if unit >= 2:
                real, imag = jnp.where(keep, real, 0.0), jnp.where(keep, imag, 0.0)
            at += 64 * (unit % 2)
            wide[at : at + 8, lanes] = real
            wide[128 + at : 136 + at, lanes] = imag
    high, low_part = halves(wide[...])
    table = channel_rows()
    return dot_rows(table, high) + dot_rows(table, low_part)


def y_behind(modes, twiddle, scale, pads, wide, out_ref):
    wide[...] = dot2(jnp.transpose(modes), channel_rows())
    row = iota((8, 128), 0)
    low = row < 4
    keep = row % 4 == iota((8, 128), 1) // 32
    turns = [odd_turn(y, 1.0) for y in range(8)]
    rests = [pads] * 8
    for unit in range(4):
        k = unit % 2
        lanes = slice(0, 128) if unit < 2 else slice(128, 256)
        values = []
        for pair in range(8):
            at = 8 * pair
            factor = (twiddle[at : at + 8, :] * scale, twiddle[64 + at : 72 + at, :] * scale)
            at += 64 * k
            values.append(times((wide[at : at + 8, lanes], wide[128 + at : 136 + at, lanes]), factor))
        groups = fourth([plus(values[n], values[n + 4]) for n in range(4)], 1.0)
        for y in range(8):
            real, imag = groups[y % 4] if y == 0 else times(groups[y % 4], turns[y])
            if unit < 2:
                real = real + pltpu.roll(real, 4, 0)
                imag = imag + pltpu.roll(imag, 4, 0)
                value = jnp.where(low, real, imag)
                write_main(out_ref, y, k, value)
                write_main(out_ref, 8 + y, k, value)
            else:
                for r, value in ((0, real), (1, imag)):
                    value = jnp.where(keep, value, 0.0)
                    for step in (4, 2, 1):
                        value = value + pltpu.roll(value, step, 0)
                    rests[y] = jnp.where(row == 4 * r + k, value, rests[y])
    for y in range(8):
        write_rest(out_ref, y, rests[y])
        write_rest(out_ref, 8 + y, rests[y])


def mix_kernel(blocks, weights, twiddle, out_ref, spectrum, wide, mixed):
    spectrum[...] = y_ahead(blocks, twiddle, wide)
    out_real = out_imag = jnp.zeros((24, 128), F32)
    for c in range(C):
        first = jnp.broadcast_to(spectrum[c : c + 1, 0:128], (24, 128))
        second = jnp.broadcast_to(spectrum[c : c + 1, 128:256], (24, 128))
        w_real, w_imag = weights[0, c], weights[1, c]
        out_real += first * w_real - second * w_imag
        out_imag += first * w_imag + second * w_real
    mixed[0:24, 0:128] = out_real
    mixed[0:24, 128:256] = out_imag
    mixed[24:32, :] = jnp.zeros((8, 256), F32)
    y_behind(mixed[...], twiddle, 2.0, jnp.zeros((8, 128), F32), wide, out_ref)


def mix_grad_kernel(blocks, weights, twiddle, field, slopes, out_ref, dmixed, wide, mixed):
    sums = cell_sums(field, slopes)
    dmixed[...] = 2.0 * y_ahead(blocks, twiddle, wide)
    real, imag = dmixed[0:24, 0:128], dmixed[0:24, 128:256]
    for c in range(C):
        w_real, w_imag = weights[0, c], weights[1, c]
        mixed[c : c + 1, 0:128] = jnp.sum(w_real * real + w_imag * imag, axis=0, keepdims=True)
        mixed[c : c + 1, 128:256] = jnp.sum(w_real * imag - w_imag * real, axis=0, keepdims=True)
    mixed[C:32, :] = jnp.zeros((32 - C, 256), F32)
    y_behind(mixed[...], twiddle, 1.0, sums, wide, out_ref)


def weight_grad_body(spectrum, dmixed, out_ref, scale):
    turned, other = jnp.transpose(spectrum[...]), jnp.transpose(dmixed[...]) * scale
    for at in range(0, 128, 32):
        rows = slice(at, at + 32)
        under = slice(128 + at, 160 + at)
        real, imag = other[rows, 0:C], other[under, 0:C]
        s_real, s_imag = turned[rows, :], turned[under, :]
        for c in range(C):
            first = jnp.broadcast_to(s_real[:, c : c + 1], (32, C))
            second = jnp.broadcast_to(s_imag[:, c : c + 1], (32, C))
            out_ref[0, 0, c, rows, :] = first * real - second * imag
            out_ref[0, 1, c, rows, :] = first * imag + second * real


MODE_SCALE = math.sqrt(2.0 * KX * KY * KZ * KT / (NX * NY * NZ * NT))
CELL_SCALE = 1.0 / math.sqrt(NX * NY * NZ * NT)


def weight_grad_first(spectrum, dmixed, out_ref):
    weight_grad_body(spectrum, dmixed, out_ref, MODE_SCALE)


def weight_grad_second(spectrum, dmixed, held, out_ref):
    weight_grad_body(spectrum, dmixed, out_ref, MODE_SCALE)


def layer_kernel(blocks, field, local, offset, ahead, behind, out_ref, new_field, slope, main, rest):
    layer = 0
    high, low = halves(unpack(blocks, main, rest))
    spectra = None
    for at in range(0, Q, 256):
        cols = slice(at, at + 256)
        table = behind[:, cols]
        preact = jnp.dot(high, table, preferred_element_type=F32)
        preact += jnp.dot(low, table, preferred_element_type=F32)
        preact += jnp.dot(local[layer], field[:, cols], preferred_element_type=F32)
        preact += offset[:, layer : layer + 1]
        value, factor = gelu_parts(preact)
        value = value.astype(BF16)
        new_field[:, cols] = value
        slope[:, cols] = factor
        term = dot_rows(value, ahead[:, cols])
        spectra = term if spectra is None else spectra + term
    pack(spectra, out_ref, main, rest)


def top_kernel(blocks, field, local, offset, upstream, behind, out_ref, slopes, main, rest):
    layer = 1
    high, low = halves(unpack(blocks, main, rest))
    spectra = None
    for at in range(0, Q, 256):
        cols = slice(at, at + 256)
        table = behind[:, cols]
        preact = jnp.dot(high, table, preferred_element_type=F32)
        preact += jnp.dot(low, table, preferred_element_type=F32)
        preact += jnp.dot(local[layer], field[:, cols], preferred_element_type=F32)
        preact += offset[:, layer : layer + 1]
        factor = gelu_parts(preact)[1]
        slope = (upstream[:, cols].astype(F32) * factor).astype(BF16)
        slopes[:, cols] = slope
        term = dot_rows(slope, table)
        spectra = term if spectra is None else spectra + term
    pack(spectra, out_ref, main, rest)


def final_kernel(blocks, field, local, offset, behind, final, main, rest):
    layer = 1
    high, low = halves(unpack(blocks, main, rest))
    for at in range(0, Q, 256):
        cols = slice(at, at + 256)
        table = behind[:, cols]
        preact = jnp.dot(high, table, preferred_element_type=F32)
        preact += jnp.dot(low, table, preferred_element_type=F32)
        preact += jnp.dot(local[layer], field[:, cols], preferred_element_type=F32)
        preact += offset[:, layer : layer + 1]
        final[:, cols] = gelu_parts(preact)[0]


def block_sums(blocks):
    total = blocks[0, 16:24, :]
    for g in range(1, 16):
        total = total + blocks[g, 16:24, :]
    return jnp.where(pad_rows(), total, 0.0)


def back_kernel(
    blocks, slopes, local, factor, ahead, behind, out_ref, new_slopes, sums, main, rest
):
    layer = 1
    sums[...] = block_sums(blocks)
    high, low = halves(unpack(blocks, main, rest))
    spectra = None
    for at in range(0, Q, 256):
        cols = slice(at, at + 256)
        table = ahead[:, cols]
        grad = jnp.dot(high, table, preferred_element_type=F32)
        grad += jnp.dot(low, table, preferred_element_type=F32)
        grad += jnp.dot(local[layer], slopes[:, cols], preferred_element_type=F32)
        grad = grad.astype(BF16).astype(F32)
        slope = (grad * factor[:, cols]).astype(BF16)
        new_slopes[:, cols] = slope
        term = dot_rows(slope, behind[:, cols])
        spectra = term if spectra is None else spectra + term
    pack(spectra, out_ref, main, rest)


def end_kernel(blocks, slopes, local, ahead, later, grad_ref, mixing, offsets, main, rest):
    for at_layer, total in ((0, block_sums(blocks)), (1, later[...])):
        row = iota((24, 8), 0) // 6
        col = iota((24, 8), 1)
        pick = sum(((row == i) & (col == PADS[i])).astype(F32) for i in range(4))
        wide = jnp.dot(pick, total, precision=HIGH, preferred_element_type=F32)
        wide = jnp.where(iota((24, 128), 1) // C == iota((24, 128), 0) % 6, wide, 0.0)
        place = (iota((128, 128), 0) % C == iota((128, 128), 1)).astype(F32)
        found = jnp.dot(wide, place, precision=HIGH, preferred_element_type=F32) * CELL_SCALE
        for c in range(C):
            mixing[c, at_layer : at_layer + 1, :] = found[c : c + 1, 0:C]
        offsets[at_layer : at_layer + 1, :] = found[C : C + 1, 0:C]
    layer = 0
    high, low = halves(unpack(blocks, main, rest))
    for at in range(0, Q, 256):
        cols = slice(at, at + 256)
        table = ahead[:, cols]
        grad = jnp.dot(high, table, preferred_element_type=F32)
        grad += jnp.dot(low, table, preferred_element_type=F32)
        grad += jnp.dot(local[layer], slopes[:, cols], preferred_element_type=F32)
        grad_ref[:, cols] = grad


def cell_sums(field, slopes):
    slope = slopes[...]
    pairs = jnp.concatenate(
        [dot_rows(field[...], slope), dot_rows(jnp.ones((8, Q), BF16), slope)], axis=0
    )
    pairs = jnp.where(iota((168, ROWS), 0) % 8 == iota((168, ROWS), 1) % 8, pairs, 0.0)
    lane = iota((ROWS, 128), 1)
    place = ((lane < 6 * C) & (lane % C == iota((ROWS, 128), 0) // 8)).astype(F32)
    wide = dot2(pairs, place.astype(BF16))
    wide = jnp.where(iota((168, 128), 1) // C == iota((168, 128), 0) // 8 % 6, wide, 0.0)
    row = iota((8, 168), 0)
    owner = iota((8, 168), 1) // 48
    pick = sum(((owner == i) & (row == PADS[i])).astype(F32) for i in range(4))
    pick, (high, low) = pick.astype(BF16), halves(wide)
    return jnp.dot(pick, high, preferred_element_type=F32) + jnp.dot(
        pick, low, preferred_element_type=F32
    )


VM = pl.BlockSpec(memory_space=pltpu.VMEM)
FAR = pl.BlockSpec(memory_space=pltpu.HBM)
BLOCKS = jax.ShapeDtypeStruct((16, 24, 128), F32)
SLABS = jax.ShapeDtypeStruct((16, 5, 4, 128), F32)
MODES = jax.ShapeDtypeStruct((32, 256), F32)
WIDE16 = jax.ShapeDtypeStruct((ROWS, Q), BF16)
WIDE32 = jax.ShapeDtypeStruct((ROWS, Q), F32)
SUMS = jax.ShapeDtypeStruct((8, 128), F32)
TURN = [pltpu.VMEM((256, 128), F32), pltpu.VMEM((128, 128), F32)]
MIX = [pltpu.VMEM((256, 256), F32), pltpu.VMEM((32, 256), F32)]
WEIGHTS = jax.ShapeDtypeStruct((2, C, 24, 128), F32)


def call(kernel, shapes, scratch, *operands, specs=None, cost=None, params=PARAMS):
    many = isinstance(shapes, (list, tuple))
    return pl.pallas_call(
        kernel,
        out_shape=shapes,
        in_specs=specs or [VM] * len(operands),
        out_specs=[VM] * len(shapes) if many else VM,
        scratch_shapes=scratch,
        compiler_params=params,
        cost_estimate=cost,
    )(*operands)


def swap_rows(value):
    return lax.all_to_all(value, ("z", "core"), split_axis=0, concat_axis=0, tiled=True)


def swap_cols(value):
    return lax.all_to_all(value, ("h", "ylo", "x"), split_axis=0, concat_axis=0, tiled=True)


def per_device(hidden_in, spectral, pointwise, biases, upstream):
    ahead, behind = (jnp.asarray(t) for t in depth_tables())
    root = 1.0 / math.sqrt(NX)
    to_modes = [row_table(-1.0, f) for f in (root, 0.25)]
    to_rows = [row_table(1.0, f) for f in (0.25, root)]
    field = jnp.transpose(hidden_in[0], (1, 0, 2)).reshape(ROWS, Q)
    above = jnp.transpose(upstream[0], (1, 0, 2)).reshape(ROWS, Q)
    weights = jnp.transpose(spectral, (0, 1, 2, 4, 5, 6, 3)).reshape(2, 2, C, 128, C)

    def x_step(kernel, table, shape, blocks, *after):
        return call(
            functools.partial(kernel, table), shape, [], blocks, *after,
            specs=[VM] + [FAR] * len(after),
        )

    def mix_step(kernel, shape, layer, blocks, *more):
        return call(kernel, [shape, MODES], MIX, blocks, turned[layer], twiddle, *more)

    def weight_grad(layer, spectrum, dmixed, held=None):
        out_spec = pl.BlockSpec((1, 2, C, 128, C), lambda i: (layer, 0, 0, 0, 0))
        mode_spec = pl.BlockSpec((32, 256), lambda i: (0, 0))
        operands = (spectrum, dmixed) + (() if held is None else (held,))
        return pl.pallas_call(
            weight_grad_first if held is None else weight_grad_second,
            grid=(1,),
            out_shape=jax.ShapeDtypeStruct((2, 2, C, 128, C), F32),
            in_specs=[mode_spec, mode_spec] + [pl.BlockSpec(memory_space=pl.ANY)] * (held is not None),
            out_specs=out_spec,
            input_output_aliases={} if held is None else {2: 0},
            compiler_params=PARAMS,
            cost_estimate=pl.CostEstimate(flops=2000000, bytes_accessed=3000000, transcendentals=0),
        )(*operands)

    def round_trip(blocks, step, side, *after):
        blocks = swap_rows(blocks)
        blocks = swap_cols(x_step(x_ahead_kernel, to_modes[side], SLABS, blocks, *after))
        blocks, modes = step(blocks)
        blocks = swap_cols(blocks)
        blocks = swap_rows(x_step(x_behind_kernel, to_rows[side], BLOCKS if side else SLABS, blocks))
        return blocks, modes

    loads = [
        pltpu.VMEM((2, ROWS, 512), BF16),
        pltpu.VMEM((2, 256, 512), BF16),
        pltpu.SemaphoreType.DMA((4,)),
    ]
    blocks, token = call(
        start_kernel, [SLABS, SUMS], TURN + loads, field, ahead, specs=[FAR, FAR], params=None
    )
    squares = jax.ShapeDtypeStruct((2, ROWS, ROWS), BF16)
    first, second, twiddle, near_above, local_back, local_ahead, offsets = call(
        prepare_kernel,
        [
            WEIGHTS, WEIGHTS, jax.ShapeDtypeStruct((128, 128), F32), WIDE16,
            squares, squares, jax.ShapeDtypeStruct((ROWS, 2), F32),
        ],
        [
            pltpu.VMEM((2, 2, C, 128, C), F32),
            pltpu.VMEM((4, 128, 128), F32),
            pltpu.SemaphoreType.DMA((3,)),
        ],
        token, weights, jnp.asarray(column_table()), above, pointwise, biases,
        specs=[VM, FAR, VM, FAR, VM, VM],
        cost=pl.CostEstimate(flops=60000000, bytes_accessed=8000000, transcendentals=0),
    )
    turned = (first, second)
    blocks, spectrum_0 = round_trip(blocks, lambda b: mix_step(mix_kernel, SLABS, 0, b), 0, twiddle)
    blocks, field_1, factor_0 = call(
        layer_kernel, [SLABS, WIDE16, WIDE32], TURN,
        blocks, field, local_ahead, offsets, ahead, behind,
    )
    blocks, spectrum_1 = round_trip(blocks, lambda b: mix_step(mix_kernel, SLABS, 1, b), 0)
    final = call(
        final_kernel, WIDE32, TURN,
        blocks, field_1, local_ahead, offsets, behind,
        cost=pl.CostEstimate(flops=200000000, bytes_accessed=2000000, transcendentals=0),
    )
    blocks, slopes_1 = call(
        top_kernel, [SLABS, WIDE16],
        TURN,
        blocks, field_1, local_ahead, offsets, near_above, behind,
    )
    blocks, dmixed_1 = round_trip(blocks, lambda b: mix_step(mix_grad_kernel, BLOCKS, 1, b, field_1, slopes_1), 1)
    grads = weight_grad(1, spectrum_1, dmixed_1)
    blocks, slopes_0, later = call(
        back_kernel, [SLABS, WIDE16, SUMS], TURN,
        blocks, slopes_1, local_back, factor_0, ahead, behind,
    )
    blocks, dmixed_0 = round_trip(blocks, lambda b: mix_step(mix_grad_kernel, BLOCKS, 0, b, field, slopes_0), 1)
    grads = weight_grad(0, spectrum_0, dmixed_0, grads)
    grad_hidden, mixing, offset_grads = call(
        end_kernel,
        [WIDE32, jax.ShapeDtypeStruct((C, 2, C), F32), jax.ShapeDtypeStruct((2, C), F32)],
        TURN,
        blocks, slopes_0, local_back, ahead, later,
    )

    def cells(value):
        return jnp.transpose(value.reshape(C, 8, Q), (1, 0, 2))[None]

    grad_spectral = jnp.transpose(grads.reshape(2, 2, C, 2, 16, 4, C), (0, 1, 2, 6, 3, 4, 5))
    return (
        cells(final),
        cells(grad_hidden),
        grad_spectral,
        jnp.transpose(mixing, (1, 0, 2)),
        offset_grads,
    )


def solution(mesh):
    names = ("z", "h", "core", "ylo", "x")
    fine = Mesh(mesh.devices.reshape(8, 2, 2, 2, 4), names)
    rows, cols = ("z", "h", "core"), ("ylo", "x")
    grid = P(rows, cols, None, None)
    modes = P(None, None, None, None, cols, None, rows)
    return jax.shard_map(
        per_device,
        mesh=fine,
        in_specs=(grid, modes, P(), P(), grid),
        out_specs=(grid, grid, modes, P(), P()),
        check_vma=False,
    )
```

```python
import functools
import math

import jax
import jax.numpy as jnp
import ml_dtypes
import numpy as np
from jax import lax
from jax.experimental import pallas as pl
from jax.experimental.pallas import tpu as pltpu
from jax.sharding import Mesh, PartitionSpec as P

KX = 16
KY = 16
KZ = 16
KT = 8
NZ = 64
NT = 16
NX = 32
NY = 64
C = 20
Q = NZ * NT
ROWS = 160
PADS = (2, 3, 6, 7)

F32 = jnp.float32
BF16 = jnp.bfloat16
HIGH = lax.Precision.HIGHEST
PARAMS = pltpu.CompilerParams(vmem_limit_bytes=32 * 1024 * 1024)


def depth_tables():
    rows = np.arange(256)
    g, m4, r, mh = rows % 16, rows // 16 % 4, rows // 64 % 2, rows // 128
    m = 16 * (g // 2) + 8 * mh + 4 * (g % 2) + m4
    freq_z, freq_t = m // KT - KZ // 2, m % KT
    cells = np.arange(Q)
    phase = (freq_z[:, None] * (cells // NT) * NT + freq_t[:, None] * (cells % NT) * NZ) % Q
    angle = phase * (2.0 * np.pi / Q)
    parts = np.where(r[:, None] == 0, np.cos(angle), -np.sin(angle))
    weight = np.where(freq_t == 0, 1.0, 2.0)[:, None]
    ahead = (parts / math.sqrt(Q)).astype(np.float32).astype(ml_dtypes.bfloat16)
    behind = (parts * weight / math.sqrt(2 * KZ * KT)).astype(np.float32)
    return ahead, behind.astype(ml_dtypes.bfloat16)


def row_table(sign, factor):
    half, jj, kx = np.meshgrid(np.arange(2), np.arange(4), np.arange(KX), indexing="ij")
    x = 4 * (jj // 2) + 2 * half + jj % 2
    angle = (x * (kx - KX // 2) % NX) * (2.0 * np.pi / NX)
    pairs = np.stack([np.cos(angle), sign * np.sin(angle)], axis=-1) * factor
    pairs = pairs.astype(np.float32).astype(ml_dtypes.bfloat16).astype(np.float32)
    return pairs


def column_table():
    y = np.arange(128)[None, :] % 8
    ky = np.arange(64)[:, None] // 4
    angle = (y * (ky - KY // 2) % NY) * (2.0 * np.pi / NY)
    both = np.concatenate([np.cos(angle), np.sin(angle)], axis=0) / math.sqrt(NY)
    return both.astype(np.float32)


def iota(shape, axis):
    return lax.broadcasted_iota(jnp.int32, shape, axis)


def halves(value):
    high = value.astype(BF16)
    return high, (value - high.astype(F32)).astype(BF16)


def dot2(value, table):
    high, low = halves(value)
    return jnp.dot(high, table, preferred_element_type=F32) + jnp.dot(
        low, table, preferred_element_type=F32
    )


def dot_rows(left, right):
    return lax.dot_general(left, right, (((1,), (1,)), ((), ())), preferred_element_type=F32)


def erf(value):
    value = jnp.clip(value, -3.832506856900711, 3.832506856900711)
    square = value * value
    top = jnp.full_like(value, 0.00022905065861350646)
    for term in (0.0034082910107109506, 0.050955695062380861, 0.18520832239976145, 1.128379143519084):
        top = top * square + term
    base = jnp.full_like(value, -1.1791602954361697e-7)
    for term in (
        0.000023547966471313185,
        0.0010179625278914885,
        0.014070470171167667,
        0.11098505178285362,
        0.49746925110067538,
        1.0,
    ):
        base = base * square + term
    return value * top / base


def gelu_parts(preact):
    ramp = 0.5 * (1.0 + erf(preact * (1.0 / math.sqrt(2.0))))
    bell = jnp.exp(-0.5 * preact * preact) * (1.0 / math.sqrt(2.0 * math.pi))
    return preact * ramp, ramp + preact * bell


def compact(ref):
    return len(ref.shape) == 4


def read_main(ref, g, k):
    if compact(ref):
        return jnp.concatenate([ref[g, 2 * k], ref[g, 2 * k + 1]], axis=0)
    return ref[g, 8 * k : 8 * k + 8, :]


def read_rest(ref, g):
    if compact(ref):
        both = jnp.concatenate([ref[g, 4], ref[g, 4]], axis=0)
        return jnp.where(iota((8, 128), 0) < 4, both, pltpu.roll(both, 2, 0))
    return ref[g, 16:24, :]


def write_main(ref, g, k, value):
    if compact(ref):
        ref[g, 2 * k] = value[0:4, :]
        ref[g, 2 * k + 1] = value[4:8, :]
    else:
        ref[g, 8 * k : 8 * k + 8, :] = value


def write_rest(ref, g, value):
    if compact(ref):
        ref[g, 4] = jnp.where(iota((8, 128), 0) < 2, value, pltpu.roll(value, 6, 0))[0:4, :]
    else:
        ref[g, 16:24, :] = value


def pack(spectra, out_ref, main, rest):
    main[...] = jnp.transpose(spectra[:128, :])
    for g in range(16):
        for k in range(2):
            write_main(out_ref, g, k, main[pl.ds(128 * k + g, 8, stride=16), :])
    left, right = spectra[128:, :128], spectra[128:, 128:]
    lane = iota((32, 128), 1) % 64 // 16
    pieces = []
    for m in range(4):
        first = pltpu.roll(left, (128 - 16 * m) % 128, 1)
        second = pltpu.roll(right, (144 - 16 * m) % 128, 1)
        pieces.append(jnp.where(lane == 0, first, jnp.where(lane == 1, second, 0.0)))
    rest[...] = jnp.transpose(jnp.concatenate(pieces, axis=0))
    for g in range(16):
        write_rest(out_ref, g, rest[pl.ds(g, 8, stride=16), :])


def unpack(blocks, main, rest):
    for g in range(16):
        for k in range(2):
            main[pl.ds(128 * k + g, 8, stride=16), :] = read_main(blocks, g, k)
        rest[pl.ds(g, 8, stride=16), :] = read_rest(blocks, g)
    turned = jnp.transpose(rest[...])
    lane = iota((32, 128), 1) % 64 // 16
    left = right = jnp.zeros((32, 128), F32)
    for m in range(4):
        piece = turned[32 * m : 32 * m + 32, :]
        left = jnp.where(lane == m, pltpu.roll(piece, 16 * m, 1), left)
        right = jnp.where(lane == m, pltpu.roll(piece, (112 + 16 * m) % 128, 1), right)
    return jnp.concatenate(
        [jnp.transpose(main[...]), jnp.concatenate([left, right], axis=1)], axis=0
    )


def rotate(value, sign):
    return sign * pltpu.roll(value, 4, 0)


def turn_sign():
    return jnp.where(iota((8, 128), 0) < 4, -1.0, 1.0).astype(F32)


def pad_rows():
    return iota((8, 128), 0) % 4 >= 2


def start_kernel(field, ahead, out_ref, token, main, rest, near, table, sems):
    copies = []
    for part in range(2):
        cols = pl.ds(512 * part, 512)
        copies.append(
            (
                pltpu.make_async_copy(field.at[:, cols], near.at[part], sems.at[2 * part]),
                pltpu.make_async_copy(ahead.at[:, cols], table.at[part], sems.at[2 * part + 1]),
            )
        )
        for copy in copies[-1]:
            copy.start()
    token[...] = jnp.zeros_like(token)
    spectra = None
    for part in range(2):
        for copy in copies[part]:
            copy.wait()
        term = dot_rows(near[part], table[part])
        spectra = term if spectra is None else spectra + term
    pack(spectra, out_ref, main, rest)


def prepare_kernel(
    token, weights, table, above, far_pointwise, far_biases,
    first, second, twiddle, near_above, local_back, local_ahead, offsets,
    near, padded_rows, pointwise, biases, sems,
):
    small = [
        pltpu.make_async_copy(far_pointwise, pointwise, sems.at[2]),
        pltpu.make_async_copy(far_biases, biases, sems.at[3]),
    ]
    for copy in small:
        copy.start()
    copies = [
        pltpu.make_async_copy(weights.at[layer], near.at[layer], sems.at[layer]) for layer in range(2)
    ]
    late = [
        pltpu.make_async_copy(table, twiddle, sems.at[4]),
        pltpu.make_async_copy(above, near_above, sems.at[5]),
    ]
    for copy in copies + late:
        copy.start()
    padded_rows[...] = jnp.zeros_like(padded_rows)
    for copy in small:
        copy.wait()
    owner = (iota((ROWS, C), 0) // 8 == iota((ROWS, C), 1)).astype(F32)
    same = iota((ROWS, ROWS), 0) % 8 == iota((ROWS, ROWS), 1) % 8
    for layer in range(2):
        mixing = pointwise[layer].astype(F32)
        rows = jnp.dot(owner, mixing, precision=HIGH, preferred_element_type=F32)
        wide = lax.dot_general(
            rows, owner, (((1,), (1,)), ((), ())), precision=HIGH, preferred_element_type=F32
        )
        wide = jnp.where(same, wide, 0.0)
        local_back[layer] = wide.astype(BF16)
        padded = jnp.zeros((256, 256), F32)
        padded = jnp.concatenate(
            [
                jnp.concatenate([wide, jnp.zeros((ROWS, 96), F32)], axis=1),
                jnp.zeros((96, 256), F32),
            ],
            axis=0,
        )
        local_ahead[layer] = jnp.transpose(padded)[:ROWS, :ROWS].astype(BF16)
    offsets[...] = lax.dot_general(
        owner, biases[...], (((1,), (1,)), ((), ())), precision=HIGH, preferred_element_type=F32
    )
    for layer, out_ref in ((0, first), (1, second)):
        copies[layer].wait()
        for part in range(2):
            for c in range(C):
                slot = c % 4
                padded_rows[slot, :, 0:C] = near[layer, part, c]
                out_ref[part, c] = jnp.transpose(padded_rows[slot])[:24, :]
    for copy in late:
        copy.wait()


def entry(table, half, jj, kx):
    first, second = (jnp.where(half == 0, float(a), float(b)) for a, b in zip(*table[:, jj, kx]))
    return first, second


def x_ahead_kernel(table, blocks, *others):
    out_ref = others[-1]
    half = lax.axis_index("h")
    sign = turn_sign()
    place = iota((8, 128), 0) % 4
    for part in range(3):
        groups = [[None] * 4 for _ in range(4)]
        turned = [[None] * 4 for _ in range(4)]
        for jj in range(4):
            x0, x1, x2, x3 = (
                read_main(blocks, jj + 4 * i, part) if part < 2 else read_rest(blocks, jj + 4 * i)
                for i in range(4)
            )
            even, odd = x0 + x2, x0 - x2
            even_other, odd_other = x1 + x3, rotate(x1 - x3, sign)
            found = (even + even_other, odd - odd_other, even - even_other, odd + odd_other)
            for k in range(4):
                groups[k][jj] = found[k]
                turned[k][jj] = rotate(found[k], sign)
        modes = []
        for kx in range(KX):
            total = None
            for jj in range(4):
                real, imag = entry(table, half, jj, kx)
                term = real * groups[kx % 4][jj] + imag * turned[kx % 4][jj]
                total = term if total is None else total + term
            if part < 2:
                write_main(out_ref, part * 8 + kx // 2, kx % 2, total)
            else:
                modes.append(total)
        if part == 2:
            for k in range(8):
                first, second = modes[2 * k], modes[2 * k + 1]
                near = jnp.where(place == 0, first, pltpu.roll(second, 1, 0))
                write_rest(out_ref, k, near)
                near = jnp.where(place == 0, pltpu.roll(first, 7, 0), second)
                write_rest(out_ref, 8 + k, near)


def x_behind_kernel(table, blocks, out_ref):
    half = lax.axis_index("h")
    sign = turn_sign()
    place = iota((8, 128), 0) % 4
    sums = None if compact(blocks) else block_sums(blocks)
    for part in range(3):
        totals = [[None] * 4 for _ in range(4)]
        for kx in range(KX):
            if part < 2:
                mode = read_main(blocks, part * 8 + kx // 2, kx % 2)
            else:
                first, second = read_rest(blocks, kx // 2), read_rest(blocks, 8 + kx // 2)
                if kx % 2 == 0:
                    second = pltpu.roll(second, 1, 0)
                else:
                    first = pltpu.roll(first, 7, 0)
                mode = jnp.where(place == 0, first, jnp.where(place == 1, second, 0.0))
            turned = rotate(mode, sign)
            for jj in range(4):
                real, imag = entry(table, half, jj, kx)
                term = real * mode + imag * turned
                old = totals[kx % 4][jj]
                totals[kx % 4][jj] = term if old is None else old + term
        for jj in range(4):
            h0, h1, h2, h3 = (totals[k][jj] for k in range(4))
            even, odd = h0 + h2, h0 - h2
            even_other, odd_other = h1 + h3, rotate(h1 - h3, sign)
            found = (even + even_other, odd + odd_other, even - even_other, odd - odd_other)
            for i in range(4):
                if part < 2:
                    write_main(out_ref, jj + 4 * i, part, found[i])
                elif sums is None:
                    write_rest(out_ref, jj + 4 * i, found[i])
                else:
                    write_rest(out_ref, jj + 4 * i, jnp.where(place >= 2, sums, found[i]))


def channel_rows():
    lane = iota((32, 256), 1)
    owner = jnp.where(lane < 128, lane // 8, 16 + lane // 8 % 4)
    return (owner == iota((32, 256), 0)).astype(F32).astype(BF16)


def times(value, factor):
    return (
        value[0] * factor[0] - value[1] * factor[1],
        value[0] * factor[1] + value[1] * factor[0],
    )


def plus(one, two):
    return one[0] + two[0], one[1] + two[1]


def minus(one, two):
    return one[0] - two[0], one[1] - two[1]


def fourth(values, sign):
    even, odd = plus(values[0], values[2]), minus(values[0], values[2])
    even_other, odd_other = plus(values[1], values[3]), minus(values[1], values[3])
    turned = (-sign * odd_other[1], sign * odd_other[0])
    return plus(even, even_other), plus(odd, turned), minus(even, even_other), minus(odd, turned)


def odd_turn(y, sign):
    low = iota((8, 128), 0) < 4
    angle = math.pi * y / 4
    return jnp.where(low, 1.0, math.cos(angle)), jnp.where(low, 0.0, sign * math.sin(angle))


def y_ahead(blocks, twiddle, wide):
    low = iota((8, 128), 0) < 4
    keep = iota((8, 128), 0) % 4 == iota((8, 128), 1) // 32
    units = [[] for _ in range(4)]
    for y in range(8):
        other = read_rest(blocks, y) + read_rest(blocks, 8 + y)
        for k in range(2):
            value = read_main(blocks, y, k) + read_main(blocks, 8 + y, k)
            swapped = pltpu.roll(value, 4, 0)
            units[k].append((jnp.where(low, value, swapped), jnp.where(low, swapped, value)))
            units[2 + k].append(
                (
                    jnp.broadcast_to(other[k : k + 1, :], (8, 128)),
                    jnp.broadcast_to(other[4 + k : 5 + k, :], (8, 128)),
                )
            )
    turns = [odd_turn(y, -1.0) for y in range(8)]
    for unit in range(4):
        values = [units[unit][0]] + [times(units[unit][y], turns[y]) for y in range(1, 8)]
        groups = fourth([plus(values[n], values[n + 4]) for n in range(4)], -1.0)
        lanes = slice(0, 128) if unit < 2 else slice(128, 256)
        for pair in range(8):
            at = 8 * pair
            factor = (twiddle[at : at + 8, :], -twiddle[64 + at : 72 + at, :])
            real, imag = times(groups[pair % 4], factor)
            if unit >= 2:
                real, imag = jnp.where(keep, real, 0.0), jnp.where(keep, imag, 0.0)
            at += 64 * (unit % 2)
            wide[at : at + 8, lanes] = real
            wide[128 + at : 136 + at, lanes] = imag
    high, low_part = halves(wide[...])
    table = channel_rows()
    return dot_rows(table, high) + dot_rows(table, low_part)


def y_behind(modes, twiddle, scale, pads, wide, out_ref):
    wide[...] = dot2(jnp.transpose(modes), channel_rows())
    row = iota((8, 128), 0)
    low = row < 4
    keep = row % 4 == iota((8, 128), 1) // 32
    turns = [odd_turn(y, 1.0) for y in range(8)]
    rests = [pads] * 8
    for unit in range(4):
        k = unit % 2
        lanes = slice(0, 128) if unit < 2 else slice(128, 256)
        values = []
        for pair in range(8):
            at = 8 * pair
            factor = (twiddle[at : at + 8, :] * scale, twiddle[64 + at : 72 + at, :] * scale)
            at += 64 * k
            values.append(times((wide[at : at + 8, lanes], wide[128 + at : 136 + at, lanes]), factor))
        groups = fourth([plus(values[n], values[n + 4]) for n in range(4)], 1.0)
        for y in range(8):
            real, imag = groups[y % 4] if y == 0 else times(groups[y % 4], turns[y])
            if unit < 2:
                real = real + pltpu.roll(real, 4, 0)
                imag = imag + pltpu.roll(imag, 4, 0)
                value = jnp.where(low, real, imag)
                write_main(out_ref, y, k, value)
                write_main(out_ref, 8 + y, k, value)
            else:
                for r, value in ((0, real), (1, imag)):
                    value = jnp.where(keep, value, 0.0)
                    for step in (4, 2, 1):
                        value = value + pltpu.roll(value, step, 0)
                    rests[y] = jnp.where(row == 4 * r + k, value, rests[y])
    for y in range(8):
        write_rest(out_ref, y, rests[y])
        write_rest(out_ref, 8 + y, rests[y])


def mix_kernel(blocks, weights, twiddle, out_ref, spectrum, wide, mixed):
    spectrum[...] = y_ahead(blocks, twiddle, wide)
    out_real = out_imag = jnp.zeros((24, 128), F32)
    for c in range(C):
        first = jnp.broadcast_to(spectrum[c : c + 1, 0:128], (24, 128))
        second = jnp.broadcast_to(spectrum[c : c + 1, 128:256], (24, 128))
        w_real, w_imag = weights[0, c], weights[1, c]
        out_real += first * w_real - second * w_imag
        out_imag += first * w_imag + second * w_real
    mixed[0:24, 0:128] = out_real
    mixed[0:24, 128:256] = out_imag
    mixed[24:32, :] = jnp.zeros((8, 256), F32)
    y_behind(mixed[...], twiddle, 2.0, jnp.zeros((8, 128), F32), wide, out_ref)


def mix_grad_kernel(blocks, weights, twiddle, field, slopes, out_ref, dmixed, wide, mixed):
    sums = cell_sums(field, slopes)
    dmixed[...] = 2.0 * y_ahead(blocks, twiddle, wide)
    real, imag = dmixed[0:24, 0:128], dmixed[0:24, 128:256]
    for c in range(C):
        w_real, w_imag = weights[0, c], weights[1, c]
        mixed[c : c + 1, 0:128] = jnp.sum(w_real * real + w_imag * imag, axis=0, keepdims=True)
        mixed[c : c + 1, 128:256] = jnp.sum(w_real * imag - w_imag * real, axis=0, keepdims=True)
    mixed[C:32, :] = jnp.zeros((32 - C, 256), F32)
    y_behind(mixed[...], twiddle, 1.0, sums, wide, out_ref)


def weight_grad_body(spectrum, dmixed, out_ref, scale):
    turned, other = jnp.transpose(spectrum[...]), jnp.transpose(dmixed[...]) * scale
    for at in range(0, 128, 32):
        rows = slice(at, at + 32)
        under = slice(128 + at, 160 + at)
        real, imag = other[rows, 0:C], other[under, 0:C]
        s_real, s_imag = turned[rows, :], turned[under, :]
        for c in range(C):
            first = jnp.broadcast_to(s_real[:, c : c + 1], (32, C))
            second = jnp.broadcast_to(s_imag[:, c : c + 1], (32, C))
            out_ref[0, 0, c, rows, :] = first * real - second * imag
            out_ref[0, 1, c, rows, :] = first * imag + second * real


MODE_SCALE = math.sqrt(2.0 * KX * KY * KZ * KT / (NX * NY * NZ * NT))
CELL_SCALE = 1.0 / math.sqrt(NX * NY * NZ * NT)


def weight_grad_first(spectrum, dmixed, out_ref):
    weight_grad_body(spectrum, dmixed, out_ref, MODE_SCALE)


def weight_grad_second(spectrum, dmixed, held, out_ref):
    weight_grad_body(spectrum, dmixed, out_ref, MODE_SCALE)


def layer_kernel(blocks, field, local, offset, ahead, behind, out_ref, new_field, slope, main, rest):
    layer = 0
    high, low = halves(unpack(blocks, main, rest))
    spectra = None
    for at in range(0, Q, 256):
        cols = slice(at, at + 256)
        table = behind[:, cols]
        preact = jnp.dot(high, table, preferred_element_type=F32)
        preact += jnp.dot(low, table, preferred_element_type=F32)
        preact += jnp.dot(local[layer], field[:, cols], preferred_element_type=F32)
        preact += offset[:, layer : layer + 1]
        value, factor = gelu_parts(preact)
        value = value.astype(BF16)
        new_field[:, cols] = value
        slope[:, cols] = factor
        term = dot_rows(value, ahead[:, cols])
        spectra = term if spectra is None else spectra + term
    pack(spectra, out_ref, main, rest)


def top_kernel(blocks, field, local, offset, upstream, behind, out_ref, slopes, main, rest):
    layer = 1
    high, low = halves(unpack(blocks, main, rest))
    spectra = None
    for at in range(0, Q, 256):
        cols = slice(at, at + 256)
        table = behind[:, cols]
        preact = jnp.dot(high, table, preferred_element_type=F32)
        preact += jnp.dot(low, table, preferred_element_type=F32)
        preact += jnp.dot(local[layer], field[:, cols], preferred_element_type=F32)
        preact += offset[:, layer : layer + 1]
        factor = gelu_parts(preact)[1]
        slope = (upstream[:, cols].astype(F32) * factor).astype(BF16)
        slopes[:, cols] = slope
        term = dot_rows(slope, table)
        spectra = term if spectra is None else spectra + term
    pack(spectra, out_ref, main, rest)


def final_kernel(blocks, field, local, offset, behind, final, main, rest):
    layer = 1
    high, low = halves(unpack(blocks, main, rest))
    for at in range(0, Q, 256):
        cols = slice(at, at + 256)
        table = behind[:, cols]
        preact = jnp.dot(high, table, preferred_element_type=F32)
        preact += jnp.dot(low, table, preferred_element_type=F32)
        preact += jnp.dot(local[layer], field[:, cols], preferred_element_type=F32)
        preact += offset[:, layer : layer + 1]
        final[:, cols] = gelu_parts(preact)[0]


def block_sums(blocks):
    total = blocks[0, 16:24, :]
    for g in range(1, 16):
        total = total + blocks[g, 16:24, :]
    return jnp.where(pad_rows(), total, 0.0)


def back_kernel(
    blocks, slopes, local, factor, ahead, behind, out_ref, new_slopes, sums, main, rest
):
    layer = 1
    sums[...] = block_sums(blocks)
    high, low = halves(unpack(blocks, main, rest))
    spectra = None
    for at in range(0, Q, 256):
        cols = slice(at, at + 256)
        table = ahead[:, cols]
        grad = jnp.dot(high, table, preferred_element_type=F32)
        grad += jnp.dot(low, table, preferred_element_type=F32)
        grad += jnp.dot(local[layer], slopes[:, cols], preferred_element_type=F32)
        grad = grad.astype(BF16).astype(F32)
        slope = (grad * factor[:, cols]).astype(BF16)
        new_slopes[:, cols] = slope
        term = dot_rows(slope, behind[:, cols])
        spectra = term if spectra is None else spectra + term
    pack(spectra, out_ref, main, rest)


def end_kernel(blocks, slopes, local, ahead, later, grad_ref, mixing, offsets, main, rest):
    for at_layer, total in ((0, block_sums(blocks)), (1, later[...])):
        row = iota((24, 8), 0) // 6
        col = iota((24, 8), 1)
        pick = sum(((row == i) & (col == PADS[i])).astype(F32) for i in range(4))
        wide = jnp.dot(pick, total, precision=HIGH, preferred_element_type=F32)
        wide = jnp.where(iota((24, 128), 1) // C == iota((24, 128), 0) % 6, wide, 0.0)
        place = (iota((128, 128), 0) % C == iota((128, 128), 1)).astype(F32)
        found = jnp.dot(wide, place, precision=HIGH, preferred_element_type=F32) * CELL_SCALE
        for c in range(C):
            mixing[c, at_layer : at_layer + 1, :] = found[c : c + 1, 0:C]
        offsets[at_layer : at_layer + 1, :] = found[C : C + 1, 0:C]
    layer = 0
    high, low = halves(unpack(blocks, main, rest))
    for at in range(0, Q, 256):
        cols = slice(at, at + 256)
        table = ahead[:, cols]
        grad = jnp.dot(high, table, preferred_element_type=F32)
        grad += jnp.dot(low, table, preferred_element_type=F32)
        grad += jnp.dot(local[layer], slopes[:, cols], preferred_element_type=F32)
        grad_ref[:, cols] = grad


def cell_sums(field, slopes):
    slope = slopes[...]
    pairs = jnp.concatenate(
        [dot_rows(field[...], slope), dot_rows(jnp.ones((8, Q), BF16), slope)], axis=0
    )
    pairs = jnp.where(iota((168, ROWS), 0) % 8 == iota((168, ROWS), 1) % 8, pairs, 0.0)
    lane = iota((ROWS, 128), 1)
    place = ((lane < 6 * C) & (lane % C == iota((ROWS, 128), 0) // 8)).astype(F32)
    wide = dot2(pairs, place.astype(BF16))
    wide = jnp.where(iota((168, 128), 1) // C == iota((168, 128), 0) // 8 % 6, wide, 0.0)
    row = iota((8, 168), 0)
    owner = iota((8, 168), 1) // 48
    pick = sum(((owner == i) & (row == PADS[i])).astype(F32) for i in range(4))
    pick, (high, low) = pick.astype(BF16), halves(wide)
    return jnp.dot(pick, high, preferred_element_type=F32) + jnp.dot(
        pick, low, preferred_element_type=F32
    )


VM = pl.BlockSpec(memory_space=pltpu.VMEM)
FAR = pl.BlockSpec(memory_space=pltpu.HBM)
BLOCKS = jax.ShapeDtypeStruct((16, 24, 128), F32)
SLABS = jax.ShapeDtypeStruct((16, 5, 4, 128), F32)
MODES = jax.ShapeDtypeStruct((32, 256), F32)
WIDE16 = jax.ShapeDtypeStruct((ROWS, Q), BF16)
WIDE32 = jax.ShapeDtypeStruct((ROWS, Q), F32)
SUMS = jax.ShapeDtypeStruct((8, 128), F32)
TURN = [pltpu.VMEM((256, 128), F32), pltpu.VMEM((128, 128), F32)]
MIX = [pltpu.VMEM((256, 256), F32), pltpu.VMEM((32, 256), F32)]
WEIGHTS = jax.ShapeDtypeStruct((2, C, 24, 128), F32)


def call(kernel, shapes, scratch, *operands, specs=None, cost=None, params=PARAMS):
    many = isinstance(shapes, (list, tuple))
    return pl.pallas_call(
        kernel,
        out_shape=shapes,
        in_specs=specs or [VM] * len(operands),
        out_specs=[VM] * len(shapes) if many else VM,
        scratch_shapes=scratch,
        compiler_params=params,
        cost_estimate=cost,
    )(*operands)


def far(value):
    return pltpu.with_memory_space_constraint(value, pltpu.HBM)


def swap_rows(value):
    return lax.all_to_all(value, ("z", "core"), split_axis=0, concat_axis=0, tiled=True)


def swap_cols(value):
    return lax.all_to_all(value, ("h", "ylo", "x"), split_axis=0, concat_axis=0, tiled=True)


def per_device(hidden_in, spectral, pointwise, biases, upstream):
    ahead, behind = (jnp.asarray(t) for t in depth_tables())
    root = 1.0 / math.sqrt(NX)
    to_modes = [row_table(-1.0, f) for f in (root, 0.25)]
    to_rows = [row_table(1.0, f) for f in (0.25, root)]
    field = jnp.transpose(hidden_in[0], (1, 0, 2)).reshape(ROWS, Q)
    above = jnp.transpose(upstream[0], (1, 0, 2)).reshape(ROWS, Q)
    weights = jnp.transpose(spectral, (0, 1, 2, 4, 5, 6, 3)).reshape(2, 2, C, 128, C)

    def x_step(kernel, table, shape, blocks, *after):
        return call(
            functools.partial(kernel, table), shape, [], blocks, *after,
            specs=[VM] + [FAR] * len(after),
        )

    def mix_step(kernel, shape, layer, blocks, *more):
        return call(kernel, [shape, MODES], MIX, blocks, turned[layer], twiddle, *more)

    def weight_grad(layer, spectrum, dmixed, held=None):
        out_spec = pl.BlockSpec((1, 2, C, 128, C), lambda i: (layer, 0, 0, 0, 0))
        mode_spec = pl.BlockSpec((32, 256), lambda i: (0, 0))
        operands = (spectrum, dmixed) + (() if held is None else (held,))
        return pl.pallas_call(
            weight_grad_first if held is None else weight_grad_second,
            grid=(1,),
            out_shape=jax.ShapeDtypeStruct((2, 2, C, 128, C), F32),
            in_specs=[mode_spec, mode_spec] + [pl.BlockSpec(memory_space=pl.ANY)] * (held is not None),
            out_specs=out_spec,
            input_output_aliases={} if held is None else {2: 0},
            compiler_params=PARAMS,
            cost_estimate=pl.CostEstimate(flops=2000000, bytes_accessed=3000000, transcendentals=0),
        )(*operands)

    def round_trip(blocks, step, side, *after):
        blocks = swap_rows(blocks)
        blocks = swap_cols(x_step(x_ahead_kernel, to_modes[side], SLABS, blocks, *after))
        blocks, modes = step(blocks)
        blocks = swap_cols(blocks)
        blocks = swap_rows(x_step(x_behind_kernel, to_rows[side], BLOCKS if side else SLABS, blocks))
        return blocks, modes

    loads = [
        pltpu.VMEM((2, ROWS, 512), BF16),
        pltpu.VMEM((2, 256, 512), BF16),
        pltpu.SemaphoreType.DMA((4,)),
    ]
    blocks, token = call(
        start_kernel, [SLABS, SUMS], TURN + loads, far(field), far(ahead), specs=[FAR, FAR]
    )
    squares = jax.ShapeDtypeStruct((2, ROWS, ROWS), BF16)
    first, second, twiddle, near_above, local_back, local_ahead, offsets = call(
        prepare_kernel,
        [
            WEIGHTS, WEIGHTS, jax.ShapeDtypeStruct((128, 128), F32), WIDE16,
            squares, squares, jax.ShapeDtypeStruct((ROWS, 2), F32),
        ],
        [
            pltpu.VMEM((2, 2, C, 128, C), F32),
            pltpu.VMEM((4, 128, 128), F32),
            pltpu.VMEM((2, C, C), BF16),
            pltpu.VMEM((2, C), F32),
            pltpu.SemaphoreType.DMA((6,)),
        ],
        token, *(far(a) for a in (weights, jnp.asarray(column_table()), above, pointwise, biases)),
        specs=[pl.BlockSpec(memory_space=pl.ANY)] + [FAR] * 5,
        cost=pl.CostEstimate(flops=60000000, bytes_accessed=8000000, transcendentals=0),
    )
    turned = (first, second)
    blocks, spectrum_0 = round_trip(blocks, lambda b: mix_step(mix_kernel, SLABS, 0, b), 0, twiddle)
    blocks, field_1, factor_0 = call(
        layer_kernel, [SLABS, WIDE16, WIDE32], TURN,
        blocks, field, local_ahead, offsets, ahead, behind,
    )
    blocks, spectrum_1 = round_trip(blocks, lambda b: mix_step(mix_kernel, SLABS, 1, b), 0)
    final = call(
        final_kernel, WIDE32, TURN,
        blocks, field_1, local_ahead, offsets, behind,
        cost=pl.CostEstimate(flops=200000000, bytes_accessed=2000000, transcendentals=0),
    )
    blocks, slopes_1 = call(
        top_kernel, [SLABS, WIDE16],
        TURN,
        blocks, field_1, local_ahead, offsets, near_above, behind,
    )
    blocks, dmixed_1 = round_trip(blocks, lambda b: mix_step(mix_grad_kernel, BLOCKS, 1, b, field_1, slopes_1), 1)
    grads = weight_grad(1, spectrum_1, dmixed_1)
    blocks, slopes_0, later = call(
        back_kernel, [SLABS, WIDE16, SUMS], TURN,
        blocks, slopes_1, local_back, factor_0, ahead, behind,
    )
    blocks, dmixed_0 = round_trip(blocks, lambda b: mix_step(mix_grad_kernel, BLOCKS, 0, b, field, slopes_0), 1)
    grads = weight_grad(0, spectrum_0, dmixed_0, grads)
    grad_hidden, mixing, offset_grads = call(
        end_kernel,
        [WIDE32, jax.ShapeDtypeStruct((C, 2, C), F32), jax.ShapeDtypeStruct((2, C), F32)],
        TURN,
        blocks, slopes_0, local_back, ahead, later,
    )

    def cells(value):
        return jnp.transpose(value.reshape(C, 8, Q), (1, 0, 2))[None]

    grad_spectral = jnp.transpose(grads.reshape(2, 2, C, 2, 16, 4, C), (0, 1, 2, 6, 3, 4, 5))
    return (
        cells(final),
        cells(grad_hidden),
        grad_spectral,
        jnp.transpose(mixing, (1, 0, 2)),
        offset_grads,
    )


def solution(mesh):
    names = ("z", "h", "core", "ylo", "x")
    fine = Mesh(mesh.devices.reshape(8, 2, 2, 2, 4), names)
    rows, cols = ("z", "h", "core"), ("ylo", "x")
    grid = P(rows, cols, None, None)
    modes = P(None, None, None, None, cols, None, rows)
    return jax.shard_map(
        per_device,
        mesh=fine,
        in_specs=(grid, modes, P(), P(), grid),
        out_specs=(grid, grid, modes, P(), P()),
        check_vma=False,
    )
```

```python
import functools
import math

import jax
import jax.numpy as jnp
import ml_dtypes
import numpy as np
from jax import lax
from jax.experimental import pallas as pl
from jax.experimental.pallas import tpu as pltpu
from jax.sharding import Mesh, PartitionSpec as P

KX = 16
KY = 16
KZ = 16
KT = 8
NZ = 64
NT = 16
NX = 32
NY = 64
C = 20
Q = NZ * NT
ROWS = 160
PADS = (2, 3, 6, 7)

F32 = jnp.float32
BF16 = jnp.bfloat16
HIGH = lax.Precision.HIGHEST
PARAMS = pltpu.CompilerParams(vmem_limit_bytes=32 * 1024 * 1024)


def depth_tables():
    rows = np.arange(256)
    g, m4, r, mh = rows % 16, rows // 16 % 4, rows // 64 % 2, rows // 128
    m = 16 * (g // 2) + 8 * mh + 4 * (g % 2) + m4
    freq_z, freq_t = m // KT - KZ // 2, m % KT
    cells = np.arange(Q)
    phase = (freq_z[:, None] * (cells // NT) * NT + freq_t[:, None] * (cells % NT) * NZ) % Q
    angle = phase * (2.0 * np.pi / Q)
    parts = np.where(r[:, None] == 0, np.cos(angle), -np.sin(angle))
    weight = np.where(freq_t == 0, 1.0, 2.0)[:, None]
    ahead = (parts / math.sqrt(Q)).astype(np.float32).astype(ml_dtypes.bfloat16)
    behind = (parts * weight / math.sqrt(2 * KZ * KT)).astype(np.float32)
    return ahead, behind.astype(ml_dtypes.bfloat16)


def row_table(sign, factor):
    half, jj, kx = np.meshgrid(np.arange(2), np.arange(4), np.arange(KX), indexing="ij")
    x = 4 * (jj // 2) + 2 * half + jj % 2
    angle = (x * (kx - KX // 2) % NX) * (2.0 * np.pi / NX)
    pairs = np.stack([np.cos(angle), sign * np.sin(angle)], axis=-1) * factor
    pairs = pairs.astype(np.float32).astype(ml_dtypes.bfloat16).astype(np.float32)
    return pairs


def column_table():
    y = np.arange(128)[None, :] % 8
    ky = np.arange(64)[:, None] // 4
    angle = (y * (ky - KY // 2) % NY) * (2.0 * np.pi / NY)
    both = np.concatenate([np.cos(angle), np.sin(angle)], axis=0) / math.sqrt(NY)
    return both.astype(np.float32)


def iota(shape, axis):
    return lax.broadcasted_iota(jnp.int32, shape, axis)


def halves(value):
    high = value.astype(BF16)
    return high, (value - high.astype(F32)).astype(BF16)


def dot2(value, table):
    high, low = halves(value)
    return jnp.dot(high, table, preferred_element_type=F32) + jnp.dot(
        low, table, preferred_element_type=F32
    )


def dot_rows(left, right):
    return lax.dot_general(left, right, (((1,), (1,)), ((), ())), preferred_element_type=F32)


def erf(value):
    value = jnp.clip(value, -3.832506856900711, 3.832506856900711)
    square = value * value
    top = jnp.full_like(value, 0.00022905065861350646)
    for term in (0.0034082910107109506, 0.050955695062380861, 0.18520832239976145, 1.128379143519084):
        top = top * square + term
    base = jnp.full_like(value, -1.1791602954361697e-7)
    for term in (
        0.000023547966471313185,
        0.0010179625278914885,
        0.014070470171167667,
        0.11098505178285362,
        0.49746925110067538,
        1.0,
    ):
        base = base * square + term
    return value * top / base


def gelu_parts(preact):
    ramp = 0.5 * (1.0 + erf(preact * (1.0 / math.sqrt(2.0))))
    bell = jnp.exp(-0.5 * preact * preact) * (1.0 / math.sqrt(2.0 * math.pi))
    return preact * ramp, ramp + preact * bell


def compact(ref):
    return len(ref.shape) == 4


def read_main(ref, g, k):
    if compact(ref):
        return jnp.concatenate([ref[g, 2 * k], ref[g, 2 * k + 1]], axis=0)
    return ref[g, 8 * k : 8 * k + 8, :]


def read_rest(ref, g):
    if compact(ref):
        both = jnp.concatenate([ref[g, 4], ref[g, 4]], axis=0)
        return jnp.where(iota((8, 128), 0) < 4, both, pltpu.roll(both, 2, 0))
    return ref[g, 16:24, :]


def write_main(ref, g, k, value):
    if compact(ref):
        ref[g, 2 * k] = value[0:4, :]
        ref[g, 2 * k + 1] = value[4:8, :]
    else:
        ref[g, 8 * k : 8 * k + 8, :] = value


def write_rest(ref, g, value):
    if compact(ref):
        ref[g, 4] = jnp.where(iota((8, 128), 0) < 2, value, pltpu.roll(value, 6, 0))[0:4, :]
    else:
        ref[g, 16:24, :] = value


def pack(spectra, out_ref, main, rest):
    main[0:256, :] = jnp.transpose(spectra[:128, :])
    for g in range(16):
        for k in range(2):
            write_main(out_ref, g, k, main[pl.ds(128 * k + g, 8, stride=16), :])
    left, right = spectra[128:, :128], spectra[128:, 128:]
    lane = iota((32, 128), 1) % 64 // 16
    pieces = []
    for m in range(4):
        first = pltpu.roll(left, (128 - 16 * m) % 128, 1)
        second = pltpu.roll(right, (144 - 16 * m) % 128, 1)
        pieces.append(jnp.where(lane == 0, first, jnp.where(lane == 1, second, 0.0)))
    rest[0:128, :] = jnp.transpose(jnp.concatenate(pieces, axis=0))
    for g in range(16):
        write_rest(out_ref, g, rest[pl.ds(g, 8, stride=16), :])


def unpack(blocks, main, rest):
    for g in range(16):
        for k in range(2):
            main[pl.ds(128 * k + g, 8, stride=16), :] = read_main(blocks, g, k)
        rest[pl.ds(g, 8, stride=16), :] = read_rest(blocks, g)
    turned = jnp.transpose(rest[0:128, :])
    lane = iota((32, 128), 1) % 64 // 16
    left = right = jnp.zeros((32, 128), F32)
    for m in range(4):
        piece = turned[32 * m : 32 * m + 32, :]
        left = jnp.where(lane == m, pltpu.roll(piece, 16 * m, 1), left)
        right = jnp.where(lane == m, pltpu.roll(piece, (112 + 16 * m) % 128, 1), right)
    return jnp.concatenate(
        [jnp.transpose(main[0:256, :]), jnp.concatenate([left, right], axis=1)], axis=0
    )


def rotate(value, sign):
    return sign * pltpu.roll(value, 4, 0)


def turn_sign():
    return jnp.where(iota((8, 128), 0) < 4, -1.0, 1.0).astype(F32)


def pad_rows():
    return iota((8, 128), 0) % 4 >= 2


def start_kernel(field, ahead, out_ref, token, main, rest, near, table, sems):
    copies = []
    for part in range(2):
        cols = pl.ds(512 * part, 512)
        copies.append(
            (
                pltpu.make_async_copy(field.at[:, cols], near.at[part], sems.at[2 * part]),
                pltpu.make_async_copy(ahead.at[:, cols], table.at[part], sems.at[2 * part + 1]),
            )
        )
        for copy in copies[-1]:
            copy.start()
    token[...] = jnp.zeros_like(token)
    spectra = None
    for part in range(2):
        for copy in copies[part]:
            copy.wait()
        term = dot_rows(near[part], table[part])
        spectra = term if spectra is None else spectra + term
    pack(spectra, out_ref, main, rest)


def prepare_kernel(
    token, weights, table, above, far_pointwise, far_biases,
    first, second, twiddle, near_above, local_back, local_ahead, offsets,
    near, padded_rows, pointwise, biases, sems,
):
    small = [
        pltpu.make_async_copy(far_pointwise, pointwise, sems.at[2]),
        pltpu.make_async_copy(far_biases, biases, sems.at[3]),
    ]
    for copy in small:
        copy.start()
    copies = [
        pltpu.make_async_copy(weights.at[layer], near.at[layer], sems.at[layer]) for layer in range(2)
    ]
    late = [
        pltpu.make_async_copy(table, twiddle, sems.at[4]),
        pltpu.make_async_copy(above, near_above, sems.at[5]),
    ]
    for copy in copies + late:
        copy.start()
    padded_rows[...] = jnp.zeros_like(padded_rows)
    for copy in small:
        copy.wait()
    owner = (iota((ROWS, C), 0) // 8 == iota((ROWS, C), 1)).astype(F32)
    same = iota((ROWS, ROWS), 0) % 8 == iota((ROWS, ROWS), 1) % 8
    for layer in range(2):
        mixing = pointwise[layer].astype(F32)
        rows = jnp.dot(owner, mixing, precision=HIGH, preferred_element_type=F32)
        wide = lax.dot_general(
            rows, owner, (((1,), (1,)), ((), ())), precision=HIGH, preferred_element_type=F32
        )
        wide = jnp.where(same, wide, 0.0)
        local_back[layer] = wide.astype(BF16)
        padded = jnp.zeros((256, 256), F32)
        padded = jnp.concatenate(
            [
                jnp.concatenate([wide, jnp.zeros((ROWS, 96), F32)], axis=1),
                jnp.zeros((96, 256), F32),
            ],
            axis=0,
        )
        local_ahead[layer] = jnp.transpose(padded)[:ROWS, :ROWS].astype(BF16)
    offsets[...] = lax.dot_general(
        owner, biases[...], (((1,), (1,)), ((), ())), precision=HIGH, preferred_element_type=F32
    )
    for layer, out_ref in ((0, first), (1, second)):
        copies[layer].wait()
        for part in range(2):
            for c in range(C):
                slot = c % 4
                padded_rows[slot, :, 0:C] = near[layer, part, c]
                out_ref[part, c] = jnp.transpose(padded_rows[slot])[:24, :]
    for copy in late:
        copy.wait()


def entry(table, half, jj, kx):
    first, second = (jnp.where(half == 0, float(a), float(b)) for a, b in zip(*table[:, jj, kx]))
    return first, second


def x_ahead_kernel(table, blocks, *others):
    out_ref = others[-1]
    half = lax.axis_index("h")
    sign = turn_sign()
    place = iota((8, 128), 0) % 4
    for part in range(3):
        groups = [[None] * 4 for _ in range(4)]
        turned = [[None] * 4 for _ in range(4)]
        for jj in range(4):
            x0, x1, x2, x3 = (
                read_main(blocks, jj + 4 * i, part) if part < 2 else read_rest(blocks, jj + 4 * i)
                for i in range(4)
            )
            even, odd = x0 + x2, x0 - x2
            even_other, odd_other = x1 + x3, rotate(x1 - x3, sign)
            found = (even + even_other, odd - odd_other, even - even_other, odd + odd_other)
            for k in range(4):
                groups[k][jj] = found[k]
                turned[k][jj] = rotate(found[k], sign)
        modes = []
        for kx in range(KX):
            total = None
            for jj in range(4):
                real, imag = entry(table, half, jj, kx)
                term = real * groups[kx % 4][jj] + imag * turned[kx % 4][jj]
                total = term if total is None else total + term
            if part < 2:
                write_main(out_ref, part * 8 + kx // 2, kx % 2, total)
            else:
                modes.append(total)
        if part == 2:
            for k in range(8):
                first, second = modes[2 * k], modes[2 * k + 1]
                near = jnp.where(place == 0, first, pltpu.roll(second, 1, 0))
                write_rest(out_ref, k, near)
                near = jnp.where(place == 0, pltpu.roll(first, 7, 0), second)
                write_rest(out_ref, 8 + k, near)


def x_behind_kernel(table, blocks, out_ref):
    half = lax.axis_index("h")
    sign = turn_sign()
    place = iota((8, 128), 0) % 4
    sums = None if compact(blocks) else block_sums(blocks)
    for part in range(3):
        totals = [[None] * 4 for _ in range(4)]
        for kx in range(KX):
            if part < 2:
                mode = read_main(blocks, part * 8 + kx // 2, kx % 2)
            else:
                first, second = read_rest(blocks, kx // 2), read_rest(blocks, 8 + kx // 2)
                if kx % 2 == 0:
                    second = pltpu.roll(second, 1, 0)
                else:
                    first = pltpu.roll(first, 7, 0)
                mode = jnp.where(place == 0, first, jnp.where(place == 1, second, 0.0))
            turned = rotate(mode, sign)
            for jj in range(4):
                real, imag = entry(table, half, jj, kx)
                term = real * mode + imag * turned
                old = totals[kx % 4][jj]
                totals[kx % 4][jj] = term if old is None else old + term
        for jj in range(4):
            h0, h1, h2, h3 = (totals[k][jj] for k in range(4))
            even, odd = h0 + h2, h0 - h2
            even_other, odd_other = h1 + h3, rotate(h1 - h3, sign)
            found = (even + even_other, odd + odd_other, even - even_other, odd - odd_other)
            for i in range(4):
                if part < 2:
                    write_main(out_ref, jj + 4 * i, part, found[i])
                elif sums is None:
                    write_rest(out_ref, jj + 4 * i, found[i])
                else:
                    write_rest(out_ref, jj + 4 * i, jnp.where(place >= 2, sums, found[i]))


def channel_rows():
    lane = iota((32, 256), 1)
    owner = jnp.where(lane < 128, lane // 8, 16 + lane // 8 % 4)
    return (owner == iota((32, 256), 0)).astype(F32).astype(BF16)


def times(value, factor):
    return (
        value[0] * factor[0] - value[1] * factor[1],
        value[0] * factor[1] + value[1] * factor[0],
    )


def plus(one, two):
    return one[0] + two[0], one[1] + two[1]


def minus(one, two):
    return one[0] - two[0], one[1] - two[1]


def fourth(values, sign):
    even, odd = plus(values[0], values[2]), minus(values[0], values[2])
    even_other, odd_other = plus(values[1], values[3]), minus(values[1], values[3])
    turned = (-sign * odd_other[1], sign * odd_other[0])
    return plus(even, even_other), plus(odd, turned), minus(even, even_other), minus(odd, turned)


def odd_turn(y, sign):
    low = iota((8, 128), 0) < 4
    angle = math.pi * y / 4
    return jnp.where(low, 1.0, math.cos(angle)), jnp.where(low, 0.0, sign * math.sin(angle))


def y_ahead(blocks, twiddle, wide):
    low = iota((8, 128), 0) < 4
    keep = iota((8, 128), 0) % 4 == iota((8, 128), 1) // 32
    units = [[] for _ in range(4)]
    for y in range(8):
        other = read_rest(blocks, y) + read_rest(blocks, 8 + y)
        for k in range(2):
            value = read_main(blocks, y, k) + read_main(blocks, 8 + y, k)
            swapped = pltpu.roll(value, 4, 0)
            units[k].append((jnp.where(low, value, swapped), jnp.where(low, swapped, value)))
            units[2 + k].append(
                (
                    jnp.broadcast_to(other[k : k + 1, :], (8, 128)),
                    jnp.broadcast_to(other[4 + k : 5 + k, :], (8, 128)),
                )
            )
    turns = [odd_turn(y, -1.0) for y in range(8)]
    for unit in range(4):
        values = [units[unit][0]] + [times(units[unit][y], turns[y]) for y in range(1, 8)]
        groups = fourth([plus(values[n], values[n + 4]) for n in range(4)], -1.0)
        lanes = slice(0, 128) if unit < 2 else slice(128, 256)
        for pair in range(8):
            at = 8 * pair
            factor = (twiddle[at : at + 8, :], -twiddle[64 + at : 72 + at, :])
            real, imag = times(groups[pair % 4], factor)
            if unit >= 2:
                real, imag = jnp.where(keep, real, 0.0), jnp.where(keep, imag, 0.0)
            at += 64 * (unit % 2)
            wide[at : at + 8, lanes] = real
            wide[128 + at : 136 + at, lanes] = imag
    high, low_part = halves(wide[...])
    table = channel_rows()
    return dot_rows(table, high) + dot_rows(table, low_part)


def y_behind(modes, twiddle, scale, pads, wide, out_ref):
    wide[...] = dot2(jnp.transpose(modes), channel_rows())
    row = iota((8, 128), 0)
    low = row < 4
    keep = row % 4 == iota((8, 128), 1) // 32
    turns = [odd_turn(y, 1.0) for y in range(8)]
    rests = [pads] * 8
    for unit in range(4):
        k = unit % 2
        lanes = slice(0, 128) if unit < 2 else slice(128, 256)
        values = []
        for pair in range(8):
            at = 8 * pair
            factor = (twiddle[at : at + 8, :] * scale, twiddle[64 + at : 72 + at, :] * scale)
            at += 64 * k
            values.append(times((wide[at : at + 8, lanes], wide[128 + at : 136 + at, lanes]), factor))
        groups = fourth([plus(values[n], values[n + 4]) for n in range(4)], 1.0)
        for y in range(8):
            real, imag = groups[y % 4] if y == 0 else times(groups[y % 4], turns[y])
            if unit < 2:
                real = real + pltpu.roll(real, 4, 0)
                imag = imag + pltpu.roll(imag, 4, 0)
                value = jnp.where(low, real, imag)
                write_main(out_ref, y, k, value)
                write_main(out_ref, 8 + y, k, value)
            else:
                for r, value in ((0, real), (1, imag)):
                    value = jnp.where(keep, value, 0.0)
                    for step in (4, 2, 1):
                        value = value + pltpu.roll(value, step, 0)
                    rests[y] = jnp.where(row == 4 * r + k, value, rests[y])
    for y in range(8):
        write_rest(out_ref, y, rests[y])
        write_rest(out_ref, 8 + y, rests[y])


def mix_kernel(blocks, weights, twiddle, out_ref, spectrum, wide, mixed):
    spectrum[...] = y_ahead(blocks, twiddle, wide)
    out_real = out_imag = jnp.zeros((24, 128), F32)
    for c in range(C):
        first = jnp.broadcast_to(spectrum[c : c + 1, 0:128], (24, 128))
        second = jnp.broadcast_to(spectrum[c : c + 1, 128:256], (24, 128))
        w_real, w_imag = weights[0, c], weights[1, c]
        out_real += first * w_real - second * w_imag
        out_imag += first * w_imag + second * w_real
    mixed[0:24, 0:128] = out_real
    mixed[0:24, 128:256] = out_imag
    mixed[24:32, :] = jnp.zeros((8, 256), F32)
    y_behind(mixed[...], twiddle, 2.0, jnp.zeros((8, 128), F32), wide, out_ref)


def mix_grad_kernel(blocks, weights, twiddle, field, slopes, out_ref, dmixed, wide, mixed):
    sums = cell_sums(field, slopes)
    dmixed[...] = 2.0 * y_ahead(blocks, twiddle, wide)
    real, imag = dmixed[0:24, 0:128], dmixed[0:24, 128:256]
    for c in range(C):
        w_real, w_imag = weights[0, c], weights[1, c]
        mixed[c : c + 1, 0:128] = jnp.sum(w_real * real + w_imag * imag, axis=0, keepdims=True)
        mixed[c : c + 1, 128:256] = jnp.sum(w_real * imag - w_imag * real, axis=0, keepdims=True)
    mixed[C:32, :] = jnp.zeros((32 - C, 256), F32)
    y_behind(mixed[...], twiddle, 1.0, sums, wide, out_ref)


def weight_grad_body(spectrum, dmixed, out_ref, scale):
    turned, other = jnp.transpose(spectrum[...]), jnp.transpose(dmixed[...]) * scale
    for at in range(0, 128, 32):
        rows = slice(at, at + 32)
        under = slice(128 + at, 160 + at)
        real, imag = other[rows, 0:C], other[under, 0:C]
        s_real, s_imag = turned[rows, :], turned[under, :]
        for c in range(C):
            first = jnp.broadcast_to(s_real[:, c : c + 1], (32, C))
            second = jnp.broadcast_to(s_imag[:, c : c + 1], (32, C))
            out_ref[0, 0, c, rows, :] = first * real - second * imag
            out_ref[0, 1, c, rows, :] = first * imag + second * real


MODE_SCALE = math.sqrt(2.0 * KX * KY * KZ * KT / (NX * NY * NZ * NT))
CELL_SCALE = 1.0 / math.sqrt(NX * NY * NZ * NT)


def weight_grad_first(spectrum, dmixed, out_ref):
    weight_grad_body(spectrum, dmixed, out_ref, MODE_SCALE)


def weight_grad_second(spectrum, dmixed, held, out_ref):
    weight_grad_body(spectrum, dmixed, out_ref, MODE_SCALE)


def layer_kernel(blocks, field, local, offset, ahead, behind, out_ref, new_field, slope, main, rest):
    layer = 0
    high, low = halves(unpack(blocks, main, rest))
    spectra = None
    for at in range(0, Q, 256):
        cols = slice(at, at + 256)
        table = behind[:, cols]
        preact = jnp.dot(high, table, preferred_element_type=F32)
        preact += jnp.dot(low, table, preferred_element_type=F32)
        preact += jnp.dot(local[layer], field[:, cols], preferred_element_type=F32)
        preact += offset[:, layer : layer + 1]
        value, factor = gelu_parts(preact)
        value = value.astype(BF16)
        new_field[:, cols] = value
        slope[:, cols] = factor
        term = dot_rows(value, ahead[:, cols])
        spectra = term if spectra is None else spectra + term
    pack(spectra, out_ref, main, rest)


def top_kernel(blocks, field, local, offset, upstream, behind, out_ref, slopes, main, rest):
    layer = 1
    high, low = halves(unpack(blocks, main, rest))
    spectra = None
    for at in range(0, Q, 256):
        cols = slice(at, at + 256)
        table = behind[:, cols]
        preact = jnp.dot(high, table, preferred_element_type=F32)
        preact += jnp.dot(low, table, preferred_element_type=F32)
        preact += jnp.dot(local[layer], field[:, cols], preferred_element_type=F32)
        preact += offset[:, layer : layer + 1]
        factor = gelu_parts(preact)[1]
        slope = (upstream[:, cols].astype(F32) * factor).astype(BF16)
        slopes[:, cols] = slope
        term = dot_rows(slope, table)
        spectra = term if spectra is None else spectra + term
    pack(spectra, out_ref, main, rest)


def final_kernel(blocks, field, local, offset, behind, final, main, rest):
    layer = 1
    high, low = halves(unpack(blocks, main, rest))
    for at in range(0, Q, 256):
        cols = slice(at, at + 256)
        table = behind[:, cols]
        preact = jnp.dot(high, table, preferred_element_type=F32)
        preact += jnp.dot(low, table, preferred_element_type=F32)
        preact += jnp.dot(local[layer], field[:, cols], preferred_element_type=F32)
        preact += offset[:, layer : layer + 1]
        final[:, cols] = gelu_parts(preact)[0]


def block_sums(blocks):
    total = blocks[0, 16:24, :]
    for g in range(1, 16):
        total = total + blocks[g, 16:24, :]
    return jnp.where(pad_rows(), total, 0.0)


def back_kernel(
    blocks, slopes, local, factor, ahead, behind, out_ref, new_slopes, sums, main, rest
):
    layer = 1
    sums[...] = block_sums(blocks)
    high, low = halves(unpack(blocks, main, rest))
    spectra = None
    for at in range(0, Q, 256):
        cols = slice(at, at + 256)
        table = ahead[:, cols]
        grad = jnp.dot(high, table, preferred_element_type=F32)
        grad += jnp.dot(low, table, preferred_element_type=F32)
        grad += jnp.dot(local[layer], slopes[:, cols], preferred_element_type=F32)
        grad = grad.astype(BF16).astype(F32)
        slope = (grad * factor[:, cols]).astype(BF16)
        new_slopes[:, cols] = slope
        term = dot_rows(slope, behind[:, cols])
        spectra = term if spectra is None else spectra + term
    pack(spectra, out_ref, main, rest)


def end_kernel(blocks, slopes, local, ahead, later, grad_ref, mixing, offsets, main, rest):
    layer = 0
    high, low = halves(unpack(blocks, main, rest))
    for at in range(0, Q, 256):
        cols = slice(at, at + 256)
        table = ahead[:, cols]
        grad = jnp.dot(high, table, preferred_element_type=F32)
        grad += jnp.dot(low, table, preferred_element_type=F32)
        grad += jnp.dot(local[layer], slopes[:, cols], preferred_element_type=F32)
        grad_ref[:, cols] = grad
    row = iota((24, 8), 0) // 6
    col = iota((24, 8), 1)
    pick = sum(((row == i) & (col == PADS[i])).astype(F32) for i in range(4)).astype(BF16)
    place = (iota((128, 128), 0) % C == iota((128, 128), 1)).astype(F32).astype(BF16)
    keep = iota((24, 128), 1) // C == iota((24, 128), 0) % 6
    for at_layer, total in ((0, block_sums(blocks)), (1, later[...])):
        first, second = halves(total)
        wide = jnp.dot(pick, first, preferred_element_type=F32)
        wide += jnp.dot(pick, second, preferred_element_type=F32)
        found = dot2(jnp.where(keep, wide, 0.0), place) * CELL_SCALE
        for c in range(C):
            mixing[c, at_layer : at_layer + 1, :] = found[c : c + 1, 0:C]
        offsets[at_layer : at_layer + 1, :] = found[C : C + 1, 0:C]


def cell_sums(field, slopes):
    slope = slopes[...]
    pairs = jnp.concatenate(
        [dot_rows(field[...], slope), dot_rows(jnp.ones((8, Q), BF16), slope)], axis=0
    )
    pairs = jnp.where(iota((168, ROWS), 0) % 8 == iota((168, ROWS), 1) % 8, pairs, 0.0)
    lane = iota((ROWS, 128), 1)
    place = ((lane < 6 * C) & (lane % C == iota((ROWS, 128), 0) // 8)).astype(F32)
    wide = dot2(pairs, place.astype(BF16))
    wide = jnp.where(iota((168, 128), 1) // C == iota((168, 128), 0) // 8 % 6, wide, 0.0)
    row = iota((8, 168), 0)
    owner = iota((8, 168), 1) // 48
    pick = sum(((owner == i) & (row == PADS[i])).astype(F32) for i in range(4))
    pick, (high, low) = pick.astype(BF16), halves(wide)
    return jnp.dot(pick, high, preferred_element_type=F32) + jnp.dot(
        pick, low, preferred_element_type=F32
    )


VM = pl.BlockSpec(memory_space=pltpu.VMEM)
FAR = pl.BlockSpec(memory_space=pltpu.HBM)
BLOCKS = jax.ShapeDtypeStruct((16, 24, 128), F32)
SLABS = jax.ShapeDtypeStruct((16, 5, 4, 128), F32)
MODES = jax.ShapeDtypeStruct((32, 256), F32)
WIDE16 = jax.ShapeDtypeStruct((ROWS, Q), BF16)
WIDE32 = jax.ShapeDtypeStruct((ROWS, Q), F32)
SUMS = jax.ShapeDtypeStruct((8, 128), F32)
TURN = [pltpu.VMEM((272, 128), F32), pltpu.VMEM((144, 128), F32)]
MIX = [pltpu.VMEM((256, 256), F32), pltpu.VMEM((32, 256), F32)]
WEIGHTS = jax.ShapeDtypeStruct((2, C, 24, 128), F32)


def call(kernel, shapes, scratch, *operands, specs=None, cost=None, params=PARAMS):
    many = isinstance(shapes, (list, tuple))
    return pl.pallas_call(
        kernel,
        out_shape=shapes,
        in_specs=specs or [VM] * len(operands),
        out_specs=[VM] * len(shapes) if many else VM,
        scratch_shapes=scratch,
        compiler_params=params,
        cost_estimate=cost,
    )(*operands)


def far(value):
    return pltpu.with_memory_space_constraint(value, pltpu.HBM)


def swap_rows(value):
    return lax.all_to_all(value, ("z", "core"), split_axis=0, concat_axis=0, tiled=True)


def swap_cols(value):
    return lax.all_to_all(value, ("h", "ylo", "x"), split_axis=0, concat_axis=0, tiled=True)


def per_device(hidden_in, spectral, pointwise, biases, upstream):
    ahead, behind = (jnp.asarray(t) for t in depth_tables())
    root = 1.0 / math.sqrt(NX)
    to_modes = [row_table(-1.0, f) for f in (root, 0.25)]
    to_rows = [row_table(1.0, f) for f in (0.25, root)]
    field = jnp.transpose(hidden_in[0], (1, 0, 2)).reshape(ROWS, Q)
    above = jnp.transpose(upstream[0], (1, 0, 2)).reshape(ROWS, Q)
    weights = jnp.transpose(spectral, (0, 1, 2, 4, 5, 6, 3)).reshape(2, 2, C, 128, C)

    def x_step(kernel, table, shape, blocks, *after):
        return call(
            functools.partial(kernel, table), shape, [], blocks, *after,
            specs=[VM] + [FAR] * len(after),
        )

    def mix_step(kernel, shape, layer, blocks, *more):
        return call(kernel, [shape, MODES], MIX, blocks, turned[layer], twiddle, *more)

    def weight_grad(layer, spectrum, dmixed, held=None):
        out_spec = pl.BlockSpec((1, 2, C, 128, C), lambda i: (layer, 0, 0, 0, 0))
        mode_spec = pl.BlockSpec((32, 256), lambda i: (0, 0))
        operands = (spectrum, dmixed) + (() if held is None else (held,))
        return pl.pallas_call(
            weight_grad_first if held is None else weight_grad_second,
            grid=(1,),
            out_shape=jax.ShapeDtypeStruct((2, 2, C, 128, C), F32),
            in_specs=[mode_spec, mode_spec] + [pl.BlockSpec(memory_space=pl.ANY)] * (held is not None),
            out_specs=out_spec,
            input_output_aliases={} if held is None else {2: 0},
            compiler_params=PARAMS,
            cost_estimate=pl.CostEstimate(flops=2000000, bytes_accessed=3000000, transcendentals=0),
        )(*operands)

    def round_trip(blocks, step, side, *after):
        blocks = swap_rows(blocks)
        blocks = swap_cols(x_step(x_ahead_kernel, to_modes[side], SLABS, blocks, *after))
        blocks, modes = step(blocks)
        blocks = swap_cols(blocks)
        blocks = swap_rows(x_step(x_behind_kernel, to_rows[side], BLOCKS if side else SLABS, blocks))
        return blocks, modes

    loads = [
        pltpu.VMEM((2, ROWS, 512), BF16),
        pltpu.VMEM((2, 256, 512), BF16),
        pltpu.SemaphoreType.DMA((4,)),
    ]
    blocks, token = call(
        start_kernel, [SLABS, SUMS], TURN + loads, far(field), far(ahead), specs=[FAR, FAR]
    )
    squares = jax.ShapeDtypeStruct((2, ROWS, ROWS), BF16)
    first, second, twiddle, near_above, local_back, local_ahead, offsets = call(
        prepare_kernel,
        [
            WEIGHTS, WEIGHTS, jax.ShapeDtypeStruct((128, 128), F32), WIDE16,
            squares, squares, jax.ShapeDtypeStruct((ROWS, 2), F32),
        ],
        [
            pltpu.VMEM((2, 2, C, 128, C), F32),
            pltpu.VMEM((4, 128, 128), F32),
            pltpu.VMEM((2, C, C), BF16),
            pltpu.VMEM((2, C), F32),
            pltpu.SemaphoreType.DMA((6,)),
        ],
        token, *(far(a) for a in (weights, jnp.asarray(column_table()), above, pointwise, biases)),
        specs=[pl.BlockSpec(memory_space=pl.ANY)] + [FAR] * 5,
        cost=pl.CostEstimate(flops=60000000, bytes_accessed=8000000, transcendentals=0),
    )
    turned = (first, second)
    blocks, spectrum_0 = round_trip(blocks, lambda b: mix_step(mix_kernel, SLABS, 0, b), 0, twiddle)
    blocks, field_1, factor_0 = call(
        layer_kernel, [SLABS, WIDE16, WIDE32], TURN,
        blocks, field, local_ahead, offsets, ahead, behind,
    )
    blocks, spectrum_1 = round_trip(blocks, lambda b: mix_step(mix_kernel, SLABS, 1, b), 0)
    final = call(
        final_kernel, WIDE32, TURN,
        blocks, field_1, local_ahead, offsets, behind,
        cost=pl.CostEstimate(flops=200000000, bytes_accessed=2000000, transcendentals=0),
    )
    blocks, slopes_1 = call(
        top_kernel, [SLABS, WIDE16],
        TURN,
        blocks, field_1, local_ahead, offsets, near_above, behind,
    )
    blocks, dmixed_1 = round_trip(blocks, lambda b: mix_step(mix_grad_kernel, BLOCKS, 1, b, field_1, slopes_1), 1)
    grads = weight_grad(1, spectrum_1, dmixed_1)
    blocks, slopes_0, later = call(
        back_kernel, [SLABS, WIDE16, SUMS], TURN,
        blocks, slopes_1, local_back, factor_0, ahead, behind,
    )
    blocks, dmixed_0 = round_trip(blocks, lambda b: mix_step(mix_grad_kernel, BLOCKS, 0, b, field, slopes_0), 1)
    grads = weight_grad(0, spectrum_0, dmixed_0, grads)
    grad_hidden, mixing, offset_grads = call(
        end_kernel,
        [WIDE32, jax.ShapeDtypeStruct((C, 2, C), F32), jax.ShapeDtypeStruct((2, C), F32)],
        TURN,
        blocks, slopes_0, local_back, ahead, later,
    )

    def cells(value):
        return jnp.transpose(value.reshape(C, 8, Q), (1, 0, 2))[None]

    grad_spectral = jnp.transpose(grads.reshape(2, 2, C, 2, 16, 4, C), (0, 1, 2, 6, 3, 4, 5))
    return (
        cells(final),
        cells(grad_hidden),
        grad_spectral,
        jnp.transpose(mixing, (1, 0, 2)),
        offset_grads,
    )


def solution(mesh):
    names = ("z", "h", "core", "ylo", "x")
    fine = Mesh(mesh.devices.reshape(8, 2, 2, 2, 4), names)
    rows, cols = ("z", "h", "core"), ("ylo", "x")
    grid = P(rows, cols, None, None)
    modes = P(None, None, None, None, cols, None, rows)
    return jax.shard_map(
        per_device,
        mesh=fine,
        in_specs=(grid, modes, P(), P(), grid),
        out_specs=(grid, grid, modes, P(), P()),
        check_vma=False,
    )
```

```python
import functools
import math

import jax
import jax.numpy as jnp
import ml_dtypes
import numpy as np
from jax import lax
from jax.experimental import pallas as pl
from jax.experimental.pallas import tpu as pltpu
from jax.sharding import Mesh, PartitionSpec as P

KX = 16
KY = 16
KZ = 16
KT = 8
NZ = 64
NT = 16
NX = 32
NY = 64
C = 20
Q = NZ * NT
ROWS = 160
PADS = (2, 3, 6, 7)

F32 = jnp.float32
BF16 = jnp.bfloat16
HIGH = lax.Precision.HIGHEST
PARAMS = pltpu.CompilerParams(vmem_limit_bytes=32 * 1024 * 1024)


def depth_tables():
    rows = np.arange(256)
    g, m4, r, mh = rows % 16, rows // 16 % 4, rows // 64 % 2, rows // 128
    m = 16 * (g // 2) + 8 * mh + 4 * (g % 2) + m4
    freq_z, freq_t = m // KT - KZ // 2, m % KT
    cells = np.arange(Q)
    phase = (freq_z[:, None] * (cells // NT) * NT + freq_t[:, None] * (cells % NT) * NZ) % Q
    angle = phase * (2.0 * np.pi / Q)
    parts = np.where(r[:, None] == 0, np.cos(angle), -np.sin(angle))
    weight = np.where(freq_t == 0, 1.0, 2.0)[:, None]
    ahead = (parts / math.sqrt(Q)).astype(np.float32).astype(ml_dtypes.bfloat16)
    behind = (parts * weight / math.sqrt(2 * KZ * KT)).astype(np.float32)
    return ahead, behind.astype(ml_dtypes.bfloat16)


def row_table(sign, factor):
    half, jj, kx = np.meshgrid(np.arange(2), np.arange(4), np.arange(KX), indexing="ij")
    x = 4 * (jj // 2) + 2 * half + jj % 2
    angle = (x * (kx - KX // 2) % NX) * (2.0 * np.pi / NX)
    pairs = np.stack([np.cos(angle), sign * np.sin(angle)], axis=-1) * factor
    pairs = pairs.astype(np.float32).astype(ml_dtypes.bfloat16).astype(np.float32)
    return pairs


def column_table():
    y = np.arange(128)[None, :] % 8
    ky = np.arange(64)[:, None] // 4
    angle = (y * (ky - KY // 2) % NY) * (2.0 * np.pi / NY)
    both = np.concatenate([np.cos(angle), np.sin(angle)], axis=0) / math.sqrt(NY)
    return both.astype(np.float32)


def iota(shape, axis):
    return lax.broadcasted_iota(jnp.int32, shape, axis)


def halves(value):
    high = value.astype(BF16)
    return high, (value - high.astype(F32)).astype(BF16)


def dot2(value, table):
    high, low = halves(value)
    return jnp.dot(high, table, preferred_element_type=F32) + jnp.dot(
        low, table, preferred_element_type=F32
    )


def dot_rows(left, right):
    return lax.dot_general(left, right, (((1,), (1,)), ((), ())), preferred_element_type=F32)


def erf(value):
    value = jnp.clip(value, -3.832506856900711, 3.832506856900711)
    square = value * value
    top = jnp.full_like(value, 0.00022905065861350646)
    for term in (0.0034082910107109506, 0.050955695062380861, 0.18520832239976145, 1.128379143519084):
        top = top * square + term
    base = jnp.full_like(value, -1.1791602954361697e-7)
    for term in (
        0.000023547966471313185,
        0.0010179625278914885,
        0.014070470171167667,
        0.11098505178285362,
        0.49746925110067538,
        1.0,
    ):
        base = base * square + term
    return value * top / base


def gelu_parts(preact):
    ramp = 0.5 * (1.0 + erf(preact * (1.0 / math.sqrt(2.0))))
    bell = jnp.exp(-0.5 * preact * preact) * (1.0 / math.sqrt(2.0 * math.pi))
    return preact * ramp, ramp + preact * bell


def compact(ref):
    return len(ref.shape) == 4


def read_main(ref, g, k):
    if compact(ref):
        return jnp.concatenate([ref[g, 2 * k], ref[g, 2 * k + 1]], axis=0)
    return ref[g, 8 * k : 8 * k + 8, :]


def read_rest(ref, g):
    if compact(ref):
        both = jnp.concatenate([ref[g, 4], ref[g, 4]], axis=0)
        return jnp.where(iota((8, 128), 0) < 4, both, pltpu.roll(both, 2, 0))
    return ref[g, 16:24, :]


def write_main(ref, g, k, value):
    if compact(ref):
        ref[g, 2 * k] = value[0:4, :]
        ref[g, 2 * k + 1] = value[4:8, :]
    else:
        ref[g, 8 * k : 8 * k + 8, :] = value


def write_rest(ref, g, value):
    if compact(ref):
        ref[g, 4] = jnp.where(iota((8, 128), 0) < 2, value, pltpu.roll(value, 6, 0))[0:4, :]
    else:
        ref[g, 16:24, :] = value


def pack(spectra, out_ref, main, rest):
    main[0:256, :] = jnp.transpose(spectra[:128, :])
    for g in range(16):
        for k in range(2):
            write_main(out_ref, g, k, main[pl.ds(128 * k + g, 8, stride=16), :])
    left, right = spectra[128:, :128], spectra[128:, 128:]
    lane = iota((32, 128), 1) % 64 // 16
    pieces = []
    for m in range(4):
        first = pltpu.roll(left, (128 - 16 * m) % 128, 1)
        second = pltpu.roll(right, (144 - 16 * m) % 128, 1)
        pieces.append(jnp.where(lane == 0, first, jnp.where(lane == 1, second, 0.0)))
    rest[0:128, :] = jnp.transpose(jnp.concatenate(pieces, axis=0))
    for g in range(16):
        write_rest(out_ref, g, rest[pl.ds(g, 8, stride=16), :])


def unpack(blocks, main, rest):
    for g in range(16):
        for k in range(2):
            main[pl.ds(128 * k + g, 8, stride=16), :] = read_main(blocks, g, k)
        rest[pl.ds(g, 8, stride=16), :] = read_rest(blocks, g)
    turned = jnp.transpose(rest[0:128, :])
    lane = iota((32, 128), 1) % 64 // 16
    left = right = jnp.zeros((32, 128), F32)
    for m in range(4):
        piece = turned[32 * m : 32 * m + 32, :]
        left = jnp.where(lane == m, pltpu.roll(piece, 16 * m, 1), left)
        right = jnp.where(lane == m, pltpu.roll(piece, (112 + 16 * m) % 128, 1), right)
    return jnp.concatenate(
        [jnp.transpose(main[0:256, :]), jnp.concatenate([left, right], axis=1)], axis=0
    )


def rotate(value, sign):
    return sign * pltpu.roll(value, 4, 0)


def turn_sign():
    return jnp.where(iota((8, 128), 0) < 4, -1.0, 1.0).astype(F32)


def pad_rows():
    return iota((8, 128), 0) % 4 >= 2


def start_kernel(field, ahead, out_ref, token, main, rest, near, table, sems):
    copies = []
    for part in range(2):
        cols = pl.ds(512 * part, 512)
        copies.append(
            (
                pltpu.make_async_copy(field.at[:, cols], near.at[part], sems.at[2 * part]),
                pltpu.make_async_copy(ahead.at[:, cols], table.at[part], sems.at[2 * part + 1]),
            )
        )
        for copy in copies[-1]:
            copy.start()
    token[...] = jnp.zeros_like(token)
    spectra = None
    for part in range(2):
        for copy in copies[part]:
            copy.wait()
        term = dot_rows(near[part], table[part])
        spectra = term if spectra is None else spectra + term
    pack(spectra, out_ref, main, rest)


def prepare_kernel(
    token, weights, table, above, far_pointwise, far_biases,
    first, second, twiddle, near_above, local_back, local_ahead, offsets,
    near, padded_rows, pointwise, biases, sems,
):
    small = [
        pltpu.make_async_copy(far_pointwise, pointwise, sems.at[2]),
        pltpu.make_async_copy(far_biases, biases, sems.at[3]),
    ]
    for copy in small:
        copy.start()
    copies = [
        pltpu.make_async_copy(weights.at[layer], near.at[layer], sems.at[layer]) for layer in range(2)
    ]
    late = [
        pltpu.make_async_copy(table, twiddle, sems.at[4]),
        pltpu.make_async_copy(above, near_above, sems.at[5]),
    ]
    for copy in copies + late:
        copy.start()
    padded_rows[...] = jnp.zeros_like(padded_rows)
    for copy in small:
        copy.wait()
    owner = (iota((ROWS, C), 0) // 8 == iota((ROWS, C), 1)).astype(F32)
    same = iota((ROWS, ROWS), 0) % 8 == iota((ROWS, ROWS), 1) % 8
    for layer in range(2):
        mixing = pointwise[layer].astype(F32)
        rows = jnp.dot(owner, mixing, precision=HIGH, preferred_element_type=F32)
        wide = lax.dot_general(
            rows, owner, (((1,), (1,)), ((), ())), precision=HIGH, preferred_element_type=F32
        )
        wide = jnp.where(same, wide, 0.0)
        local_back[layer] = wide.astype(BF16)
        padded = jnp.zeros((256, 256), F32)
        padded = jnp.concatenate(
            [
                jnp.concatenate([wide, jnp.zeros((ROWS, 96), F32)], axis=1),
                jnp.zeros((96, 256), F32),
            ],
            axis=0,
        )
        local_ahead[layer] = jnp.transpose(padded)[:ROWS, :ROWS].astype(BF16)
    offsets[...] = lax.dot_general(
        owner, biases[...], (((1,), (1,)), ((), ())), precision=HIGH, preferred_element_type=F32
    )
    for layer, out_ref in ((0, first), (1, second)):
        copies[layer].wait()
        for part in range(2):
            for c in range(C):
                slot = c % 4
                padded_rows[slot, :, 0:C] = near[layer, part, c]
                out_ref[part, c] = jnp.transpose(padded_rows[slot])[:24, :]
    for copy in late:
        copy.wait()


def entry(table, half, jj, kx):
    first, second = (jnp.where(half == 0, float(a), float(b)) for a, b in zip(*table[:, jj, kx]))
    return first, second


def x_ahead_kernel(table, blocks, *others):
    out_ref = others[-1]
    half = lax.axis_index("h")
    sign = turn_sign()
    place = iota((8, 128), 0) % 4
    for part in range(3):
        groups = [[None] * 4 for _ in range(4)]
        turned = [[None] * 4 for _ in range(4)]
        for jj in range(4):
            x0, x1, x2, x3 = (
                read_main(blocks, jj + 4 * i, part) if part < 2 else read_rest(blocks, jj + 4 * i)
                for i in range(4)
            )
            even, odd = x0 + x2, x0 - x2
            even_other, odd_other = x1 + x3, rotate(x1 - x3, sign)
            found = (even + even_other, odd - odd_other, even - even_other, odd + odd_other)
            for k in range(4):
                groups[k][jj] = found[k]
                turned[k][jj] = rotate(found[k], sign)
        modes = []
        for kx in range(KX):
            total = None
            for jj in range(4):
                real, imag = entry(table, half, jj, kx)
                term = real * groups[kx % 4][jj] + imag * turned[kx % 4][jj]
                total = term if total is None else total + term
            if part < 2:
                write_main(out_ref, part * 8 + kx // 2, kx % 2, total)
            else:
                modes.append(total)
        if part == 2:
            for k in range(8):
                first, second = modes[2 * k], modes[2 * k + 1]
                near = jnp.where(place == 0, first, pltpu.roll(second, 1, 0))
                write_rest(out_ref, k, near)
                near = jnp.where(place == 0, pltpu.roll(first, 7, 0), second)
                write_rest(out_ref, 8 + k, near)


def x_behind_kernel(table, blocks, out_ref):
    half = lax.axis_index("h")
    sign = turn_sign()
    place = iota((8, 128), 0) % 4
    sums = None if compact(blocks) else block_sums(blocks)
    for part in range(3):
        totals = [[None] * 4 for _ in range(4)]
        for kx in range(KX):
            if part < 2:
                mode = read_main(blocks, part * 8 + kx // 2, kx % 2)
            else:
                first, second = read_rest(blocks, kx // 2), read_rest(blocks, 8 + kx // 2)
                if kx % 2 == 0:
                    second = pltpu.roll(second, 1, 0)
                else:
                    first = pltpu.roll(first, 7, 0)
                mode = jnp.where(place == 0, first, jnp.where(place == 1, second, 0.0))
            turned = rotate(mode, sign)
            for jj in range(4):
                real, imag = entry(table, half, jj, kx)
                term = real * mode + imag * turned
                old = totals[kx % 4][jj]
                totals[kx % 4][jj] = term if old is None else old + term
        for jj in range(4):
            h0, h1, h2, h3 = (totals[k][jj] for k in range(4))
            even, odd = h0 + h2, h0 - h2
            even_other, odd_other = h1 + h3, rotate(h1 - h3, sign)
            found = (even + even_other, odd + odd_other, even - even_other, odd - odd_other)
            for i in range(4):
                if part < 2:
                    write_main(out_ref, jj + 4 * i, part, found[i])
                elif sums is None:
                    write_rest(out_ref, jj + 4 * i, found[i])
                else:
                    write_rest(out_ref, jj + 4 * i, jnp.where(place >= 2, sums, found[i]))


def channel_rows():
    lane = iota((32, 256), 1)
    owner = jnp.where(lane < 128, lane // 8, 16 + lane // 8 % 4)
    return (owner == iota((32, 256), 0)).astype(F32).astype(BF16)


def times(value, factor):
    return (
        value[0] * factor[0] - value[1] * factor[1],
        value[0] * factor[1] + value[1] * factor[0],
    )


def plus(one, two):
    return one[0] + two[0], one[1] + two[1]


def minus(one, two):
    return one[0] - two[0], one[1] - two[1]


def fourth(values, sign):
    even, odd = plus(values[0], values[2]), minus(values[0], values[2])
    even_other, odd_other = plus(values[1], values[3]), minus(values[1], values[3])
    turned = (-sign * odd_other[1], sign * odd_other[0])
    return plus(even, even_other), plus(odd, turned), minus(even, even_other), minus(odd, turned)


def odd_turn(y, sign):
    low = iota((8, 128), 0) < 4
    angle = math.pi * y / 4
    return jnp.where(low, 1.0, math.cos(angle)), jnp.where(low, 0.0, sign * math.sin(angle))


def y_ahead(blocks, twiddle, wide):
    low = iota((8, 128), 0) < 4
    keep = iota((8, 128), 0) % 4 == iota((8, 128), 1) // 32
    units = [[] for _ in range(4)]
    for y in range(8):
        other = read_rest(blocks, y) + read_rest(blocks, 8 + y)
        for k in range(2):
            value = read_main(blocks, y, k) + read_main(blocks, 8 + y, k)
            swapped = pltpu.roll(value, 4, 0)
            units[k].append((jnp.where(low, value, swapped), jnp.where(low, swapped, value)))
            units[2 + k].append(
                (
                    jnp.broadcast_to(other[k : k + 1, :], (8, 128)),
                    jnp.broadcast_to(other[4 + k : 5 + k, :], (8, 128)),
                )
            )
    turns = [odd_turn(y, -1.0) for y in range(8)]
    for unit in range(4):
        values = [units[unit][0]] + [times(units[unit][y], turns[y]) for y in range(1, 8)]
        groups = fourth([plus(values[n], values[n + 4]) for n in range(4)], -1.0)
        lanes = slice(0, 128) if unit < 2 else slice(128, 256)
        for pair in range(8):
            at = 8 * pair
            factor = (twiddle[at : at + 8, :], -twiddle[64 + at : 72 + at, :])
            real, imag = times(groups[pair % 4], factor)
            if unit >= 2:
                real, imag = jnp.where(keep, real, 0.0), jnp.where(keep, imag, 0.0)
            at += 64 * (unit % 2)
            wide[at : at + 8, lanes] = real
            wide[128 + at : 136 + at, lanes] = imag
    high, low_part = halves(wide[...])
    table = channel_rows()
    return dot_rows(table, high) + dot_rows(table, low_part)


def y_behind(modes, twiddle, scale, pads, wide, out_ref):
    wide[...] = dot2(jnp.transpose(modes), channel_rows())
    row = iota((8, 128), 0)
    low = row < 4
    keep = row % 4 == iota((8, 128), 1) // 32
    turns = [odd_turn(y, 1.0) for y in range(8)]
    rests = [pads] * 8
    for unit in range(4):
        k = unit % 2
        lanes = slice(0, 128) if unit < 2 else slice(128, 256)
        values = []
        for pair in range(8):
            at = 8 * pair
            factor = (twiddle[at : at + 8, :] * scale, twiddle[64 + at : 72 + at, :] * scale)
            at += 64 * k
            values.append(times((wide[at : at + 8, lanes], wide[128 + at : 136 + at, lanes]), factor))
        groups = fourth([plus(values[n], values[n + 4]) for n in range(4)], 1.0)
        for y in range(8):
            real, imag = groups[y % 4] if y == 0 else times(groups[y % 4], turns[y])
            if unit < 2:
                real = real + pltpu.roll(real, 4, 0)
                imag = imag + pltpu.roll(imag, 4, 0)
                value = jnp.where(low, real, imag)
                write_main(out_ref, y, k, value)
                write_main(out_ref, 8 + y, k, value)
            else:
                for r, value in ((0, real), (1, imag)):
                    value = jnp.where(keep, value, 0.0)
                    for step in (4, 2, 1):
                        value = value + pltpu.roll(value, step, 0)
                    rests[y] = jnp.where(row == 4 * r + k, value, rests[y])
    for y in range(8):
        write_rest(out_ref, y, rests[y])
        write_rest(out_ref, 8 + y, rests[y])


def mix_kernel(blocks, weights, twiddle, out_ref, spectrum, wide, mixed):
    spectrum[...] = y_ahead(blocks, twiddle, wide)
    out_real = out_imag = jnp.zeros((24, 128), F32)
    for c in range(C):
        first = jnp.broadcast_to(spectrum[c : c + 1, 0:128], (24, 128))
        second = jnp.broadcast_to(spectrum[c : c + 1, 128:256], (24, 128))
        w_real, w_imag = weights[0, c], weights[1, c]
        out_real += first * w_real - second * w_imag
        out_imag += first * w_imag + second * w_real
    mixed[0:24, 0:128] = out_real
    mixed[0:24, 128:256] = out_imag
    mixed[24:32, :] = jnp.zeros((8, 256), F32)
    y_behind(mixed[...], twiddle, 2.0, jnp.zeros((8, 128), F32), wide, out_ref)


def mix_grad_kernel(blocks, weights, twiddle, field, slopes, out_ref, dmixed, wide, mixed):
    sums = cell_sums(field, slopes)
    dmixed[...] = 2.0 * y_ahead(blocks, twiddle, wide)
    real, imag = dmixed[0:24, 0:128], dmixed[0:24, 128:256]
    for c in range(C):
        w_real, w_imag = weights[0, c], weights[1, c]
        mixed[c : c + 1, 0:128] = jnp.sum(w_real * real + w_imag * imag, axis=0, keepdims=True)
        mixed[c : c + 1, 128:256] = jnp.sum(w_real * imag - w_imag * real, axis=0, keepdims=True)
    mixed[C:32, :] = jnp.zeros((32 - C, 256), F32)
    y_behind(mixed[...], twiddle, 1.0, sums, wide, out_ref)


def weight_grad_body(spectrum, dmixed, out_ref, scale):
    for group in range(4):
        pl.when(pl.program_id(0) == group)(
            functools.partial(weight_grad_group, group, spectrum, dmixed, out_ref, scale)
        )


def weight_grad_group(group, spectrum, dmixed, out_ref, scale):
    turned, other = jnp.transpose(spectrum[...]), jnp.transpose(dmixed[...]) * scale
    for at in range(0, 128, 32):
        rows = slice(at, at + 32)
        under = slice(128 + at, 160 + at)
        real, imag = other[rows, 0:C], other[under, 0:C]
        s_real, s_imag = turned[rows, :], turned[under, :]
        for place in range(5):
            c = 5 * group + place
            first = jnp.broadcast_to(s_real[:, c : c + 1], (32, C))
            second = jnp.broadcast_to(s_imag[:, c : c + 1], (32, C))
            out_ref[0, 0, place, rows, :] = first * real - second * imag
            out_ref[0, 1, place, rows, :] = first * imag + second * real


MODE_SCALE = math.sqrt(2.0 * KX * KY * KZ * KT / (NX * NY * NZ * NT))
CELL_SCALE = 1.0 / math.sqrt(NX * NY * NZ * NT)


def weight_grad_first(spectrum, dmixed, out_ref):
    weight_grad_body(spectrum, dmixed, out_ref, MODE_SCALE)


def weight_grad_second(spectrum, dmixed, held, out_ref):
    weight_grad_body(spectrum, dmixed, out_ref, MODE_SCALE)


def layer_kernel(blocks, field, local, offset, ahead, behind, out_ref, new_field, slope, main, rest):
    layer = 0
    high, low = halves(unpack(blocks, main, rest))
    spectra = None
    for at in range(0, Q, 256):
        cols = slice(at, at + 256)
        table = behind[:, cols]
        preact = jnp.dot(high, table, preferred_element_type=F32)
        preact += jnp.dot(low, table, preferred_element_type=F32)
        preact += jnp.dot(local[layer], field[:, cols], preferred_element_type=F32)
        preact += offset[:, layer : layer + 1]
        value, factor = gelu_parts(preact)
        value = value.astype(BF16)
        new_field[:, cols] = value
        slope[:, cols] = factor
        term = dot_rows(value, ahead[:, cols])
        spectra = term if spectra is None else spectra + term
    pack(spectra, out_ref, main, rest)


def top_kernel(blocks, field, local, offset, upstream, behind, out_ref, slopes, main, rest):
    layer = 1
    high, low = halves(unpack(blocks, main, rest))
    spectra = None
    for at in range(0, Q, 256):
        cols = slice(at, at + 256)
        table = behind[:, cols]
        preact = jnp.dot(high, table, preferred_element_type=F32)
        preact += jnp.dot(low, table, preferred_element_type=F32)
        preact += jnp.dot(local[layer], field[:, cols], preferred_element_type=F32)
        preact += offset[:, layer : layer + 1]
        factor = gelu_parts(preact)[1]
        slope = (upstream[:, cols].astype(F32) * factor).astype(BF16)
        slopes[:, cols] = slope
        term = dot_rows(slope, table)
        spectra = term if spectra is None else spectra + term
    pack(spectra, out_ref, main, rest)


def final_kernel(blocks, field, local, offset, behind, final, main, rest):
    layer = 1
    high, low = halves(unpack(blocks, main, rest))
    for at in range(0, Q, 256):
        cols = slice(at, at + 256)
        table = behind[:, cols]
        preact = jnp.dot(high, table, preferred_element_type=F32)
        preact += jnp.dot(low, table, preferred_element_type=F32)
        preact += jnp.dot(local[layer], field[:, cols], preferred_element_type=F32)
        preact += offset[:, layer : layer + 1]
        final[:, cols] = gelu_parts(preact)[0]


def block_sums(blocks):
    total = blocks[0, 16:24, :]
    for g in range(1, 16):
        total = total + blocks[g, 16:24, :]
    return jnp.where(pad_rows(), total, 0.0)


def back_kernel(
    blocks, slopes, local, factor, ahead, behind, out_ref, new_slopes, sums, main, rest
):
    layer = 1
    sums[...] = block_sums(blocks)
    high, low = halves(unpack(blocks, main, rest))
    spectra = None
    for at in range(0, Q, 256):
        cols = slice(at, at + 256)
        table = ahead[:, cols]
        grad = jnp.dot(high, table, preferred_element_type=F32)
        grad += jnp.dot(low, table, preferred_element_type=F32)
        grad += jnp.dot(local[layer], slopes[:, cols], preferred_element_type=F32)
        grad = grad.astype(BF16).astype(F32)
        slope = (grad * factor[:, cols]).astype(BF16)
        new_slopes[:, cols] = slope
        term = dot_rows(slope, behind[:, cols])
        spectra = term if spectra is None else spectra + term
    pack(spectra, out_ref, main, rest)


def end_kernel(blocks, slopes, local, ahead, later, grad_ref, mixing, offsets, main, rest):
    layer = 0
    high, low = halves(unpack(blocks, main, rest))
    for at in range(0, Q, 256):
        cols = slice(at, at + 256)
        table = ahead[:, cols]
        grad = jnp.dot(high, table, preferred_element_type=F32)
        grad += jnp.dot(low, table, preferred_element_type=F32)
        grad += jnp.dot(local[layer], slopes[:, cols], preferred_element_type=F32)
        grad_ref[:, cols] = grad
    row = iota((24, 8), 0) // 6
    col = iota((24, 8), 1)
    pick = sum(((row == i) & (col == PADS[i])).astype(F32) for i in range(4)).astype(BF16)
    place = (iota((128, 128), 0) % C == iota((128, 128), 1)).astype(F32).astype(BF16)
    keep = iota((24, 128), 1) // C == iota((24, 128), 0) % 6
    for at_layer, total in ((0, block_sums(blocks)), (1, later[...])):
        first, second = halves(total)
        wide = jnp.dot(pick, first, preferred_element_type=F32)
        wide += jnp.dot(pick, second, preferred_element_type=F32)
        found = dot2(jnp.where(keep, wide, 0.0), place) * CELL_SCALE
        for c in range(C):
            mixing[c, at_layer : at_layer + 1, :] = found[c : c + 1, 0:C]
        offsets[at_layer : at_layer + 1, :] = found[C : C + 1, 0:C]


def cell_sums(field, slopes):
    slope = slopes[...]
    pairs = jnp.concatenate(
        [dot_rows(field[...], slope), dot_rows(jnp.ones((8, Q), BF16), slope)], axis=0
    )
    pairs = jnp.where(iota((168, ROWS), 0) % 8 == iota((168, ROWS), 1) % 8, pairs, 0.0)
    lane = iota((ROWS, 128), 1)
    place = ((lane < 6 * C) & (lane % C == iota((ROWS, 128), 0) // 8)).astype(F32)
    wide = dot2(pairs, place.astype(BF16))
    wide = jnp.where(iota((168, 128), 1) // C == iota((168, 128), 0) // 8 % 6, wide, 0.0)
    row = iota((8, 168), 0)
    owner = iota((8, 168), 1) // 48
    pick = sum(((owner == i) & (row == PADS[i])).astype(F32) for i in range(4))
    pick, (high, low) = pick.astype(BF16), halves(wide)
    return jnp.dot(pick, high, preferred_element_type=F32) + jnp.dot(
        pick, low, preferred_element_type=F32
    )


VM = pl.BlockSpec(memory_space=pltpu.VMEM)
FAR = pl.BlockSpec(memory_space=pltpu.HBM)
BLOCKS = jax.ShapeDtypeStruct((16, 24, 128), F32)
SLABS = jax.ShapeDtypeStruct((16, 5, 4, 128), F32)
MODES = jax.ShapeDtypeStruct((32, 256), F32)
WIDE16 = jax.ShapeDtypeStruct((ROWS, Q), BF16)
WIDE32 = jax.ShapeDtypeStruct((ROWS, Q), F32)
SUMS = jax.ShapeDtypeStruct((8, 128), F32)
TURN = [pltpu.VMEM((272, 128), F32), pltpu.VMEM((144, 128), F32)]
MIX = [pltpu.VMEM((256, 256), F32), pltpu.VMEM((32, 256), F32)]
WEIGHTS = jax.ShapeDtypeStruct((2, C, 24, 128), F32)


def call(kernel, shapes, scratch, *operands, specs=None, cost=None, params=PARAMS):
    many = isinstance(shapes, (list, tuple))
    return pl.pallas_call(
        kernel,
        out_shape=shapes,
        in_specs=specs or [VM] * len(operands),
        out_specs=[VM] * len(shapes) if many else VM,
        scratch_shapes=scratch,
        compiler_params=params,
        cost_estimate=cost,
    )(*operands)


def far(value):
    return pltpu.with_memory_space_constraint(value, pltpu.HBM)


def swap_rows(value):
    return lax.all_to_all(value, ("z", "core"), split_axis=0, concat_axis=0, tiled=True)


def swap_cols(value):
    return lax.all_to_all(value, ("h", "ylo", "x"), split_axis=0, concat_axis=0, tiled=True)


def per_device(hidden_in, spectral, pointwise, biases, upstream):
    ahead, behind = (jnp.asarray(t) for t in depth_tables())
    root = 1.0 / math.sqrt(NX)
    to_modes = [row_table(-1.0, f) for f in (root, 0.25)]
    to_rows = [row_table(1.0, f) for f in (0.25, root)]
    field = jnp.transpose(hidden_in[0], (1, 0, 2)).reshape(ROWS, Q)
    above = jnp.transpose(upstream[0], (1, 0, 2)).reshape(ROWS, Q)
    weights = jnp.transpose(spectral, (0, 1, 2, 4, 5, 6, 3)).reshape(2, 2, C, 128, C)

    def x_step(kernel, table, shape, blocks, *after):
        return call(
            functools.partial(kernel, table), shape, [], blocks, *after,
            specs=[VM] + [FAR] * len(after),
        )

    def mix_step(kernel, shape, layer, blocks, *more):
        return call(kernel, [shape, MODES], MIX, blocks, turned[layer], twiddle, *more)

    def weight_grad(layer, spectrum, dmixed, held=None):
        out_spec = pl.BlockSpec((1, 2, 5, 128, C), lambda i: (layer, 0, i, 0, 0))
        mode_spec = pl.BlockSpec((32, 256), lambda i: (0, 0))
        operands = (spectrum, dmixed) + (() if held is None else (held,))
        return pl.pallas_call(
            weight_grad_first if held is None else weight_grad_second,
            grid=(4,),
            out_shape=jax.ShapeDtypeStruct((2, 2, C, 128, C), F32),
            in_specs=[mode_spec, mode_spec] + [pl.BlockSpec(memory_space=pl.ANY)] * (held is not None),
            out_specs=out_spec,
            input_output_aliases={} if held is None else {2: 0},
            compiler_params=PARAMS,
            cost_estimate=pl.CostEstimate(flops=2000000, bytes_accessed=3000000, transcendentals=0),
        )(*operands)

    def round_trip(blocks, step, side, *after):
        blocks = swap_rows(blocks)
        blocks = swap_cols(x_step(x_ahead_kernel, to_modes[side], SLABS, blocks, *after))
        blocks, modes = step(blocks)
        blocks = swap_cols(blocks)
        blocks = swap_rows(x_step(x_behind_kernel, to_rows[side], BLOCKS if side else SLABS, blocks))
        return blocks, modes

    loads = [
        pltpu.VMEM((2, ROWS, 512), BF16),
        pltpu.VMEM((2, 256, 512), BF16),
        pltpu.SemaphoreType.DMA((4,)),
    ]
    blocks, token = call(
        start_kernel, [SLABS, SUMS], TURN + loads, far(field), far(ahead), specs=[FAR, FAR]
    )
    squares = jax.ShapeDtypeStruct((2, ROWS, ROWS), BF16)
    first, second, twiddle, near_above, local_back, local_ahead, offsets = call(
        prepare_kernel,
        [
            WEIGHTS, WEIGHTS, jax.ShapeDtypeStruct((128, 128), F32), WIDE16,
            squares, squares, jax.ShapeDtypeStruct((ROWS, 2), F32),
        ],
        [
            pltpu.VMEM((2, 2, C, 128, C), F32),
            pltpu.VMEM((4, 128, 128), F32),
            pltpu.VMEM((2, C, C), BF16),
            pltpu.VMEM((2, C), F32),
            pltpu.SemaphoreType.DMA((6,)),
        ],
        token, *(far(a) for a in (weights, jnp.asarray(column_table()), above, pointwise, biases)),
        specs=[pl.BlockSpec(memory_space=pl.ANY)] + [FAR] * 5,
        cost=pl.CostEstimate(flops=60000000, bytes_accessed=8000000, transcendentals=0),
    )
    turned = (first, second)
    blocks, spectrum_0 = round_trip(blocks, lambda b: mix_step(mix_kernel, SLABS, 0, b), 0, twiddle)
    blocks, field_1, factor_0 = call(
        layer_kernel, [SLABS, WIDE16, WIDE32], TURN,
        blocks, field, local_ahead, offsets, ahead, behind,
    )
    blocks, spectrum_1 = round_trip(blocks, lambda b: mix_step(mix_kernel, SLABS, 1, b), 0)
    final = call(
        final_kernel, WIDE32, TURN,
        blocks, field_1, local_ahead, offsets, behind,
        cost=pl.CostEstimate(flops=200000000, bytes_accessed=2000000, transcendentals=0),
    )
    blocks, slopes_1 = call(
        top_kernel, [SLABS, WIDE16],
        TURN,
        blocks, field_1, local_ahead, offsets, near_above, behind,
    )
    blocks, dmixed_1 = round_trip(blocks, lambda b: mix_step(mix_grad_kernel, BLOCKS, 1, b, field_1, slopes_1), 1)
    grads = weight_grad(1, spectrum_1, dmixed_1)
    blocks, slopes_0, later = call(
        back_kernel, [SLABS, WIDE16, SUMS], TURN,
        blocks, slopes_1, local_back, factor_0, ahead, behind,
    )
    blocks, dmixed_0 = round_trip(blocks, lambda b: mix_step(mix_grad_kernel, BLOCKS, 0, b, field, slopes_0), 1)
    grads = weight_grad(0, spectrum_0, dmixed_0, grads)
    grad_hidden, mixing, offset_grads = call(
        end_kernel,
        [WIDE32, jax.ShapeDtypeStruct((C, 2, C), F32), jax.ShapeDtypeStruct((2, C), F32)],
        TURN,
        blocks, slopes_0, local_back, ahead, later,
    )

    def cells(value):
        return jnp.transpose(value.reshape(C, 8, Q), (1, 0, 2))[None]

    grad_spectral = jnp.transpose(grads.reshape(2, 2, C, 2, 16, 4, C), (0, 1, 2, 6, 3, 4, 5))
    return (
        cells(final),
        cells(grad_hidden),
        grad_spectral,
        jnp.transpose(mixing, (1, 0, 2)),
        offset_grads,
    )


def solution(mesh):
    names = ("z", "h", "core", "ylo", "x")
    fine = Mesh(mesh.devices.reshape(8, 2, 2, 2, 4), names)
    rows, cols = ("z", "h", "core"), ("ylo", "x")
    grid = P(rows, cols, None, None)
    modes = P(None, None, None, None, cols, None, rows)
    return jax.shard_map(
        per_device,
        mesh=fine,
        in_specs=(grid, modes, P(), P(), grid),
        out_specs=(grid, grid, modes, P(), P()),
        check_vma=False,
    )
```
